32 devices in a mesh: dp: 4 (over z), section: 4 (over y, x), tensor: 2 (over core).
Axes of the slice: x: 2, y: 2, z: 4, core: 2. Of those that a mesh axis runs over, the one named last changes fastest.
Arguments:
- inputs: float32 [12, 256, 768], P('dp', 'tensor', 'section'), may hold values from -6 to 6
- counts: int32 [12], P('dp'), may hold values from 2 to 4, as said below
- w_query: bfloat16 [2, 768, 768], P(None, None, 'tensor'), may hold values from -0.21875 to 0.21875
- w_key: bfloat16 [2, 768, 768], P(None, None, 'tensor'), may hold values from -0.21875 to 0.21875
- w_value: bfloat16 [2, 768, 768], P(None, None, 'tensor'), may hold values from -0.21875 to 0.21875
- w_out: bfloat16 [2, 768, 768], P(None, None, 'tensor'), may hold values from -0.875 to 0.875
- w_up: bfloat16 [2, 768, 3072], P(None, None, 'tensor'), may hold values from -0.21875 to 0.21875
- w_down: bfloat16 [2, 768, 3072], P(None, None, 'tensor'), may hold values from -0.109375 to 0.109375
- gain_one: float32 [2, 768], replicated, may hold values from 0.5 to 1.5
- bias_one: float32 [2, 768], replicated, may hold values from -1.25 to 1.25
- gain_two: float32 [2, 768], replicated, may hold values from 0.5 to 1.5
- bias_two: float32 [2, 768], replicated, may hold values from -1.25 to 1.25
- pass_embed: float32 [4, 768], replicated, may hold values from -3 to 3
- cotangent: float32 [4, 12, 256, 768], P('section', 'dp', 'tensor'), may hold values from -6 to 6
Outputs:
- passes: float32 [4, 12, 256, 768], P('section', 'dp', 'tensor')
- grad_inputs: float32 [12, 256, 768], P('dp', 'tensor', 'section')
- grad_w_query: float32 [2, 768, 768], P(None, None, 'tensor')
- grad_w_key: float32 [2, 768, 768], P(None, None, 'tensor')
- grad_w_value: float32 [2, 768, 768], P(None, None, 'tensor')
- grad_w_out: float32 [2, 768, 768], P(None, None, 'tensor')
- grad_w_up: float32 [2, 768, 3072], P(None, None, 'tensor')
- grad_w_down: float32 [2, 768, 3072], P(None, None, 'tensor')
- grad_gain_one: float32 [2, 768], replicated
- grad_bias_one: float32 [2, 768], replicated
- grad_gain_two: float32 [2, 768], replicated
- grad_bias_two: float32 [2, 768], replicated
- grad_pass_embed: float32 [4, 768], replicated
The draws below stay inside these ranges and needn't reach their ends.
Inputs may be any that keep to these rules, and one draw needn't show every extreme that they name: `counts`: each item's number of passes; among the 3 items of each index of dp at least one has 4 passes.
All inputs are finite; a program needn't handle non-finite values.
Results may differ from the reference program's by a relative error of at most 0.015.
Values may be sent and summed in bfloat16 or wider, within the bound.
No kernel may reach another device: no remote copies, remote signals or barrier semaphores. Data moves between devices by JAX's collectives and lax.ppermute only.
A program may use at most 192 MiB of HBM per device.

```python
import jax
import jax.numpy as jnp
from jax import lax

D = 768
HEADS = 12
HEAD_DIM = 64
FF = 3072
PASSES = 4
LEN = 256
MB = 3
ITEMS = 12


def draw_counts(key, part):
    key = jax.random.fold_in(key, 11)
    first_key, second_key = jax.random.split(key)
    base_counts = jax.random.randint(first_key, (ITEMS,), 2, PASSES + 1)
    chosen = jax.random.randint(second_key, (ITEMS // MB,), 0, MB)
    full_rows = jnp.arange(ITEMS) % MB == jnp.repeat(chosen, MB, total_repeat_length=ITEMS)
    return jnp.where(full_rows, PASSES, base_counts).astype(jnp.int32)


def block_scale(key, extent, cuts, smallest, largest):
    gain, own = 1.0, jax.random.fold_in(key, 6)
    for dim, shards_of in cuts:
        draws = jnp.exp(jax.random.uniform(jax.random.fold_in(own, dim), (shards_of,), jnp.float32, smallest / len(cuts), largest / len(cuts)))
        gain = gain * jnp.repeat(draws, extent[dim] // shards_of).reshape([-1 if axis == dim else 1 for axis in range(len(extent))])
    return gain


def noise(stream_key, dims, scale, reach, shards=(), held_as=jnp.bfloat16):
    result = scale * jax.random.normal(stream_key, dims, jnp.float32)
    if shards:
        result = result * block_scale(stream_key, dims, shards, -0.22, 0.18)
    return jnp.clip(result, -reach, reach).astype(held_as)


def setup_inputs(seed: int = 0) -> dict:
    key_of = jax.random.split(jax.random.key(seed), 15)
    return {
        "inputs": noise(key_of[0], (ITEMS, LEN, D), 1.0, 6.0, ((0, 4), (1, 2), (2, 4)), jnp.float32),
        "counts": draw_counts(jax.random.fold_in(key_of[14], 71), 0),
        "w_query": noise(key_of[2], (2, D, D), D ** -0.5, 0.21875, ((2, 2),)),
        "w_key": noise(key_of[3], (2, D, D), D ** -0.5, 0.21875, ((2, 2),)),
        "w_value": noise(key_of[4], (2, D, D), D ** -0.5, 0.21875, ((2, 2),)),
        "w_out": noise(key_of[5], (2, D, D), (D // 16) ** -0.5, 0.875, ((2, 2),)),
        "w_up": noise(key_of[6], (2, D, FF), D ** -0.5, 0.21875, ((2, 2),)),
        "w_down": noise(key_of[7], (2, D, FF), FF ** -0.5, 0.109375, ((2, 2),)),
        "gain_one": jnp.clip(1.0 + 0.1 * jax.random.normal(key_of[8], (2, D), jnp.float32), 0.5, 1.5),
        "bias_one": noise(key_of[9], (2, D), 0.2, 1.25, (), jnp.float32),
        "gain_two": jnp.clip(1.0 + 0.1 * jax.random.normal(key_of[10], (2, D), jnp.float32), 0.5, 1.5),
        "bias_two": noise(key_of[11], (2, D), 0.2, 1.25, (), jnp.float32),
        "pass_embed": noise(key_of[12], (PASSES, D), 0.5, 3.0, (), jnp.float32),
        "cotangent": noise(key_of[13], (PASSES, ITEMS, LEN, D), 1.0, 6.0, ((0, 4), (1, 4), (2, 2)), jnp.float32),
    }


EPSILON = 1e-05
MASKED = -1e+30
HIGHEST = lax.Precision.HIGHEST

@jax.custom_vjp
def low(v):
    return lax.optimization_barrier(v.astype(jnp.bfloat16)).astype(jnp.float32)

@jax.custom_vjp
def low_back(v):
    return v

def low_keep(v):
    return (low(v), None)

def low_pass(kept, grad):
    return (grad,)

def back_keep(v):
    return (v, None)

def back_low(kept, grad):
    return (low(grad),)
low.defvjp(low_keep, low_pass)
low_back.defvjp(back_keep, back_low)

def layer_norm(source, gain_row, bias_row):
    average = lax.optimization_barrier(jnp.mean(source, axis=-1, keepdims=True))
    centred = source - average
    spread = lax.optimization_barrier(jnp.mean(centred * centred, axis=-1, keepdims=True))
    return centred * lax.rsqrt(spread + EPSILON) * gain_row + bias_row

def project(left_side, right_side):
    return jnp.matmul(left_side, right_side, precision=HIGHEST)

def attend_item(queries, key_all, value_all):
    length = queries.shape[0]
    key_count = key_all.shape[0]
    query_heads = queries.reshape(length, HEADS, HEAD_DIM)
    key_heads = key_all.reshape(key_count, HEADS, HEAD_DIM)
    value_heads = value_all.reshape(key_count, HEADS, HEAD_DIM)
    scores = jnp.einsum('thd,khd->htk', query_heads, key_heads, precision=HIGHEST) * HEAD_DIM ** (-0.5)
    scores = low_back(scores)
    position = jnp.arange(length)
    key_place = jnp.arange(key_count) % length
    allowed = key_place[None, :] <= position[:, None]
    scores = jnp.where(allowed[None], scores, MASKED)
    weights = low(jax.nn.softmax(scores, axis=-1))
    mixed_heads = jnp.einsum('htk,khd->thd', weights, value_heads, precision=HIGHEST)
    return mixed_heads.reshape(length, HEADS * HEAD_DIM)

def reference(inputs, counts, w_query, w_key, w_value, w_out, w_up, w_down, gain_one, bias_one, gain_two, bias_two, pass_embed, cotangent):
    checked = jax.checkpoint(attend_item)

    def forward(inputs, w_query, w_key, w_value, w_out, w_up, w_down, gain_one, bias_one, gain_two, bias_two, pass_embed):
        current = inputs
        key_list = []
        value_list = []
        results = []
        for pass_index in range(PASSES):
            layer_id = min(pass_index, 1)
            entered = current + pass_embed[pass_index]
            normed = low(layer_norm(entered, gain_one[layer_id], bias_one[layer_id]))
            queries = low_back(low(project(normed, w_query[layer_id])))
            key_new = low_back(low(project(normed, w_key[layer_id])))
            value_new = low_back(low(project(normed, w_value[layer_id])))
            key_list.append(key_new)
            value_list.append(value_new)
            key_all = jnp.concatenate(key_list, axis=1)
            value_all = jnp.concatenate(value_list, axis=1)
            mixed_heads = lax.map(lambda triple: checked(triple[0], triple[1], triple[2]), (queries, key_all, value_all))
            mixed_heads = low_back(low(mixed_heads))
            branch = low_back(project(mixed_heads, jnp.swapaxes(w_out[layer_id], 0, 1)))
            middle = entered + branch
            normed_two = low(layer_norm(middle, gain_two[layer_id], bias_two[layer_id]))
            hidden = low_back(project(normed_two, w_up[layer_id]))
            active = low(jax.nn.gelu(hidden, approximate=True))
            current = middle + low_back(project(active, jnp.swapaxes(w_down[layer_id], 0, 1)))
            present = (counts > pass_index)[:, None, None]
            results.append(jnp.where(present, current, 0.0))
        return jnp.stack(results)
    outputs, backward = jax.vjp(forward, inputs, w_query.astype(jnp.float32), w_key.astype(jnp.float32), w_value.astype(jnp.float32), w_out.astype(jnp.float32), w_up.astype(jnp.float32), w_down.astype(jnp.float32), gain_one, bias_one, gain_two, bias_two, pass_embed)
    grads = backward(cotangent)
    return (outputs, grads[0], grads[1], grads[2], grads[3], grads[4], grads[5], grads[6], grads[7], grads[8], grads[9], grads[10], grads[11])
```

```python
import functools

import jax
import jax.numpy as jnp
from jax import lax
from jax.experimental import pallas as pl
from jax.experimental.pallas import tpu as pltpu
from jax.sharding import PartitionSpec as P

HEADS = 12
EPSILON = 1e-05
MASKED = -1e30
F32 = jnp.float32
BF16 = jnp.bfloat16
ROOT = 0.7978845608028654
CUBIC = 0.044715
NN = (((1,), (0,)), ((), ()))
NT = (((1,), (1,)), ((), ()))
TN = (((0,), (0,)), ((), ()))
VMEM_LIMIT = 40 * 1024 * 1024


def dot(left, right, dims=NN):
    return lax.dot_general(left, right, dims, preferred_element_type=F32)


def norm_parts(rows):
    centred = rows - jnp.mean(rows, axis=-1, keepdims=True)
    spread = jnp.mean(centred * centred, axis=-1, keepdims=True)
    inverse = lax.rsqrt(spread + EPSILON)
    return centred * inverse, inverse


def norm_back(rows, gain, grad):
    normal, inverse = norm_parts(rows)
    scaled = gain * grad
    middle = jnp.mean(scaled, axis=-1, keepdims=True)
    along = jnp.mean(scaled * normal, axis=-1, keepdims=True)
    back = inverse * (scaled - middle - normal * along)
    gain_sum = jnp.sum(grad * normal, axis=0, keepdims=True)
    bias_sum = jnp.sum(grad, axis=0, keepdims=True)
    return back, gain_sum, bias_sum


def both(own, other):
    return own[...].astype(F32) + other[...].astype(F32)


def fetch(sources, layer, places, sems):
    copies = []
    for index, (source, place) in enumerate(zip(sources, places)):
        copy = pltpu.make_async_copy(source.at[layer], place, sems.at[index])
        copy.start()
        copies.append(copy)
    return copies


def causal_mask(length):
    key_place = lax.broadcasted_iota(jnp.int32, (length, length), 0)
    query_place = lax.broadcasted_iota(jnp.int32, (length, length), 1)
    return key_place <= query_place


def lane_half(rows, half, pair):
    lane = lax.broadcasted_iota(jnp.int32, pair.shape, 1)
    keep = (lane < 64) if half == 0 else (lane >= 64)
    return jnp.where(keep, pair, jnp.zeros_like(pair))


def attention_forward(step, layer, *refs):
    refs = list(refs)
    take = lambda count: [refs.pop(0) for _ in range(count)]
    if step == 0:
        (x_ref,) = take(1)
    else:
        r_ref, own_ref, other_ref = take(3)
    embed_ref, gain_ref, bias_ref = take(3)
    wq, wk, wv, wo = take(4)
    past_k = take(step)
    past_vt = take(step)
    if step > 0:
        (h_ref,) = take(1)
    u_ref, a_ref, q_ref, k_ref, kt_ref, v_ref, vt_ref, lse_ref, o_ref, part_ref = take(10)
    wq_v, wk_v, wv_v, wo_v, ot_v, sems = take(6)
    copies = fetch((wq, wk, wv, wo), layer, (wq_v, wk_v, wv_v, wo_v), sems)
    if step == 0:
        entered = x_ref[...] + embed_ref[0:1, :]
    else:
        result = r_ref[...] + both(own_ref, other_ref)
        h_ref[...] = result
        entered = result + embed_ref[step : step + 1, :]
    u_ref[...] = entered
    normal, _ = norm_parts(entered)
    a = (normal * gain_ref[layer : layer + 1, :] + bias_ref[layer : layer + 1, :]).astype(BF16)
    a_ref[...] = a
    copies[0].wait()
    q_ref[...] = (dot(a, wq_v[...]).astype(BF16).astype(F32) * 0.125).astype(BF16)
    copies[1].wait()
    k_full = dot(a, wk_v[...])
    k_ref[...] = k_full.astype(BF16)
    kt_ref[...] = k_full.T.astype(BF16)
    copies[2].wait()
    v_full = dot(a, wv_v[...])
    v_ref[...] = v_full.astype(BF16)
    vt_ref[...] = v_full.T.astype(BF16)
    length = entered.shape[0]
    seen = causal_mask(length)
    all_k = past_k + [k_ref]
    all_vt = past_vt + [vt_ref]
    head_count = q_ref.shape[1] // 64
    for head in range(head_count):
        pair, half = divmod(head, 2)
        lanes = slice(128 * pair, 128 * pair + 128)
        query = lane_half(length, half, q_ref[:, lanes])
        scores = [jnp.where(seen, dot(key[:, lanes], query, NT), MASKED) for key in all_k]
        highest = functools.reduce(
            jnp.maximum, [jnp.max(one, axis=0, keepdims=True) for one in scores]
        )
        powers = [jnp.exp(one - highest) for one in scores]
        total = functools.reduce(jnp.add, [jnp.sum(one, axis=0, keepdims=True) for one in powers])
        inverse = 1.0 / total
        lse_ref[head : head + 1, :] = highest + jnp.log(total)
        rows = slice(64 * head, 64 * head + 64)
        mixed = None
        for power, value in zip(powers, all_vt):
            term = dot(value[rows, :], (power * inverse).astype(BF16))
            mixed = term if mixed is None else mixed + term
        ot_v[rows, :] = mixed
    o = ot_v[...].T.astype(BF16)
    o_ref[...] = o
    copies[3].wait()
    part_ref[...] = dot(o, wo_v[...], NT).astype(BF16)


def gelu_parts(hidden):
    square = hidden * hidden
    bent = jnp.tanh(ROOT * hidden * (1.0 + CUBIC * square))
    return square, bent


def feed_forward(layer, u_ref, own_ref, other_ref, gain_ref, bias_ref, wu, wd, *refs):
    r_ref, b_ref, g_ref, m_ref, part_ref, wu_v, wd_v, sems = refs
    copies = fetch((wu, wd), layer, (wu_v, wd_v), sems)
    middle = u_ref[...] + both(own_ref, other_ref)
    r_ref[...] = middle
    normal, _ = norm_parts(middle)
    b = (normal * gain_ref[layer : layer + 1, :] + bias_ref[layer : layer + 1, :]).astype(BF16)
    b_ref[...] = b
    copies[0].wait()
    hidden = dot(b, wu_v[...])
    g_ref[...] = hidden
    _, bent = gelu_parts(hidden)
    m = (0.5 * hidden * (1.0 + bent)).astype(BF16)
    m_ref[...] = m
    copies[1].wait()
    part_ref[...] = dot(m, wd_v[...], NT).astype(BF16)


def feed_backward(step, layer, last, *refs):
    refs = list(refs)
    take = lambda count: [refs.pop(0) for _ in range(count)]
    (cot_ref,) = take(1)
    if not last:
        dr_ref, own_ref, other_ref, u_ref, gain_ref = take(5)
    g_ref, wu, wd = take(3)
    dh_ref, e_ref, dg_ref, part_ref = take(4)
    if not last:
        (small_ref,) = take(1)
    wu_v, wd_v, sems = take(3)
    copies = fetch((wd, wu), layer, (wd_v, wu_v), sems)
    grad = cot_ref[...]
    if not last:
        back, gain_sum, bias_sum = norm_back(
            u_ref[...], gain_ref[1:2, :], both(own_ref, other_ref)
        )
        entered = dr_ref[...] + back
        small_ref[0:1, :] = gain_sum
        small_ref[1:2, :] = bias_sum
        small_ref[2:3, :] = jnp.sum(entered, axis=0, keepdims=True)
        grad = grad + entered
    dh_ref[...] = grad
    e = grad.astype(BF16)
    e_ref[...] = e
    hidden = g_ref[...]
    square, bent = gelu_parts(hidden)
    slope = 0.5 * (1.0 + bent) + 0.5 * hidden * (1.0 - bent * bent) * ROOT * (
        1.0 + 3.0 * CUBIC * square
    )
    copies[0].wait()
    dg = (dot(e, wd_v[...]) * slope).astype(BF16)
    dg_ref[...] = dg
    copies[1].wait()
    part_ref[...] = dot(dg, wu_v[...], NT).astype(BF16)


def attention_backward(step, layer, last, *refs):
    refs = list(refs)
    take = lambda count: [refs.pop(0) for _ in range(count)]
    dh_ref, own_ref, other_ref, r_ref, gain_ref = take(5)
    wq, wk, wv, wo = take(4)
    q_ref, lse_ref = take(2)
    keys = take(step + 1)
    keys_t = take(step + 1)
    values = take(step + 1)
    if not last:
        dk_in, dv_in = take(2)
    dr_ref, f_ref, dq_ref, dk_ref, dv_ref, part_ref, small_ref = take(7)
    if step > 0:
        dk_out, dv_out = take(2)
    wq_v, wk_v, wv_v, wo_v, do_v, dqt_v, sems = take(7)
    copies = fetch((wo, wq, wk, wv), layer, (wo_v, wq_v, wk_v, wv_v), sems)
    back, gain_sum, bias_sum = norm_back(
        r_ref[...], gain_ref[layer : layer + 1, :], both(own_ref, other_ref)
    )
    small_ref[0:1, :] = gain_sum
    small_ref[1:2, :] = bias_sum
    grad = dh_ref[...] + back
    dr_ref[...] = grad
    f = grad.astype(BF16)
    f_ref[...] = f
    copies[0].wait()
    do_v[...] = dot(f, wo_v[...]).astype(BF16)
    length = f.shape[0]
    seen = causal_mask(length)
    head_count = q_ref.shape[1] // 64
    for pair in range(head_count // 2):
        lanes = slice(128 * pair, 128 * pair + 128)
        key_sums = [None] * (step + 1)
        value_sums = [None] * (step + 1)
        for half in range(2):
            head = 2 * pair + half
            rows = slice(64 * head, 64 * head + 64)
            query = lane_half(length, half, q_ref[:, lanes])
            grad_mix = lane_half(length, half, do_v[:, lanes])
            logsum = lse_ref[head : head + 1, :]
            exact = [
                jnp.exp(jnp.where(seen, dot(key[:, lanes], query, NT), MASKED) - logsum)
                for key in keys
            ]
            grad_weights = [dot(value[:, lanes], grad_mix, NT) for value in values]
            delta = functools.reduce(
                jnp.add,
                [jnp.sum(p * dp, axis=0, keepdims=True) for p, dp in zip(exact, grad_weights)],
            )
            query_grad = None
            for slot in range(step + 1):
                grad_scores = (exact[slot] * (grad_weights[slot] - delta)).astype(BF16)
                term = dot(keys_t[slot][rows, :], grad_scores)
                query_grad = term if query_grad is None else query_grad + term
                key_term = dot(grad_scores, query)
                value_term = dot(exact[slot].astype(BF16), grad_mix)
                if half == 0:
                    key_sums[slot] = key_term
                    value_sums[slot] = value_term
                else:
                    key_sums[slot] = key_sums[slot] + key_term
                    value_sums[slot] = value_sums[slot] + value_term
            dqt_v[rows, :] = query_grad
        for slot in range(step + 1):
            key_sum, value_sum = key_sums[slot], value_sums[slot]
            if not last:
                key_sum = key_sum + dk_in[slot, :, lanes]
                value_sum = value_sum + dv_in[slot, :, lanes]
            if slot == step:
                dk_ref[:, lanes] = key_sum.astype(BF16)
                dv_ref[:, lanes] = value_sum.astype(BF16)
            else:
                dk_out[slot, :, lanes] = key_sum
                dv_out[slot, :, lanes] = value_sum
    dq = (dqt_v[...].T * 0.125).astype(BF16)
    dq_ref[...] = dq
    for copy in copies[1:]:
        copy.wait()
    part = dot(dq, wq_v[...], NT) + dot(dk_ref[...], wk_v[...], NT) + dot(dv_ref[...], wv_v[...], NT)
    part_ref[...] = part.astype(BF16)


def entry_backward(dr_ref, own_ref, other_ref, u_ref, gain_ref, out_ref, small_ref):
    back, gain_sum, bias_sum = norm_back(u_ref[...], gain_ref[0:1, :], both(own_ref, other_ref))
    entered = dr_ref[...] + back
    out_ref[...] = entered
    small_ref[0:1, :] = gain_sum
    small_ref[1:2, :] = bias_sum
    small_ref[2:3, :] = jnp.sum(entered, axis=0, keepdims=True)


def call(body, operands, hbm, outs, scratch, flops=0, bytes_accessed=0):
    inside = pl.BlockSpec(memory_space=pltpu.VMEM)
    outside = pl.BlockSpec(memory_space=pl.ANY)
    return pl.pallas_call(
        body,
        out_shape=tuple(jax.ShapeDtypeStruct(shape, kind) for shape, kind in outs),
        in_specs=[outside if index in hbm else inside for index in range(len(operands))],
        out_specs=tuple(inside for _ in outs),
        scratch_shapes=scratch,
        compiler_params=pltpu.CompilerParams(vmem_limit_bytes=VMEM_LIMIT),
        cost_estimate=pl.CostEstimate(
            flops=flops, bytes_accessed=bytes_accessed, transcendentals=0
        ),
    )(*operands)


def swap(value):
    return lax.ppermute(value, "tensor", [(0, 1), (1, 0)])


def xor_pairs(axis, bits):
    return [(place, place ^ bits) for place in range(lax.axis_size(axis))]


def pick(stacked, index):
    return lax.dynamic_index_in_dim(stacked, index, 0, keepdims=False)


def add_low(left, right):
    return (left.astype(F32) + right.astype(F32)).astype(BF16)


def halve(buffer, axis, bits, bit):
    rows = buffer.shape[0] // 2
    kept = lax.dynamic_slice_in_dim(buffer, bit * rows, rows, 0)
    sent = lax.dynamic_slice_in_dim(buffer, (1 - bit) * rows, rows, 0)
    return add_low(kept, lax.ppermute(sent, axis, xor_pairs(axis, bits)))


def widen(buffer, axis, bits, bit):
    other = lax.ppermute(buffer, axis, xor_pairs(axis, bits))
    ring = jnp.concatenate([other, buffer, other], axis=0)
    rows = buffer.shape[0]
    return lax.dynamic_slice_in_dim(ring, (1 - bit) * rows, 2 * rows, 0)


def line_reduce(buffer, axis):
    count = lax.axis_size(axis)
    place = lax.axis_index(axis)
    rows = buffer.shape[0] // count

    def chunk(index):
        return lax.dynamic_slice_in_dim(buffer, jnp.clip(index, 0, count - 1) * rows, rows, 0)

    up = down = None
    for step in range(1, count):
        send_up = chunk(count - step + place)
        send_down = chunk(step - count + place)
        if up is not None:
            send_up = add_low(send_up, up)
            send_down = add_low(send_down, down)
        up = lax.ppermute(send_up, axis, [(i, i + 1) for i in range(step)])
        down = lax.ppermute(
            send_down, axis, [(count - 1 - i, count - 2 - i) for i in range(step)]
        )
    total = chunk(place).astype(F32) + up.astype(F32) + down.astype(F32)
    return total.astype(BF16)


def line_gather(buffer, axis):
    count = lax.axis_size(axis)
    place = lax.axis_index(axis)
    rows = buffer.shape[0]
    below, above = [], []
    up = down = buffer
    for step in range(1, count):
        up = lax.ppermute(up, axis, [(i, i + 1) for i in range(step - 1, count - 1)])
        down = lax.ppermute(
            down, axis, [(count - 1 - i, count - 2 - i) for i in range(step - 1, count - 1)]
        )
        below.insert(0, up)
        above.append(down)
    ring = jnp.concatenate(below + [buffer] + above, axis=0)
    return lax.dynamic_slice_in_dim(ring, (count - 1 - place) * rows, count * rows, 0)


def shards(
    inputs,
    counts,
    w_query,
    w_key,
    w_value,
    w_out,
    w_up,
    w_down,
    gain_one,
    bias_one,
    gain_two,
    bias_two,
    pass_embed,
    cotangent,
):
    section_count = lax.axis_size("section")
    section = lax.axis_index("section")
    tensor = lax.axis_index("tensor")
    batches, half_rows, slice_width = inputs.shape
    length = 2 * half_rows
    width = cotangent.shape[3]
    head_width = w_query.shape[2]
    hidden_width = w_up.shape[2]
    passes = pass_embed.shape[0]
    heads = HEADS // lax.axis_size("tensor")
    bit_x, bit_y = section % 2, section // 2

    def by_item(stacked, index):
        valid = index < batches
        return jnp.where(valid, pick(stacked, jnp.minimum(index, batches - 1)), 0)

    def full_rows(own):
        other = swap(own)
        axis = own.ndim - 2
        return jnp.where(
            tensor == 0,
            jnp.concatenate([own, other], axis=axis),
            jnp.concatenate([other, own], axis=axis),
        )

    def exchange(pieces):
        got = [pieces[0]]
        for bits in range(1, section_count):
            got.append(lax.ppermute(pieces[bits], "section", xor_pairs("section", bits)))
        return jnp.stack(got)

    got = exchange([by_item(inputs, section ^ bits) for bits in range(section_count)])
    entries = full_rows(
        jnp.concatenate([pick(got, section ^ place) for place in range(section_count)], axis=1)
    )
    got = exchange([by_item(cotangent[0], section ^ bits) for bits in range(section_count)])
    own_count = by_item(counts, section)
    cot = full_rows(
        jnp.stack(
            [
                jnp.where(place < own_count, pick(got, section ^ place), 0.0)
                for place in range(passes)
            ]
        )
    )

    wide = ((length, width), F32)
    wide_low = ((length, width), BF16)
    heads_low = ((length, head_width), BF16)
    heads_turned = ((head_width, length), BF16)
    hidden_low = ((length, hidden_width), BF16)
    small = ((8, width), F32)
    square_v = pltpu.VMEM((width, head_width), BF16)
    hidden_v = pltpu.VMEM((width, hidden_width), BF16)

    kept = []
    keys, keys_t, values, values_t = [], [], [], []
    results = []
    resid = None
    for step in range(passes):
        layer = min(step, 1)
        first = [entries] if step == 0 else list(resid)
        operands = first + [pass_embed, gain_one, bias_one]
        at = len(operands)
        operands += [w_query, w_key, w_value, w_out] + keys + values_t
        outs = ([] if step == 0 else [wide]) + [
            wide,
            wide_low,
            heads_low,
            heads_low,
            heads_turned,
            heads_low,
            heads_turned,
            ((8, length), F32),
            heads_low,
            wide_low,
        ]
        done = call(
            functools.partial(attention_forward, step, layer),
            operands,
            range(at, at + 4),
            outs,
            [square_v] * 4
            + [pltpu.VMEM((head_width, length), F32), pltpu.SemaphoreType.DMA((4,))],
            flops=2 * length * width * head_width * 4
            + 4 * length * length * 64 * heads * (step + 1) * 2,
            bytes_accessed=width * head_width * 8,
        )
        if step > 0:
            results.append(done[0])
            done = done[1:]
        u, a, q, k, kt, v, vt, lse, o, part = done
        keys.append(k)
        keys_t.append(kt)
        values.append(v)
        values_t.append(vt)
        r, b, g, m, part_two = call(
            functools.partial(feed_forward, layer),
            [u, part, swap(part), gain_two, bias_two, w_up, w_down],
            (5, 6),
            [wide, wide_low, ((length, hidden_width), F32), hidden_low, wide_low],
            [hidden_v] * 2 + [pltpu.SemaphoreType.DMA((2,))],
            flops=4 * length * width * hidden_width,
            bytes_accessed=width * hidden_width * 4,
        )
        resid = (r, part_two, swap(part_two))
        kept.append((u, a, q, lse, o, r, b, g, m))
    results.append(resid[0] + (resid[1].astype(F32) + resid[2].astype(F32)))

    half_start = tensor * half_rows
    sent = jnp.stack(
        [lax.dynamic_slice_in_dim(one, half_start, half_rows, 0) for one in results]
    )
    got = exchange([pick(sent, section ^ bits) for bits in range(section_count)])
    passes_out = jnp.stack(
        [
            jnp.where(section < counts[item], pick(got, section ^ item), 0.0)
            for item in range(batches)
        ]
    )[None]

    factors = [None] * passes
    rows_small = {}
    state = None
    carried = None
    for step in reversed(range(passes)):
        layer = min(step, 1)
        last = step == passes - 1
        u, a, q, lse, o, r, b, g, m = kept[step]
        operands = [cot[step]]
        if not last:
            operands += list(state) + [gain_one]
        at = len(operands) + 1
        operands += [g, w_up, w_down]
        done = call(
            functools.partial(feed_backward, step, layer, last),
            operands,
            (at, at + 1),
            [wide, wide_low, hidden_low, wide_low] + ([] if last else [small]),
            [hidden_v] * 2 + [pltpu.SemaphoreType.DMA((2,))],
            flops=4 * length * width * hidden_width,
            bytes_accessed=width * hidden_width * 4,
        )
        dh, e, dg, part = done[:4]
        if not last:
            rows_small["entry", step + 1] = done[4]
        operands = [dh, part, swap(part), r, gain_two]
        at = len(operands)
        operands += [w_query, w_key, w_value, w_out, q, lse]
        operands += keys[: step + 1] + keys_t[: step + 1] + values[: step + 1]
        if not last:
            operands += list(carried)
        outs = [wide, wide_low, heads_low, heads_low, heads_low, wide_low, small]
        if step > 0:
            outs += [((step, length, head_width), F32)] * 2
        done = call(
            functools.partial(attention_backward, step, layer, last),
            operands,
            range(at, at + 4),
            outs,
            [square_v] * 4
            + [
                pltpu.VMEM((length, head_width), BF16),
                pltpu.VMEM((head_width, length), F32),
                pltpu.SemaphoreType.DMA((4,)),
            ],
            flops=2 * length * width * head_width * 4
            + 10 * length * length * 64 * heads * (step + 1) * 2,
            bytes_accessed=width * head_width * 8,
        )
        dr, f, dq, dk, dv, part, rows_small["middle", step] = done[:7]
        carried = done[7:]
        state = (dr, part, swap(part), u)
        factors[step] = (a, dq, dk, dv, f, o, b, dg, e, m)

    entered, rows_small["entry", 0] = call(
        entry_backward, list(state) + [gain_one], (), [wide, small], []
    )

    own_half = lax.dynamic_slice_in_dim(entered, half_start, half_rows, 0)
    pieces = jnp.stack(
        [
            own_half[:, place * slice_width : (place + 1) * slice_width]
            for place in range(section_count)
        ]
    )
    got = exchange([pick(pieces, section ^ bits) for bits in range(section_count)])
    grad_inputs = jnp.stack([pick(got, section ^ item) for item in range(batches)])

    def weight_grads(steps):
        sums = []
        for left, right in ((6, 7), (0, 1), (8, 9), (4, 5), (0, 2), (0, 3)):
            lefts = jnp.concatenate([factors[step][left] for step in steps], axis=0)
            rights = jnp.concatenate([factors[step][right] for step in steps], axis=0)
            sums.append(dot(lefts, rights, TN).astype(BF16))
        return [jnp.concatenate(sums[at : at + 2], axis=1) for at in (0, 2, 4)]

    def sum_all(parts):
        first, second, third = parts
        first = halve(first, "section", 1, bit_x)
        second = halve(second, "section", 2, bit_y)
        third = line_reduce(third, "dp")
        first = halve(first, "section", 2, bit_y)
        second = halve(second, "section", 1, bit_x)
        third = halve(third, "section", 1, bit_x)
        third = halve(third, "section", 2, bit_y)
        first = line_reduce(first, "dp")
        second = line_reduce(second, "dp")
        first = line_gather(first, "dp")
        second = line_gather(second, "dp")
        third = widen(third, "section", 2, bit_y)
        third = widen(third, "section", 1, bit_x)
        first = widen(first, "section", 2, bit_y)
        second = widen(second, "section", 1, bit_x)
        first = widen(first, "section", 1, bit_x)
        second = widen(second, "section", 2, bit_y)
        third = line_gather(third, "dp")
        return first, second, third

    later = sum_all(weight_grads(range(1, passes)))
    early = sum_all(weight_grads(range(1)))
    layers = [early, later]

    def spread(group, start, size):
        return jnp.stack([one[group][:, start : start + size] for one in layers]).astype(F32)

    def small_rows(kind, row):
        early_rows = rows_small[kind, 0][row]
        later_rows = functools.reduce(
            jnp.add, [rows_small[kind, step][row] for step in range(1, passes)]
        )
        return [early_rows, later_rows]

    packed = jnp.stack(
        small_rows("entry", 0)
        + small_rows("entry", 1)
        + small_rows("middle", 0)
        + small_rows("middle", 1)
        + [rows_small["entry", step][2] for step in range(passes)]
    )
    for axis in ("section", "dp"):
        bits = 1
        while bits < lax.axis_size(axis):
            packed = packed + lax.ppermute(packed, axis, xor_pairs(axis, bits))
            bits *= 2
    return (
        passes_out,
        grad_inputs,
        spread(0, hidden_width, head_width),
        spread(2, 0, head_width),
        spread(2, head_width, head_width),
        spread(1, hidden_width, head_width),
        spread(0, 0, hidden_width),
        spread(1, 0, hidden_width),
        packed[0:2],
        packed[2:4],
        packed[4:6],
        packed[6:8],
        packed[8:],
    )


def solution(mesh):
    weight = P(None, None, "tensor")
    return jax.shard_map(
        shards,
        mesh=mesh,
        in_specs=(
            P("dp", "tensor", "section"),
            P("dp"),
            weight,
            weight,
            weight,
            weight,
            weight,
            weight,
            P(),
            P(),
            P(),
            P(),
            P(),
            P("section", "dp", "tensor", None),
        ),
        out_specs=(
            P("section", "dp", "tensor", None),
            P("dp", "tensor", "section"),
            weight,
            weight,
            weight,
            weight,
            weight,
            weight,
            P(),
            P(),
            P(),
            P(),
            P(),
        ),
        check_vma=False,
    )
```

```python
import functools

import jax
import jax.numpy as jnp
from jax import lax
from jax.experimental import pallas as pl
from jax.experimental.pallas import tpu as pltpu
from jax.sharding import PartitionSpec as P

HEADS = 12
EPSILON = 1e-05
MASKED = -1e30
F32 = jnp.float32
BF16 = jnp.bfloat16
ROOT = 0.7978845608028654
CUBIC = 0.044715
NN = (((1,), (0,)), ((), ()))
NT = (((1,), (1,)), ((), ()))
TN = (((0,), (0,)), ((), ()))


def dot(left, right, dims=NN):
    return lax.dot_general(left, right, dims, preferred_element_type=F32)


def norm_parts(rows):
    centred = rows - jnp.mean(rows, axis=-1, keepdims=True)
    spread = jnp.mean(centred * centred, axis=-1, keepdims=True)
    inverse = lax.rsqrt(spread + EPSILON)
    return centred * inverse, inverse


def norm_back(rows, gain, grad):
    normal, inverse = norm_parts(rows)
    scaled = gain * grad
    middle = jnp.mean(scaled, axis=-1, keepdims=True)
    along = jnp.mean(scaled * normal, axis=-1, keepdims=True)
    back = inverse * (scaled - middle - normal * along)
    gain_sum = jnp.sum(grad * normal, axis=0, keepdims=True)
    bias_sum = jnp.sum(grad, axis=0, keepdims=True)
    return back, gain_sum, bias_sum


def both(own, other):
    return own[...].astype(F32) + other[...].astype(F32)


class Incoming:
    def __init__(self, source, place, sem):
        self.copy = pltpu.make_async_copy(source, place, sem)
        self.copy.start()
        self.place = place
        self.waiting = True

    def ref(self):
        if self.waiting:
            self.copy.wait()
            self.waiting = False
        return self.place

    def __getitem__(self, index):
        return self.ref()[index]


class Outgoing:
    def __init__(self, place, target, sem):
        self.place = place
        self.copy = pltpu.make_async_copy(place, target, sem)

    def put(self, value):
        self.place[...] = value
        self.copy.start()

    def __getitem__(self, index):
        return self.place[index]

    def __setitem__(self, index, value):
        self.place[index] = value


class Chosen:
    def __init__(self, array, index):
        self.array, self.index = array, index


class Near:
    def __init__(self, array):
        self.array = array


class Held:
    def __init__(self, name, *index):
        self.name, self.index = name, index


class Raw:
    def __init__(self, array):
        self.array = array


class Scalars:
    def __init__(self, array):
        self.array = array


class Mover:
    def __init__(self, sems):
        self.sems, self.used = sems, 0

    def start(self, source, target):
        copy = pltpu.make_async_copy(source, target, self.sems.at[self.used])
        self.used += 1
        copy.start()
        return copy


class Order:
    def __init__(self, shapes):
        self.shapes = shapes
        self.stores = {}

    def call(self, body, operands, outs, scratch=(), limit=26, moves=0, update=None):
        kind = lambda one: one[2] if isinstance(one, tuple) and len(one) > 2 else "staged"
        plain = lambda one: not isinstance(one, (Near, Raw, Scalars))
        names = ["order"] + [one.name for one in operands + outs if isinstance(one, Held)]
        names = list(dict.fromkeys(names))
        old = [name for name in names if name in self.stores]
        new = [name for name in names if name not in self.stores]
        given = [one for one in operands if not isinstance(one, Held)]
        made = [one for one in outs if not isinstance(one, Held)]
        arrays = [one.array if isinstance(one, (Chosen, Near, Raw, Scalars)) else one for one in given]

        def shape_of(one):
            if isinstance(one, Held):
                shape, dtype = self.shapes[one.name]
                for index in one.index:
                    if isinstance(index, int):
                        shape = shape[1:]
                    else:
                        sizes = [
                            cut.stop - cut.start if isinstance(cut, slice) else cut for cut in index
                        ]
                        shape = tuple(sizes) + tuple(shape[len(sizes) :])
                return shape, dtype
            if isinstance(one, Chosen):
                return one.array.shape[1:], one.array.dtype
            if isinstance(one, tuple):
                return one[0], one[1]
            return one.shape, one.dtype

        places = [pltpu.VMEM(*shape_of(one)) for one in operands if plain(one)]
        places += [pltpu.VMEM(*shape_of(one)) for one in outs if kind(one) == "staged"]
        first_out = len(old) + len(given)
        total = first_out + len(names) + len(made)
        count = len(places)

        def part(stores, one):
            ref = stores[one.name]
            for index in one.index:
                ref = ref.at[index]
            return ref

        def kernel(*refs):
            in_refs = list(refs[len(old) : first_out])
            stores = dict(zip(old + new, refs[first_out : first_out + len(names)]))
            out_refs = list(refs[first_out + len(names) : total])
            rooms = refs[total : total + count]
            sems, more = refs[total + count], refs[total + count + 1]
            rest = refs[total + count + 2 :]
            ins, results = [], []
            at = 0
            for one in operands:
                ref = part(stores, one) if isinstance(one, Held) else in_refs.pop(0)
                if plain(one):
                    source = ref.at[one.index] if isinstance(one, Chosen) else ref
                    ins.append(Incoming(source, rooms[at], sems.at[at]))
                    at += 1
                else:
                    ins.append(ref)
            for one in outs:
                ref = part(stores, one) if isinstance(one, Held) else out_refs.pop(0)
                if kind(one) == "staged":
                    results.append(Outgoing(rooms[at], ref, sems.at[at]))
                    at += 1
                else:
                    results.append(ref)
            extra = (Mover(more),) if moves else ()
            body(ins, results, *extra, *rest)
            for one in ins:
                if isinstance(one, Incoming):
                    one.ref()
            for one in results:
                if isinstance(one, Outgoing):
                    one.copy.wait()

        anywhere = pl.BlockSpec(memory_space=pl.ANY)
        inside = pl.BlockSpec(memory_space=pltpu.VMEM)
        scalar = pl.BlockSpec(memory_space=pltpu.SMEM)
        spec = lambda one: inside if isinstance(one, Near) else scalar if isinstance(one, Scalars) else anywhere
        aliases = {at: at for at in range(len(old))}
        for out_at, in_at in (update or {}).items():
            shift_in = sum(isinstance(one, Held) for one in operands[:in_at])
            shift_out = sum(isinstance(one, Held) for one in outs[:out_at])
            aliases[len(old) + in_at - shift_in] = len(names) + out_at - shift_out
        shapes = [pltpu.HBM(*self.shapes[name]) for name in old + new]
        for one in made:
            form = pltpu.VMEM if kind(one) == "near" else jax.ShapeDtypeStruct
            shapes.append(form(one[0], one[1]))
        arrays = [
            pltpu.with_memory_space_constraint(array, pltpu.VMEM)
            if isinstance(one, Near)
            else pltpu.with_memory_space_constraint(array, pltpu.HBM)
            if isinstance(one, Chosen)
            else array
            for one, array in zip(given, arrays)
        ]
        done = pl.pallas_call(
            kernel,
            out_shape=tuple(shapes),
            in_specs=[anywhere] * len(old) + [spec(one) for one in given],
            out_specs=(anywhere,) * len(names)
            + tuple(inside if kind(one) == "near" else anywhere for one in made),
            scratch_shapes=places
            + [pltpu.SemaphoreType.DMA((max(count, 1),)), pltpu.SemaphoreType.DMA((max(moves, 1),))]
            + list(scratch),
            input_output_aliases=aliases,
            compiler_params=pltpu.CompilerParams(vmem_limit_bytes=int(limit * 1024 * 1024)),
            cost_estimate=pl.CostEstimate(flops=1000, bytes_accessed=1000, transcendentals=0),
        )(
            *[pltpu.with_memory_space_constraint(self.stores[name], pltpu.HBM) for name in old],
            *arrays,
        )
        self.stores.update(zip(old + new, done[: len(names)]))
        return done[len(names) :]


class Place:
    def __getitem__(self, slot):
        name, bits = slot
        return (lax.axis_index(name) // bits) % 2 if bits else lax.axis_index(name)


HERE = Place()


def causal_mask(length):
    key_place = lax.broadcasted_iota(jnp.int32, (length, length), 0)
    query_place = lax.broadcasted_iota(jnp.int32, (length, length), 1)
    return key_place <= query_place


def lane_half(half, pair):
    lane = lax.broadcasted_iota(jnp.int32, pair.shape, 1)
    keep = (lane < 64) if half == 0 else (lane >= 64)
    return jnp.where(keep, pair, jnp.zeros_like(pair))


def attention_forward(step, layer, ins, outs, mover, turned, *rest):
    count = 2 if step == 0 else 3
    first, (embed, gain, bias, wq, wk, wv, wo) = ins[:count], ins[count : count + 7]
    past_k, past_vt = ins[count + 7 : count + 7 + step], ins[count + 7 + step : count + 7 + 2 * step]
    sent = None
    if step == 0:
        own_t, other_t = first
        (entry_v,) = rest
        half = own_t.shape[1]
        place = pl.multiple_of(lax.axis_index("tensor") * half, half)
        entry_v[pl.ds(place, half), :] = own_t[...].T
        entry_v[pl.ds(pl.multiple_of(half - place, half), half), :] = other_t[...].T
        entered = entry_v[...] + embed[0:1, :]
    else:
        near_r, own, other = first
        (entry_v,) = rest
        result = near_r[...] + both(own, other)
        entry_v[...] = result
        half = entry_v.shape[0] // 2
        place = pl.multiple_of(lax.axis_index("tensor") * half, half)
        sent = mover.start(entry_v.at[pl.ds(place, half)], outs[0].at[step - 1])
        outs = outs[1:]
        entered = result + embed[step : step + 1, :]
    near_out = outs[0]
    near_out[...] = entered
    outs = outs[1:]
    u_out, a_out, q_out, k_out, kt_out, v_out, vt_out, lse_out, o_out, part_out = outs
    u_out.put(entered)
    normal, _ = norm_parts(entered)
    a = (normal * gain[layer : layer + 1, :] + bias[layer : layer + 1, :]).astype(BF16)
    a_out.put(a)
    q_out.put((dot(a, wq[...]).astype(BF16).astype(F32) * 0.125).astype(BF16))
    k_full = dot(a, wk[...])
    k_out.put(k_full.astype(BF16))
    v_full = dot(a, wv[...])
    vt_out.put(v_full.T.astype(BF16))
    v_out.put(v_full.astype(BF16))
    kt_out.put(k_full.T.astype(BF16))
    length = entered.shape[0]
    seen = causal_mask(length)
    all_k = past_k + [k_out]
    all_vt = past_vt + [vt_out]
    head_count = wq.place.shape[1] // 64
    sums = []
    for head in range(head_count):
        pair, half = divmod(head, 2)
        lanes = slice(128 * pair, 128 * pair + 128)
        query = lane_half(half, q_out[:, lanes])
        scores = [jnp.where(seen, dot(key[:, lanes], query, NT), MASKED) for key in all_k]
        highest = functools.reduce(
            jnp.maximum, [jnp.max(one, axis=0, keepdims=True) for one in scores]
        )
        powers = [jnp.exp(one - highest) for one in scores]
        total = functools.reduce(jnp.add, [jnp.sum(one, axis=0, keepdims=True) for one in powers])
        inverse = 1.0 / total
        sums.append(highest + jnp.log(total))
        rows = slice(64 * head, 64 * head + 64)
        mixed = None
        for power, value in zip(powers, all_vt):
            term = dot(value[rows, :], (power * inverse).astype(BF16))
            mixed = term if mixed is None else mixed + term
        turned[rows, :] = mixed
    o = turned[...].T.astype(BF16)
    part_out[...] = dot(o, wo[...], NT).astype(BF16)
    o_out.put(o)
    if sent is not None:
        sent.wait()
    sums += [jnp.zeros_like(sums[0])] * (8 - len(sums))
    lse_out.put(jnp.concatenate(sums, axis=0))


def gelu_parts(hidden):
    square = hidden * hidden
    bent = jnp.tanh(ROOT * hidden * (1.0 + CUBIC * square))
    return square, bent


def feed_forward(layer, ins, outs):
    own, other, u, gain, bias, wu, wd = ins
    near_out, r_out, b_out, g_out, m_out, part_out = outs
    middle = u[...] + both(own, other)
    near_out[...] = middle
    r_out.put(middle)
    normal, _ = norm_parts(middle)
    b = (normal * gain[layer : layer + 1, :] + bias[layer : layer + 1, :]).astype(BF16)
    b_out.put(b)
    hidden = dot(b, wu[...])
    g_out.put(hidden)
    _, bent = gelu_parts(hidden)
    m = (0.5 * hidden * (1.0 + bent)).astype(BF16)
    m_out.put(m)
    part_out[...] = dot(m, wd[...], NT).astype(BF16)


def small_put(out, rows):
    rows = rows + [jnp.zeros_like(rows[0])] * (8 - len(rows))
    out.put(jnp.concatenate(rows, axis=0))


def feed_backward(step, last, ins, outs, mover, cot_v):
    counts, cot_own, cot_other, wd, g, wu = ins[:6]
    near_out, e_out, dg_out, part_out = outs[:4]
    half = cot_v.shape[0] // 2
    place = pl.multiple_of(lax.axis_index("tensor") * half, half)
    copies = [
        mover.start(cot_own.at[step], cot_v.at[pl.ds(place, half)]),
        mover.start(cot_other.at[step], cot_v.at[pl.ds(pl.multiple_of(half - place, half), half)]),
    ]
    item = lax.axis_index("section")
    own_count = jnp.where(
        item < counts.shape[0], counts[jnp.minimum(item, counts.shape[0] - 1)], 0
    )
    present = jnp.where(own_count > step, 1.0, 0.0).astype(F32)
    if last:
        near_r, own, other, end_v = *ins[6:], outs[5]
        end_v[...] = near_r[...] + both(own, other)
        sent = mover.start(end_v.at[pl.ds(place, half)], outs[4].at[step])
    else:
        own, other, dr, u, gain = ins[6:]
        back, gain_sum, bias_sum = norm_back(u[...], gain[1:2, :], both(own, other))
        entered = dr[...] + back
        small_put(outs[4], [gain_sum, bias_sum, jnp.sum(entered, axis=0, keepdims=True)])
    for copy in copies:
        copy.wait()
    grad = cot_v[...] * present
    if not last:
        grad = grad + entered
    near_out[...] = grad
    e = grad.astype(BF16)
    e_out.put(e)
    raw = dot(e, wd[...])
    hidden = g[...]
    square, bent = gelu_parts(hidden)
    slope = 0.5 * (1.0 + bent) + 0.5 * hidden * (1.0 - bent * bent) * ROOT * (
        1.0 + 3.0 * CUBIC * square
    )
    dg = (raw * slope).astype(BF16)
    dg_out.put(dg)
    part_out[...] = dot(dg, wu[...], NT).astype(BF16)
    if last:
        sent.wait()


def attention_backward(step, layer, last, ins, outs, do_v, dqt_v):
    own, other, dh, r, gain, wo, q, lse = ins[:8]
    count = step + 1
    keys, values, keys_t = ins[8 : 8 + count], ins[8 + count : 8 + 2 * count], ins[8 + 2 * count : 8 + 3 * count]
    rest = ins[8 + 3 * count :]
    if not last:
        dk_in, dv_in = rest[:2]
    wq, wk, wv = rest[-3:]
    near_out, f_out, dq_out, dk_out, dv_out, part_out, small_out = outs[:7]
    if step > 0:
        dk_all, dv_all = outs[7:]
    back, gain_sum, bias_sum = norm_back(r[...], gain[layer : layer + 1, :], both(own, other))
    small_put(small_out, [gain_sum, bias_sum])
    grad = dh[...] + back
    near_out[...] = grad
    f = grad.astype(BF16)
    f_out.put(f)
    do_v[...] = dot(f, wo[...]).astype(BF16)
    length = f.shape[0]
    seen = causal_mask(length)
    head_count = q.place.shape[1] // 64
    for pair in range(head_count // 2):
        lanes = slice(128 * pair, 128 * pair + 128)
        key_sums = [None] * count
        value_sums = [None] * count
        for half in range(2):
            head = 2 * pair + half
            rows = slice(64 * head, 64 * head + 64)
            query = lane_half(half, q[:, lanes])
            grad_mix = lane_half(half, do_v[:, lanes])
            logsum = lse[head : head + 1, :]
            exact = [
                jnp.exp(jnp.where(seen, dot(key[:, lanes], query, NT), MASKED) - logsum)
                for key in keys
            ]
            grad_weights = [dot(value[:, lanes], grad_mix, NT) for value in values]
            delta = functools.reduce(
                jnp.add,
                [jnp.sum(p * dp, axis=0, keepdims=True) for p, dp in zip(exact, grad_weights)],
            )
            query_grad = None
            for slot in range(count):
                grad_scores = (exact[slot] * (grad_weights[slot] - delta)).astype(BF16)
                term = dot(keys_t[slot][rows, :], grad_scores)
                query_grad = term if query_grad is None else query_grad + term
                key_term = dot(grad_scores, query)
                value_term = dot(exact[slot].astype(BF16), grad_mix)
                if half == 0:
                    key_sums[slot] = key_term
                    value_sums[slot] = value_term
                else:
                    key_sums[slot] = key_sums[slot] + key_term
                    value_sums[slot] = value_sums[slot] + value_term
            dqt_v[rows, :] = query_grad
        for slot in range(count):
            key_sum, value_sum = key_sums[slot], value_sums[slot]
            if not last:
                key_sum = key_sum + dk_in[slot, :, lanes]
                value_sum = value_sum + dv_in[slot, :, lanes]
            if slot == step:
                dk_out[:, lanes] = key_sum.astype(BF16)
                dv_out[:, lanes] = value_sum.astype(BF16)
            else:
                dk_all[slot, :, lanes] = key_sum
                dv_all[slot, :, lanes] = value_sum
    dq = (dqt_v[...].T * 0.125).astype(BF16)
    part = dot(dq, wq[...], NT) + dot(dk_out[...], wk[...], NT) + dot(dv_out[...], wv[...], NT)
    part_out[...] = part.astype(BF16)
    dq_out.put(dq)
    for one in (dk_out, dv_out) + ((dk_all, dv_all) if step > 0 else ()):
        one.copy.start()


def entry_backward(ins, outs, entry_v):
    own, other, dr, u, gain = ins
    back, gain_sum, bias_sum = norm_back(u[...], gain[0:1, :], both(own, other))
    entered = dr[...] + back
    entry_v[...] = entered
    half = entry_v.shape[0] // 2
    place = pl.multiple_of(lax.axis_index("tensor") * half, half)
    outs[0].put(entry_v[pl.ds(place, half), :].T)
    small_put(outs[1], [gain_sum, bias_sum, jnp.sum(entered, axis=0, keepdims=True)])


def place_pieces(ins, outs, mover):
    pieces = ins
    rows = pieces[0].shape[0]
    copies = []
    for bits, piece in enumerate(pieces):
        at = pl.multiple_of((lax.axis_index("section") ^ bits) * rows, rows)
        copies.append(mover.start(piece, outs[0].at[pl.ds(at, rows)]))
    for copy in copies:
        copy.wait()


def place_passes(ins, outs, mover, room):
    counts, pieces = ins[0], ins[1:]
    copies = [mover.start(piece, room.at[lax.axis_index("section") ^ bits]) for bits, piece in enumerate(pieces)]
    for copy in copies:
        copy.wait()
    for item in range(outs[0].place.shape[0]):
        outs[0][item] = room[item] * jnp.where(counts[item] > lax.axis_index("section"), 1.0, 0.0).astype(F32)
    outs[0].copy.start()


def place_items(ins, outs, mover, room):
    pieces = ins
    copies = [mover.start(piece, room.at[lax.axis_index("section") ^ bits]) for bits, piece in enumerate(pieces)]
    for copy in copies:
        copy.wait()
    out = mover.start(room.at[pl.ds(0, outs[0].shape[0])], outs[0])
    out.wait()


def pack_small(ins, outs):
    passes = (len(ins)) // 2
    entry, middle = ins[:passes], ins[passes:]
    rows = []
    for kind in (entry, middle):
        for row in range(2):
            rows.append(kind[0][row : row + 1, :])
            later = kind[1][row : row + 1, :]
            for step in range(2, passes):
                later = later + kind[step][row : row + 1, :]
            rows.append(later)
    rows += [entry[step][2:3, :] for step in range(passes)]
    rows += [jnp.zeros_like(rows[0])] * (-len(rows) % 8)
    outs[0].put(jnp.concatenate(rows, axis=0))


def add_small(ins, outs):
    outs[0].put(ins[0][...] + ins[1][...])


def part_small(ins, outs):
    total = ins[0][...] + ins[1][...]
    at = 0
    for out in outs:
        count = out.place.shape[0]
        out.put(total[at : at + count])
        at += count


def halves(slot, room, axis):
    size = room.shape[axis] // 2
    kept = pl.multiple_of(HERE[slot] * size, size)
    sent = pl.multiple_of(size - kept, size)
    if axis == 0:
        return room.at[pl.ds(kept, size)], room.at[pl.ds(sent, size)]
    return room.at[:, pl.ds(kept, size)], room.at[:, pl.ds(sent, size)]


def weight_first(products, splits, ins, outs, mover, *rooms):
    factors = ins
    copies = []
    for at, (room, slot) in enumerate(zip(rooms, splits)):
        column = 0
        for lefts, rights in products[at]:
            total = None
            for left, right in zip(lefts, rights):
                term = dot(factors[left][...], factors[right][...], TN)
                total = term if total is None else total + term
            room[:, column : column + total.shape[1]] = total.astype(BF16)
            column += total.shape[1]
        kept, sent = halves(slot, room, 0)
        copies.append(mover.start(sent, outs[2 * at + 1]))
        copies.append(mover.start(kept, outs[2 * at]))
    for copy in copies:
        copy.wait()


def add_split(slots, axis, ins, outs, mover, *rooms):
    copies = []
    for at, (room, slot) in enumerate(zip(rooms, slots)):
        room[...] = (ins[2 * at][...].astype(F32) + ins[2 * at + 1][...].astype(F32)).astype(BF16)
        kept, sent = halves(slot, room, axis)
        copies.append(mover.start(sent, outs[2 * at + 1]))
        copies.append(mover.start(kept, outs[2 * at]))
    for copy in copies:
        copy.wait()


def add_merge(slot, axis, ins, outs, mover, room):
    columns = room.shape[1] // 2
    for at in range(2):
        total = ins[2 * at][...].astype(F32) + ins[2 * at + 1][...].astype(F32)
        room[:, at * columns : (at + 1) * columns] = total.astype(BF16)
    kept, sent = halves(slot, room, axis)
    copies = [mover.start(sent, outs[1]), mover.start(kept, outs[0])]
    for copy in copies:
        copy.wait()


def add_last(ins, outs):
    outs[0].put((ins[0][...].astype(F32) + ins[1][...].astype(F32)).astype(BF16))


def join(slots, axis, ins, outs, mover):
    copies = []
    for at, slot in enumerate(slots):
        own, other = halves(slot, outs[at], axis)
        copies.append(mover.start(ins[2 * at], own))
        copies.append(mover.start(ins[2 * at + 1], other))
    for copy in copies:
        copy.wait()


def join_part(slot, axis, ins, outs, mover, room):
    own, other = halves(slot, room, axis)
    copies = [mover.start(ins[0], own), mover.start(ins[1], other)]
    for copy in copies:
        copy.wait()
    columns = room.shape[1] // 2
    copies = [mover.start(room.at[:, pl.ds(at * columns, columns)], outs[at]) for at in range(2)]
    for copy in copies:
        copy.wait()


def finish(layer, parts, slots, count, ins, outs, mover, *rooms):
    halves_in = ins[:4]
    copies = []
    out_at = 0
    for at, slot in enumerate(slots):
        rows = halves_in[2 * at].place.shape[0]
        for which in range(2):
            place = HERE[slot] * rows
            place = pl.multiple_of(place if which == 0 else rows - place, rows)
            column = 0
            for part in range(parts):
                room = rooms[2 * (out_at + part) + which]
                columns = room.shape[1]
                room[...] = halves_in[2 * at + which][:, column : column + columns].astype(F32)
                copies.append(
                    mover.start(room, outs[out_at + part].at[layer].at[pl.ds(place, rows)])
                )
                column += columns
        out_at += parts
    for copy in copies:
        copy.wait()


def swap(value):
    return lax.ppermute(value, "tensor", [(0, 1), (1, 0)])


def xor_pairs(axis, bits):
    return [(place, place ^ bits) for place in range(lax.axis_size(axis))]


def pick(stacked, index):
    return lax.dynamic_index_in_dim(stacked, index, 0, keepdims=False)


def schedule(levels):
    sizes = [2.0, 1.0, 2.0, 1.0]
    unit = 13.0
    plan = []
    for size in sizes:
        hop = size * unit
        plan.append(
            [("xy", hop), ("xy", hop / 2)]
            + [("z", hop * 2 * (1 << level) / (4 << level)) for level in range(levels)]
            + [("z", hop * 2 * (1 << level) / (4 << level)) for level in reversed(range(levels))]
            + [("xy", hop / 2), ("xy", hop)]
        )
    order = []
    free = {"xy": plan[0][0][1], "z": 0.0}
    place = [1, 0, 0, 0]
    ready = [plan[0][0][1], 0.0, 0.0, 0.0]
    now = 20.0
    sides = {"small": [levels + 3, 20.0, 6.0], "inputs": [2, 20.0, 12.0]}
    while True:
        options = []
        for group in range(4):
            if place[group] > len(plan[group]):
                continue
            if place[group] == 0 and place[group - 1] < 2:
                continue
            options.append((max(ready[group], now), place[group] == 0, -place[group], group))
        for name, (left, time, gap) in sides.items():
            if left:
                options.append((max(time, now), False, -1, name))
        if not options:
            return order
        start, _, _, name = min(options, key=lambda one: one[:3])
        order.append(name)
        if name in sides:
            now = start + 1.5
            sides[name][0] -= 1
            sides[name][1] = now + sides[name][2]
            continue
        now = start + (5.0 if place[name] == 0 else 2.5)
        if place[name] < len(plan[name]):
            link, cost = plan[name][place[name]]
            free[link] = max(free[link], now) + cost
            ready[name] = free[link] + 2.5
        place[name] += 1


def shards(
    inputs,
    counts,
    w_query,
    w_key,
    w_value,
    w_out,
    w_up,
    w_down,
    gain_one,
    bias_one,
    gain_two,
    bias_two,
    pass_embed,
    cotangent,
):
    section_count = lax.axis_size("section")
    section = lax.axis_index("section")
    tensor = lax.axis_index("tensor")
    batches, half_rows, slice_width = inputs.shape
    length = 2 * half_rows
    width = cotangent.shape[3]
    head_width = w_query.shape[2]
    hidden_width = w_up.shape[2]
    passes = pass_embed.shape[0]
    dp_count = lax.axis_size("dp")
    dp_place = lax.axis_index("dp")
    dp_bits = [1 << level for level in range(dp_count.bit_length() - 1)]
    order = Order(
        {
            "order": ((2, passes, length, head_width), F32),
            "low": ((passes, 4, length, width), BF16),
            "hidden": ((passes, 2, length, hidden_width), BF16),
            "heads": ((passes, 7, length, head_width), BF16),
            "turned": ((passes, 4, head_width, length), BF16),
            "wide": ((passes, 2 * length + 24, width), F32),
            "before": ((passes, length, hidden_width), F32),
        }
    )

    def by_item(stacked, index):
        valid = index < batches
        return jnp.where(valid, pick(stacked, jnp.minimum(index, batches - 1)), 0)

    def exchange(pieces):
        return [pieces[0]] + [
            lax.ppermute(pieces[bits], "section", xor_pairs("section", bits))
            for bits in range(1, section_count)
        ]

    slot_x, slot_y = ("section", 1), ("section", 2)
    slots_dp = [("dp", bits) for bits in dp_bits]

    inputs_t = jnp.swapaxes(inputs, 1, 2)
    got = exchange([by_item(inputs_t, section ^ bits) for bits in range(section_count)])
    (entry_t,) = order.call(
        place_pieces,
        [Raw(one) for one in got],
        [((width, half_rows), F32, "near")],
        moves=section_count,
        limit=8,
    )
    entry_other = swap(entry_t)
    cot_got = exchange([by_item(cotangent[0], section ^ bits) for bits in range(section_count)])

    wide_near = ((length, width), F32, "near")
    part_near = ((length, width), BF16, "near")
    stacked = ((2 * passes, half_rows, width), F32, "raw")
    turned = pltpu.VMEM((head_width, length), F32)
    entry_v = pltpu.VMEM((length, width), F32)
    whole = slice(None)

    def low(step, name):
        return Held("low", step, "abef".index(name))

    def hidden(step, name):
        return Held("hidden", step, ("m", "dg").index(name))

    def heads(step, name):
        return Held("heads", step, ("q", "k", "v", "o", "dq", "dk", "dv").index(name))

    def turn(step, name):
        return Held("turned", step, ("kt", "vt").index(name))

    def rows(step, start, count, columns=None):
        cut = (slice(start, start + count), slice(0, columns or width))
        return Held("wide", step, cut)

    def entered(step):
        return rows(step, 0, length)

    def middle(step):
        return rows(step, length, length)

    def logsum(step):
        return rows(step, 2 * length, 8, length)

    def small_entry(step):
        return rows(step, 2 * length + 8, 8)

    def small_middle(step):
        return rows(step, 2 * length + 16, 8)

    results = None
    resid = None
    cot_own = cot_other = None
    for step in range(passes):
        layer = min(step, 1)
        first = [Near(entry_t), Near(entry_other)] if step == 0 else [Near(one) for one in resid]
        weights = [Chosen(one, layer) for one in (w_query, w_key, w_value, w_out)]
        operands = first + [pass_embed, gain_one, bias_one] + weights
        operands += [heads(past, "k") for past in range(step)]
        operands += [turn(past, "vt") for past in range(step)]
        update = None
        if step > 1:
            operands.append(Raw(results))
            update = {0: len(operands) - 1}
        done = order.call(
            functools.partial(attention_forward, step, layer),
            operands,
            ([] if step == 0 else [stacked])
            + [wide_near, entered(step), low(step, "a"), heads(step, "q"), heads(step, "k")]
            + [turn(step, "kt"), heads(step, "v"), turn(step, "vt"), logsum(step)]
            + [heads(step, "o"), part_near],
            [turned, entry_v],
            moves=1,
            update=update,
        )
        if step > 0:
            results = done[0]
            done = done[1:]
        near_u, part = done
        if step == min(2, passes - 1):
            (cot_flat,) = order.call(
                place_pieces,
                [Raw(one) for one in cot_got],
                [((section_count * half_rows, width), F32, "raw")],
                moves=section_count,
                limit=8,
            )
            cot_own = cot_flat.reshape(section_count, half_rows, width)
            cot_other = swap(cot_own)
        near_r, part_two = order.call(
            functools.partial(feed_forward, layer),
            [Near(part), Near(swap(part)), Near(near_u), gain_two, bias_two]
            + [Chosen(w_up, layer), Chosen(w_down, layer)],
            [wide_near, middle(step), low(step, "b"), Held("before", step), hidden(step, "m"), part_near],
        )
        resid = (near_r, part_two, swap(part_two))

    factors = [
        {name: low(step, name) for name in "abef"}
        | {name: hidden(step, name) for name in ("m", "dg")}
        | {name: heads(step, name) for name in ("o", "dq", "dk", "dv")}
        for step in range(passes)
    ]
    state = None

    def feed_step(step):
        nonlocal results
        layer = min(step, 1)
        last = step == passes - 1
        operands = [Scalars(counts), Raw(cot_own), Raw(cot_other)]
        operands += [Chosen(w_down, layer), Held("before", step), Chosen(w_up, layer)]
        outs = [wide_near, low(step, "e"), hidden(step, "dg"), part_near]
        update = None
        if last:
            operands += [Near(one) for one in resid]
            outs += [stacked, wide_near]
            operands.append(Raw(results))
            update = {4: len(operands) - 1}
        else:
            dr, part, other = state
            operands += [Near(part), Near(other), Near(dr), entered(step + 1), gain_one]
            outs += [small_entry(step + 1)]

        def body(ins, outs, mover, cot_v):
            feed_backward(step, last, ins[:9] if last else ins, outs, mover, cot_v)

        done = order.call(body, operands, outs, [entry_v], moves=3, update=update)
        near_dh, part = done[:2]
        if last:
            results = done[2]
        return near_dh, part, swap(part)

    def attention_step(step, fed):
        layer = min(step, 1)
        last = step == passes - 1
        near_dh, part, other = fed
        operands = [Near(part), Near(other), Near(near_dh), middle(step), gain_two]
        operands += [Chosen(w_out, layer), heads(step, "q"), logsum(step)]
        operands += [heads(past, "k") for past in range(step + 1)]
        operands += [heads(past, "v") for past in range(step + 1)]
        operands += [turn(past, "kt") for past in range(step + 1)]
        cut = (slice(0, step + 1),)
        if not last:
            operands += [Held("order", at, cut) for at in range(2)]
        operands += [Chosen(one, layer) for one in (w_query, w_key, w_value)]
        outs = [wide_near, low(step, "f"), heads(step, "dq"), heads(step, "dk"), heads(step, "dv")]
        outs += [part_near, small_middle(step)]
        if step > 0:
            outs += [Held("order", at, (slice(0, step),)) for at in range(2)]
        near_dr, part = order.call(
            functools.partial(attention_backward, step, layer, last),
            operands,
            outs,
            [pltpu.VMEM((length, head_width), BF16), turned],
        )
        return near_dr, part, swap(part)

    later, early = list(range(1, passes)), [0]
    feed_products = ([("b", "dg")], [("e", "m")])
    heads_products = ([("a", "dq"), ("a", "dk")], [("f", "o"), ("a", "dv")])
    kinds = [(later, feed_products), (later, heads_products), (early, feed_products), (early, heads_products)]
    outputs = {}

    def stages(group):
        steps, products = kinds[group]
        names = sorted({name for pair in products for product in pair for name in product})
        operands, place = [], {}
        for name in names:
            for step in steps:
                place[name, step] = len(operands)
                operands.append(factors[step][name])
        columns = sum(order.shapes[factors[steps[0]][right].name][0][-1] for _, right in products[0])
        numbered = [
            [
                ([place[left, step] for step in steps], [place[right, step] for step in steps])
                for left, right in pair
            ]
            for pair in products
        ]
        room = lambda rows, cols: pltpu.VMEM((rows, cols), BF16)
        raw = lambda rows, cols: ((rows, cols), BF16, "raw")
        send = lambda value, axis, bits: lax.ppermute(value, axis, xor_pairs(axis, bits))
        kept_a, sent_a, kept_b, sent_b = order.call(
            functools.partial(weight_first, numbered, (slot_x, slot_y)),
            operands,
            [raw(width // 2, columns)] * 4,
            [room(width, columns)] * 2,
            moves=4,
            limit=40,
        )
        got_a, got_b = send(sent_a, "section", 1), send(sent_b, "section", 2)
        yield
        kept_a, sent_a, kept_b, sent_b = order.call(
            functools.partial(add_split, (slot_y, slot_x), 0),
            [kept_a, got_a, kept_b, got_b],
            [raw(width // 4, columns)] * 4,
            [room(width // 2, columns)] * 2,
            moves=4,
            limit=30,
        )
        got_a, got_b = send(sent_a, "section", 2), send(sent_b, "section", 1)
        yield
        shape = [width // 4, 2 * columns]
        axes = []
        for level, bits in enumerate(dp_bits):
            axis = 0 if shape[0] % 32 == 0 else 1
            axes.append(axis)
            before = tuple(shape)
            shape[axis] //= 2
            if level == 0:
                own, sent = order.call(
                    functools.partial(add_merge, slots_dp[level], axis),
                    [kept_a, got_a, kept_b, got_b],
                    [raw(*shape)] * 2,
                    [room(*before)],
                    moves=2,
                    limit=24,
                )
            else:
                own, sent = order.call(
                    functools.partial(add_split, (slots_dp[level],), axis),
                    [own, got],
                    [raw(*shape)] * 2,
                    [room(*before)],
                    moves=2,
                    limit=16,
                )
            got = send(sent, "dp", bits)
            yield
        (own,) = order.call(add_last, [own, got], [(tuple(shape), BF16)], limit=16)
        got = send(own, "dp", dp_bits[-1])
        yield
        for level in reversed(range(len(dp_bits))):
            axis = axes[level]
            shape[axis] *= 2
            if level > 0:
                (own,) = order.call(
                    functools.partial(join, (slots_dp[level],), axis),
                    [Raw(own), Raw(got)],
                    [raw(*shape)],
                    moves=2,
                    limit=16,
                )
                got = send(own, "dp", dp_bits[level - 1])
                yield
        own_a, own_b = order.call(
            functools.partial(join_part, slots_dp[0], axes[0]),
            [Raw(own), Raw(got)],
            [raw(width // 4, columns)] * 2,
            [room(*shape)],
            moves=4,
            limit=16,
        )
        got_a, got_b = send(own_a, "section", 2), send(own_b, "section", 1)
        yield
        own_a, own_b = order.call(
            functools.partial(join, (slot_y, slot_x), 0),
            [Raw(own_a), Raw(got_a), Raw(own_b), Raw(got_b)],
            [raw(width // 2, columns)] * 2,
            moves=4,
            limit=16,
        )
        got_a, got_b = send(own_a, "section", 1), send(own_b, "section", 2)
        yield
        parts = len(products[0])
        family, layer = group % 2, 1 - group // 2
        result = ((2, width, columns // parts), F32, "raw")
        before = outputs.get(family)
        done = order.call(
            functools.partial(finish, layer, parts, (slot_x, slot_y), 2 * parts),
            [own_a, got_a, own_b, got_b] + [Raw(one) for one in before or ()],
            [result] * (2 * parts),
            [pltpu.VMEM((width // 2, columns // parts), F32)] * (4 * parts),
            moves=4 * parts,
            limit=40,
            update={at: 4 + at for at in range(2 * parts)} if before else None,
        )
        outputs[family] = done

    def small_stages():
        (packed,) = order.call(
            pack_small,
            [small_entry(step) for step in range(passes)] + [small_middle(step) for step in range(passes)],
            [((-(-(8 + passes) // 8) * 8, width), F32)], limit=8
        )
        hops = [("section", 1), ("section", 2)] + [("dp", bits) for bits in dp_bits]
        for axis, bits in hops[:-1]:
            got = lax.ppermute(packed, axis, xor_pairs(axis, bits))
            yield
            (packed,) = order.call(add_small, [packed, got], [(packed.shape, F32)], limit=8)
        axis, bits = hops[-1]
        got = lax.ppermute(packed, axis, xor_pairs(axis, bits))
        yield
        outputs["small"] = order.call(
            part_small,
            [packed, got],
            [((2, width), F32)] * 4 + [((passes, width), F32)],
            limit=8,
        )

    def input_stages(entered_t):
        pieces = entered_t.reshape(section_count, slice_width, half_rows)
        got = exchange([pick(pieces, section ^ bits) for bits in range(section_count)])
        yield
        (grad_t,) = order.call(
            place_items,
            [Raw(one) for one in got],
            [((batches, slice_width, half_rows), F32, "raw")],
            [pltpu.VMEM((section_count, slice_width, half_rows), F32)],
            moves=section_count + 1,
            limit=8,
        )
        outputs["inputs"] = jnp.swapaxes(grad_t, 1, 2)

    running = {}

    def advance(name):
        if name not in running:
            running[name] = stages(name)
        next(running[name], None)

    for step in reversed(range(1, passes)):
        fed = feed_step(step)
        if step == passes - 1:
            passes_got = exchange([pick(results, section ^ bits) for bits in range(section_count)])
        if step == 1:
            advance(0)
        state = attention_step(step, fed)
        if step == passes - 1:
            (passes_out,) = order.call(
                place_passes,
                [Scalars(counts)] + [Raw(one) for one in passes_got],
                [((batches, half_rows, width), F32)],
                [pltpu.VMEM((section_count, half_rows, width), F32)],
                moves=section_count,
                limit=16,
            )
    fed = feed_step(0)
    state = attention_step(0, fed)
    near_dr, part, other = state
    (entered_t,) = order.call(
        entry_backward,
        [Near(part), Near(other), Near(near_dr), entered(0), gain_one],
        [((width, half_rows), F32), small_entry(0)],
        [entry_v],
    )
    running["small"] = small_stages()
    running["inputs"] = input_stages(entered_t)
    for name in schedule(len(dp_bits)):
        advance(name)
    for name in running:
        for _ in running[name]:
            pass
    up, down = outputs[0]
    query, key, out, value = outputs[1]
    return (
        passes_out[None],
        outputs["inputs"],
        query,
        key,
        value,
        out,
        up,
        down,
        *outputs["small"],
    )


def solution(mesh):
    weight = P(None, None, "tensor")
    return jax.shard_map(
        shards,
        mesh=mesh,
        in_specs=(
            P("dp", "tensor", "section"),
            P("dp"),
            weight,
            weight,
            weight,
            weight,
            weight,
            weight,
            P(),
            P(),
            P(),
            P(),
            P(),
            P("section", "dp", "tensor", None),
        ),
        out_specs=(
            P("section", "dp", "tensor", None),
            P("dp", "tensor", "section"),
            weight,
            weight,
            weight,
            weight,
            weight,
            weight,
            P(),
            P(),
            P(),
            P(),
            P(),
        ),
        check_vma=False,
    )
```

```python
import functools

import jax
import jax.numpy as jnp
from jax import lax
from jax.experimental import pallas as pl
from jax.experimental.pallas import tpu as pltpu
from jax.sharding import PartitionSpec as P

HEADS = 12
EPSILON = 1e-05
MASKED = -1e30
F32 = jnp.float32
BF16 = jnp.bfloat16
ROOT = 0.7978845608028654
CUBIC = 0.044715
NN = (((1,), (0,)), ((), ()))
NT = (((1,), (1,)), ((), ()))
TN = (((0,), (0,)), ((), ()))


def dot(left, right, dims=NN):
    return lax.dot_general(left, right, dims, preferred_element_type=F32)


def norm_parts(rows):
    centred = rows - jnp.mean(rows, axis=-1, keepdims=True)
    spread = jnp.mean(centred * centred, axis=-1, keepdims=True)
    inverse = lax.rsqrt(spread + EPSILON)
    return centred * inverse, inverse


def norm_back(rows, gain, grad):
    normal, inverse = norm_parts(rows)
    scaled = gain * grad
    middle = jnp.mean(scaled, axis=-1, keepdims=True)
    along = jnp.mean(scaled * normal, axis=-1, keepdims=True)
    back = inverse * (scaled - middle - normal * along)
    gain_sum = jnp.sum(grad * normal, axis=0, keepdims=True)
    bias_sum = jnp.sum(grad, axis=0, keepdims=True)
    return back, gain_sum, bias_sum


def both(own, other):
    return own[...].astype(F32) + other[...].astype(F32)


class Incoming:
    def __init__(self, source, place, sem):
        self.copy = pltpu.make_async_copy(source, place, sem)
        self.copy.start()
        self.place = place
        self.waiting = True

    def ref(self):
        if self.waiting:
            self.copy.wait()
            self.waiting = False
        return self.place

    def __getitem__(self, index):
        return self.ref()[index]


class Outgoing:
    def __init__(self, place, target, sem):
        self.place = place
        self.copy = pltpu.make_async_copy(place, target, sem)

    def put(self, value):
        self.place[...] = value
        self.copy.start()

    def __getitem__(self, index):
        return self.place[index]

    def __setitem__(self, index, value):
        self.place[index] = value


class Chosen:
    def __init__(self, array, index):
        self.array, self.index = array, index


class Near:
    def __init__(self, array):
        self.array = array


class Held:
    def __init__(self, name, *index):
        self.name, self.index = name, index


class Raw:
    def __init__(self, array):
        self.array = array


class Far(Raw):
    pass


class Scalars:
    def __init__(self, array):
        self.array = array


class Mover:
    def __init__(self, sems):
        self.sems, self.used = sems, 0

    def start(self, source, target):
        copy = pltpu.make_async_copy(source, target, self.sems.at[self.used])
        self.used += 1
        copy.start()
        return copy


class Order:
    def __init__(self, shapes):
        self.shapes = shapes
        self.stores = {}

    def call(self, body, operands, outs, scratch=(), limit=20, moves=0, update=None, name=None):
        inner = body
        while isinstance(inner, functools.partial):
            inner = inner.func
        name = name or inner.__name__
        kind = lambda one: one[2] if isinstance(one, tuple) and len(one) > 2 else "staged"
        plain = lambda one: not isinstance(one, (Near, Raw, Scalars))
        names = ["order"] + [one.name for one in operands + outs if isinstance(one, Held)]
        names = list(dict.fromkeys(names))
        old = [name for name in names if name in self.stores]
        new = [name for name in names if name not in self.stores]
        given = [one for one in operands if not isinstance(one, Held)]
        made = [one for one in outs if not isinstance(one, Held)]
        arrays = [one.array if isinstance(one, (Chosen, Near, Raw, Scalars)) else one for one in given]

        def shape_of(one):
            if isinstance(one, Held):
                shape, dtype = self.shapes[one.name]
                for index in one.index:
                    if isinstance(index, int):
                        shape = shape[1:]
                    else:
                        sizes = [
                            cut.stop - cut.start if isinstance(cut, slice) else cut for cut in index
                        ]
                        shape = tuple(sizes) + tuple(shape[len(sizes) :])
                return shape, dtype
            if isinstance(one, Chosen):
                return one.array.shape[1:], one.array.dtype
            if isinstance(one, tuple):
                return one[0], one[1]
            return one.shape, one.dtype

        places = [pltpu.VMEM(*shape_of(one)) for one in operands if plain(one)]
        places += [pltpu.VMEM(*shape_of(one)) for one in outs if kind(one) == "staged"]
        first_out = len(old) + len(given)
        total = first_out + len(names) + len(made)
        count = len(places)

        def part(stores, one):
            ref = stores[one.name]
            for index in one.index:
                ref = ref.at[index]
            return ref

        def kernel(*refs):
            in_refs = list(refs[len(old) : first_out])
            stores = dict(zip(old + new, refs[first_out : first_out + len(names)]))
            out_refs = list(refs[first_out + len(names) : total])
            rooms = refs[total : total + count]
            sems, more = refs[total + count], refs[total + count + 1]
            rest = refs[total + count + 2 :]
            ins, results = [], []
            at = 0
            for one in operands:
                ref = part(stores, one) if isinstance(one, Held) else in_refs.pop(0)
                if plain(one):
                    source = ref.at[one.index] if isinstance(one, Chosen) else ref
                    ins.append(Incoming(source, rooms[at], sems.at[at]))
                    at += 1
                else:
                    ins.append(ref)
            for one in outs:
                ref = part(stores, one) if isinstance(one, Held) else out_refs.pop(0)
                if kind(one) == "staged":
                    results.append(Outgoing(rooms[at], ref, sems.at[at]))
                    at += 1
                else:
                    results.append(ref)
            extra = (Mover(more),) if moves else ()
            body(ins, results, *extra, *rest)
            for one in ins:
                if isinstance(one, Incoming):
                    one.ref()
            for one in results:
                if isinstance(one, Outgoing):
                    one.copy.wait()

        anywhere = pl.BlockSpec(memory_space=pl.ANY)
        inside = pl.BlockSpec(memory_space=pltpu.VMEM)
        scalar = pl.BlockSpec(memory_space=pltpu.SMEM)
        spec = lambda one: inside if isinstance(one, Near) else scalar if isinstance(one, Scalars) else anywhere
        aliases = {at: at for at in range(len(old))}
        for out_at, in_at in (update or {}).items():
            shift_in = sum(isinstance(one, Held) for one in operands[:in_at])
            shift_out = sum(isinstance(one, Held) for one in outs[:out_at])
            aliases[len(old) + in_at - shift_in] = len(names) + out_at - shift_out
        shapes = [pltpu.HBM(*self.shapes[name]) for name in old + new]
        for one in made:
            form = pltpu.VMEM if kind(one) == "near" else jax.ShapeDtypeStruct
            shapes.append(form(one[0], one[1]))
        arrays = [
            pltpu.with_memory_space_constraint(array, pltpu.VMEM)
            if isinstance(one, Near)
            else pltpu.with_memory_space_constraint(array, pltpu.HBM)
            if isinstance(one, (Chosen, Far)) or array.size * array.dtype.itemsize < 20000
            and not isinstance(one, (Raw, Scalars))
            else array
            for one, array in zip(given, arrays)
        ]
        done = pl.pallas_call(
            kernel,
            name=name,
            out_shape=tuple(shapes),
            in_specs=[anywhere] * len(old) + [spec(one) for one in given],
            out_specs=(anywhere,) * len(names)
            + tuple(inside if kind(one) == "near" else anywhere for one in made),
            scratch_shapes=places
            + [pltpu.SemaphoreType.DMA((max(count, 1),)), pltpu.SemaphoreType.DMA((max(moves, 1),))]
            + list(scratch),
            input_output_aliases=aliases,
            compiler_params=pltpu.CompilerParams(vmem_limit_bytes=int(limit * 1024 * 1024)),
            cost_estimate=pl.CostEstimate(flops=1000, bytes_accessed=1000, transcendentals=0),
        )(
            *[pltpu.with_memory_space_constraint(self.stores[name], pltpu.HBM) for name in old],
            *arrays,
        )
        self.stores.update(zip(old + new, done[: len(names)]))
        return done[len(names) :]


class Place:
    def __getitem__(self, slot):
        name, bits = slot
        return (lax.axis_index(name) // bits) % 2 if bits else lax.axis_index(name)


HERE = Place()


def causal_mask(length):
    key_place = lax.broadcasted_iota(jnp.int32, (length, length), 0)
    query_place = lax.broadcasted_iota(jnp.int32, (length, length), 1)
    return key_place <= query_place


def lane_half(half, pair):
    lane = lax.broadcasted_iota(jnp.int32, pair.shape, 1)
    keep = (lane < 64) if half == 0 else (lane >= 64)
    return jnp.where(keep, pair, jnp.zeros_like(pair))


def present_in(counts, step):
    item = lax.axis_index("section")
    last = counts.shape[0] - 1
    own_count = jnp.where(item <= last, counts[jnp.minimum(item, last)], 0)
    return jnp.where(own_count > step, 1.0, 0.0).astype(F32)


def attention_forward(step, layer, ins, outs, mover, turned, *rest):
    count = 2 if step == 0 else 3
    first, (embed, gain, bias, wq, wk, wv, wo) = ins[:count], ins[count : count + 7]
    past_k, past_vt = ins[count + 7 : count + 7 + step], ins[count + 7 + step : count + 7 + 2 * step]
    sent = None
    if step == 0:
        own_t, other_t = first
        (entry_v,) = rest
        half = own_t.shape[1]
        place = pl.multiple_of(lax.axis_index("tensor") * half, half)
        entry_v[pl.ds(place, half), :] = own_t[...].T
        entry_v[pl.ds(pl.multiple_of(half - place, half), half), :] = other_t[...].T
        entered = entry_v[...] + embed[0:1, :]
    else:
        near_r, own, other = first
        counts = ins[count + 7 + 2 * step]
        (entry_v,) = rest
        result = near_r[...] + both(own, other)
        entry_v[...] = result * present_in(counts, step - 1)
        half = entry_v.shape[0] // 2
        place = pl.multiple_of(lax.axis_index("tensor") * half, half)
        sent = mover.start(entry_v.at[pl.ds(place, half)], outs[0].at[step - 1])
        outs = outs[1:]
        entered = result + embed[step : step + 1, :]
    near_out = outs[0]
    near_out[...] = entered
    outs = outs[1:]
    u_out, a_out, q_out, k_out, kt_out, v_out, vt_out, lse_out, o_out, part_out = outs
    u_out.put(entered)
    normal, _ = norm_parts(entered)
    a = (normal * gain[layer : layer + 1, :] + bias[layer : layer + 1, :]).astype(BF16)
    a_out.put(a)
    q_out.put((dot(a, wq[layer]).astype(BF16).astype(F32) * 0.125).astype(BF16))
    k_full = dot(a, wk[layer])
    k_out.put(k_full.astype(BF16))
    v_full = dot(a, wv[layer])
    vt_out.put(v_full.T.astype(BF16))
    v_out.put(v_full.astype(BF16))
    kt_out.put(k_full.T.astype(BF16))
    length = entered.shape[0]
    seen = causal_mask(length)
    all_k = past_k + [k_out]
    all_vt = past_vt + [vt_out]
    pairs = wq.shape[2] // 128

    def one_pair(pair, carry):
        lanes = pl.ds(pl.multiple_of(128 * pair, 128), 128)
        for half in range(2):
            query = lane_half(half, q_out[:, lanes])
            scores = [jnp.where(seen, dot(key[:, lanes], query, NT), MASKED) for key in all_k]
            highest = functools.reduce(
                jnp.maximum, [jnp.max(one, axis=0, keepdims=True) for one in scores]
            )
            powers = [jnp.exp(one - highest) for one in scores]
            total = functools.reduce(
                jnp.add, [jnp.sum(one, axis=0, keepdims=True) for one in powers]
            )
            inverse = 1.0 / total
            lse_out[pl.ds(2 * pair + half, 1), :] = highest + jnp.log(total)
            rows = pl.ds(pl.multiple_of(128 * pair + 64 * half, 64), 64)
            mixed = None
            for power, value in zip(powers, all_vt):
                term = dot(value[rows, :], (power * inverse).astype(BF16))
                mixed = term if mixed is None else mixed + term
            turned[rows, :] = mixed
        return carry

    for one in past_k + past_vt:
        one.ref()
    lax.fori_loop(0, pairs, one_pair, 0)
    lse_out.copy.start()
    o = turned[...].T.astype(BF16)
    part_out[...] = dot(o, wo[layer], NT).astype(BF16)
    o_out.put(o)
    if sent is not None:
        sent.wait()


def gelu_parts(hidden):
    square = hidden * hidden
    bent = jnp.tanh(ROOT * hidden * (1.0 + CUBIC * square))
    return square, bent


def feed_forward(layer, ins, outs):
    own, other, u, gain, bias, wu, wd = ins[:7]
    near_out, r_out, b_out, g_out, m_out, part_out = outs[:6]
    middle = u[...] + both(own, other)
    near_out[...] = middle
    r_out.put(middle)
    normal, _ = norm_parts(middle)
    b = (normal * gain[layer : layer + 1, :] + bias[layer : layer + 1, :]).astype(BF16)
    b_out.put(b)
    hidden = dot(b, wu[layer])
    g_out.put(hidden)
    _, bent = gelu_parts(hidden)
    m = (0.5 * hidden * (1.0 + bent)).astype(BF16)
    m_out.put(m)
    part_out[...] = dot(m, wd[layer], NT).astype(BF16)


def small_put(out, rows):
    rows = rows + [jnp.zeros_like(rows[0])] * (8 - len(rows))
    out.put(jnp.concatenate(rows, axis=0))


def feed_backward(step, layer, last, ins, outs, mover, cot_v, *more):
    counts, cot_own, cot_other, wd, g, wu = ins[:6]
    near_out, e_out, dg_out, part_out = outs[:4]
    half = cot_v.shape[0] // 2
    place = pl.multiple_of(lax.axis_index("tensor") * half, half)
    copies = [
        mover.start(cot_own.at[step], cot_v.at[pl.ds(place, half)]),
        mover.start(cot_other.at[step], cot_v.at[pl.ds(pl.multiple_of(half - place, half), half)]),
    ]
    present = present_in(counts, step)
    if last:
        near_r, own, other = ins[6:]
        (end_v,) = more
        end_v[...] = (near_r[...] + both(own, other)) * present
        sent = mover.start(end_v.at[pl.ds(place, half)], outs[4].at[step])
    else:
        own, other, dr, u, gain = ins[6:]
        back, gain_sum, bias_sum = norm_back(u[...], gain[1:2, :], both(own, other))
        entered = dr[...] + back
        small_put(outs[4], [gain_sum, bias_sum, jnp.sum(entered, axis=0, keepdims=True)])
    for copy in copies:
        copy.wait()
    grad = cot_v[...].astype(F32) * present
    if not last:
        grad = grad + entered
    near_out[...] = grad
    e = grad.astype(BF16)
    e_out.put(e)
    raw = dot(e, wd[layer])
    hidden = g[...]
    square, bent = gelu_parts(hidden)
    slope = 0.5 * (1.0 + bent) + 0.5 * hidden * (1.0 - bent * bent) * ROOT * (
        1.0 + 3.0 * CUBIC * square
    )
    dg = (raw * slope).astype(BF16)
    dg_out.put(dg)
    part_out[...] = dot(dg, wu[layer], NT).astype(BF16)
    if last:
        sent.wait()


def attention_backward(step, layer, last, ins, outs, do_v, dqt_v):
    own, other, dh, r, gain, wo, q, lse = ins[:8]
    count = step + 1
    keys, values, keys_t = ins[8 : 8 + count], ins[8 + count : 8 + 2 * count], ins[8 + 2 * count : 8 + 3 * count]
    rest = ins[8 + 3 * count :]
    if not last:
        dk_in, dv_in = rest[:2]
    wq, wk, wv = rest[-3:]
    near_out, f_out, dq_out, dk_out, dv_out, part_out, small_out = outs[:7]
    if step > 0:
        dk_all, dv_all = outs[7:]
    back, gain_sum, bias_sum = norm_back(r[...], gain[layer : layer + 1, :], both(own, other))
    small_put(small_out, [gain_sum, bias_sum])
    grad = dh[...] + back
    near_out[...] = grad
    f = grad.astype(BF16)
    f_out.put(f)
    do_v[...] = dot(f, wo[layer]).astype(BF16)
    length = f.shape[0]
    seen = causal_mask(length)
    pairs = q.place.shape[1] // 128

    def one_pair(pair, carry):
        lanes = pl.ds(pl.multiple_of(128 * pair, 128), 128)
        key_sums = [None] * count
        value_sums = [None] * count
        for half in range(2):
            rows = pl.ds(pl.multiple_of(128 * pair + 64 * half, 64), 64)
            query = lane_half(half, q[:, lanes])
            grad_mix = lane_half(half, do_v[:, lanes])
            total = lse[pl.ds(2 * pair + half, 1), :]
            exact = [
                jnp.exp(jnp.where(seen, dot(key[:, lanes], query, NT), MASKED) - total)
                for key in keys
            ]
            grad_weights = [dot(value[:, lanes], grad_mix, NT) for value in values]
            delta = functools.reduce(
                jnp.add,
                [jnp.sum(p * dp, axis=0, keepdims=True) for p, dp in zip(exact, grad_weights)],
            )
            query_grad = None
            for slot in range(count):
                grad_scores = (exact[slot] * (grad_weights[slot] - delta)).astype(BF16)
                term = dot(keys_t[slot][rows, :], grad_scores)
                query_grad = term if query_grad is None else query_grad + term
                key_term = dot(grad_scores, query)
                value_term = dot(exact[slot].astype(BF16), grad_mix)
                if half == 0:
                    key_sums[slot] = key_term
                    value_sums[slot] = value_term
                else:
                    key_sums[slot] = key_sums[slot] + key_term
                    value_sums[slot] = value_sums[slot] + value_term
            dqt_v[rows, :] = query_grad
        for slot in range(count):
            key_sum, value_sum = key_sums[slot], value_sums[slot]
            if not last:
                key_sum = key_sum + dk_in[slot, :, lanes]
                value_sum = value_sum + dv_in[slot, :, lanes]
            if slot == step:
                dk_out[:, lanes] = key_sum.astype(BF16)
                dv_out[:, lanes] = value_sum.astype(BF16)
            else:
                dk_all[slot, :, lanes] = key_sum
                dv_all[slot, :, lanes] = value_sum
        return carry

    for one in [q, lse] + keys + values + keys_t + ([] if last else [dk_in, dv_in]):
        one.ref()
    lax.fori_loop(0, pairs, one_pair, 0)
    dq = (dqt_v[...].T * 0.125).astype(BF16)
    part = dot(dq, wq[layer], NT) + dot(dk_out[...], wk[layer], NT) + dot(dv_out[...], wv[layer], NT)
    part_out[...] = part.astype(BF16)
    dq_out.put(dq)
    for one in (dk_out, dv_out) + ((dk_all, dv_all) if step > 0 else ()):
        one.copy.start()


def entry_backward(ins, outs, mover, entry_v, pieces_v):
    own, other, dr, u, gain = ins
    back, gain_sum, bias_sum = norm_back(u[...], gain[0:1, :], both(own, other))
    entered = dr[...] + back
    entry_v[...] = entered
    half = entry_v.shape[0] // 2
    place = pl.multiple_of(lax.axis_index("tensor") * half, half)
    turned = entry_v[pl.ds(place, half), :].T
    pieces_v[...] = turned.reshape(pieces_v.shape)
    section = lax.axis_index("section")
    copies = [mover.start(pieces_v.at[section ^ bits], out) for bits, out in enumerate(outs[1:])]
    small_put(outs[0], [gain_sum, bias_sum, jnp.sum(entered, axis=0, keepdims=True)])
    for copy in copies:
        copy.wait()


def place_items(ins, outs, mover, room):
    section = lax.axis_index("section")
    copies = [mover.start(piece, room.at[section ^ bits]) for bits, piece in enumerate(ins)]
    for copy in copies:
        copy.wait()
    mover.start(room.at[pl.ds(0, outs[0].shape[0])], outs[0]).wait()


def place_pieces(ins, outs, mover):
    rows = ins[0].shape[0]
    copies = []
    for bits, piece in enumerate(ins):
        at = pl.multiple_of((lax.axis_index("section") ^ bits) * rows, rows)
        copies.append(mover.start(piece, outs[0].at[pl.ds(at, rows)]))
    for copy in copies:
        copy.wait()


def split_items(ins, outs, mover):
    last = ins[0].shape[0] - 1
    section = lax.axis_index("section")
    copies = [
        mover.start(ins[0].at[jnp.minimum(section ^ bits, last)], out)
        for bits, out in enumerate(outs)
    ]
    for copy in copies:
        copy.wait()


def load(ins, outs, mover, rooms, sent):
    weights = len(ins) - 1
    last = ins[-1].shape[1] - 1
    section = lax.axis_index("section")
    first = [
        mover.start(ins[-1].at[0].at[jnp.minimum(section ^ bits, last)], rooms.at[bits])
        for bits in range(rooms.shape[0])
    ]
    copies = [mover.start(source, target) for source, target in zip(ins[:-1], outs)]
    for bits, out in enumerate(outs[weights:]):
        first[bits].wait()
        sent[bits] = rooms[bits].astype(BF16)
        copies.append(mover.start(sent.at[bits], out))
    for copy in copies:
        copy.wait()


def pack_small(ins, outs):
    passes = (len(ins)) // 2
    entry, middle = ins[:passes], ins[passes:]
    rows = []
    for kind in (entry, middle):
        for row in range(2):
            rows.append(kind[0][row : row + 1, :])
            later = kind[1][row : row + 1, :]
            for step in range(2, passes):
                later = later + kind[step][row : row + 1, :]
            rows.append(later)
    rows += [entry[step][2:3, :] for step in range(passes)]
    rows += [jnp.zeros_like(rows[0])] * (-len(rows) % 8)
    outs[0].put(jnp.concatenate(rows, axis=0))


def add_small(ins, outs):
    outs[0].put(ins[0][...] + ins[1][...])


def part_small(ins, outs):
    total = ins[0][...] + ins[1][...]
    at = 0
    for out in outs:
        count = out.place.shape[0]
        out.put(total[at : at + count])
        at += count


def halves(slot, room, axis):
    size = room.shape[axis] // 2
    kept = pl.multiple_of(HERE[slot] * size, size)
    sent = pl.multiple_of(size - kept, size)
    if axis == 0:
        return room.at[pl.ds(kept, size)], room.at[pl.ds(sent, size)]
    return room.at[:, pl.ds(kept, size)], room.at[:, pl.ds(sent, size)]


def weight_first(products, splits, sharing, ins, outs, mover, *rooms):
    factors = ins
    copies = []
    for at, (room, slot) in enumerate(zip(rooms, splits)):
        column = 0
        for pairs in products[at]:
            total = None
            for left, right in pairs:
                term = dot(factors[left][...], factors[right][...], TN)
                total = term if total is None else total + term
            room[:, column : column + total.shape[1]] = total.astype(BF16)
            column += total.shape[1]
        kept, sent = halves(slot, room, 0)
        columns = room.shape[1] // sharing
        for one in range(sharing):
            across = (slice(None), pl.ds(one * columns, columns))
            copies.append(mover.start(sent.at[across], outs[4 * one + 2 * at + 1]))
            copies.append(mover.start(kept.at[across], outs[4 * one + 2 * at]))
    for copy in copies:
        copy.wait()


def add_split(slots, axis, ins, outs, mover, *rooms):
    copies = []
    for at, (room, slot) in enumerate(zip(rooms, slots)):
        room[...] = (ins[2 * at][...].astype(F32) + ins[2 * at + 1][...].astype(F32)).astype(BF16)
        kept, sent = halves(slot, room, axis)
        copies.append(mover.start(sent, outs[2 * at + 1]))
        copies.append(mover.start(kept, outs[2 * at]))
    for copy in copies:
        copy.wait()


def add_merge(slot, axis, ins, outs, mover, room):
    columns = room.shape[1] // 2
    for at in range(2):
        total = ins[2 * at][...].astype(F32) + ins[2 * at + 1][...].astype(F32)
        room[:, at * columns : (at + 1) * columns] = total.astype(BF16)
    kept, sent = halves(slot, room, axis)
    copies = [mover.start(sent, outs[1]), mover.start(kept, outs[0])]
    for copy in copies:
        copy.wait()


def add_last(ins, outs):
    outs[0].put((ins[0][...].astype(F32) + ins[1][...].astype(F32)).astype(BF16))


def join(slots, axis, ins, outs, mover):
    copies = []
    for at, slot in enumerate(slots):
        own, other = halves(slot, outs[at], axis)
        copies.append(mover.start(ins[2 * at], own))
        copies.append(mover.start(ins[2 * at + 1], other))
    for copy in copies:
        copy.wait()


def join_part(slot, axis, ins, outs, mover, room):
    own, other = halves(slot, room, axis)
    copies = [mover.start(ins[0], own), mover.start(ins[1], other)]
    for copy in copies:
        copy.wait()
    columns = room.shape[1] // 2
    copies = [mover.start(room.at[:, pl.ds(at * columns, columns)], outs[at]) for at in range(2)]
    for copy in copies:
        copy.wait()


def finish(layer, parts, slots, starts, ins, outs, mover, *rooms):
    halves_in = ins[:4]
    copies = []
    out_at = 0
    for at, slot in enumerate(slots):
        rows = halves_in[2 * at].place.shape[0]
        for which in range(2):
            place = HERE[slot] * rows
            place = pl.multiple_of(place if which == 0 else rows - place, rows)
            column = 0
            for part in range(parts):
                room = rooms[2 * (out_at + part) + which]
                columns = room.shape[1]
                room[...] = halves_in[2 * at + which][:, column : column + columns].astype(F32)
                target = outs[out_at + part].at[layer]
                across = pl.ds(starts[out_at + part], columns)
                copies.append(mover.start(room, target.at[pl.ds(place, rows), across]))
                column += columns
        out_at += parts
    for copy in copies:
        copy.wait()


def swap(value):
    return lax.ppermute(value, "tensor", [(0, 1), (1, 0)])


def xor_pairs(axis, bits):
    return [(place, place ^ bits) for place in range(lax.axis_size(axis))]


def pick(stacked, index):
    return lax.dynamic_index_in_dim(stacked, index, 0, keepdims=False)


SPLITS = (2, 2)
CHAIN, SMALL, INPUTS = 6, 7, 8
STEPS = (
    6, 0, 1, 6, 2, 6, 0, 6, 3, 0, 1, 2, 1, 0, 6, 0, 0, 4, 2, 1,
    3, 7, 1, 4, 8, 2, 1, 5, 1, 7, 2, 4, 7, 3, 2, 0, 7, 4, 1, 3,
    5, 2, 0, 4, 3, 7, 4, 5, 3, 1, 2, 4, 5, 0, 3, 5, 4, 2, 3, 5,
    5, 4, 5, 3, 5,
)


def schedule(levels, groups):
    names = {CHAIN: "chain", SMALL: "small", INPUTS: "inputs"}
    if levels == 2 and groups == sum(SPLITS) + 2:
        return [names.get(step, step) for step in STEPS]
    order = ["chain"]
    order += list(range(SPLITS[1])) + ["chain", SPLITS[1]]
    order += ["chain"] * 3
    for step in range(2 * levels + 5):
        order += list(range(groups))
    return order


def shards(
    inputs,
    counts,
    w_query,
    w_key,
    w_value,
    w_out,
    w_up,
    w_down,
    gain_one,
    bias_one,
    gain_two,
    bias_two,
    pass_embed,
    cotangent,
):
    section_count = lax.axis_size("section")
    section = lax.axis_index("section")
    tensor = lax.axis_index("tensor")
    batches, half_rows, slice_width = inputs.shape
    length = 2 * half_rows
    width = cotangent.shape[3]
    head_width = w_query.shape[2]
    hidden_width = w_up.shape[2]
    passes = pass_embed.shape[0]
    dp_count = lax.axis_size("dp")
    dp_place = lax.axis_index("dp")
    dp_bits = [1 << level for level in range(dp_count.bit_length() - 1)]
    order = Order(
        {
            "order": ((2, passes, length, head_width), F32),
            "low": ((passes, 4, length, width), BF16),
            "hidden": ((passes, 2, length, hidden_width), BF16),
            "heads": ((passes, 7, length, head_width), BF16),
            "turned": ((passes, 4, head_width, length), BF16),
            "wide": ((passes, 2 * length + 24, width), F32),
            "before": ((passes, length, hidden_width), F32),
        }
    )

    def exchange(pieces):
        return [pieces[0]] + [
            lax.ppermute(pieces[bits], "section", xor_pairs("section", bits))
            for bits in range(1, section_count)
        ]

    slot_x, slot_y = ("section", 1), ("section", 2)
    slots_dp = [("dp", bits) for bits in dp_bits]

    inputs_t = jnp.swapaxes(inputs, 1, 2)
    got = exchange(
        order.call(
            split_items,
            [Far(inputs_t)],
            [((slice_width, half_rows), F32, "raw")] * section_count,
            moves=section_count,
            limit=4,
        )
    )
    weights = (w_query, w_key, w_value, w_out, w_up, w_down)
    w_query, w_key, w_value, w_out, w_up, w_down, *cot_sent = order.call(
        load,
        [Far(one) for one in weights] + [Far(cotangent)],
        [(one.shape, one.dtype, "near") for one in weights]
        + [((half_rows, width), BF16, "raw")] * section_count,
        [pltpu.VMEM((section_count, half_rows, width), kind) for kind in (F32, BF16)],
        moves=len(weights) + 2 * section_count,
        limit=8,
    )
    (entry_t,) = order.call(
        place_pieces,
        [Raw(one) for one in got],
        [((width, half_rows), F32, "near")],
        moves=section_count,
        limit=8,
    )
    entry_other = swap(entry_t)
    cot_got = exchange(cot_sent)

    wide_near = ((length, width), F32, "near")
    part_near = ((length, width), BF16, "near")
    stacked = ((passes, half_rows, width), F32, "raw")
    turned = pltpu.VMEM((head_width, length), F32)
    entry_v = pltpu.VMEM((length, width), F32)
    cot_v = pltpu.VMEM((length, width), BF16)
    whole = slice(None)

    def low(step, name):
        return Held("low", step, "abef".index(name))

    def hidden(step, name):
        return Held("hidden", step, ("m", "dg").index(name))

    def heads(step, name):
        return Held("heads", step, ("q", "k", "v", "o", "dq", "dk", "dv").index(name))

    def turn(step, name):
        return Held("turned", step, ("kt", "vt").index(name))

    def rows(step, start, count, columns=None):
        cut = (slice(start, start + count), slice(0, columns or width))
        return Held("wide", step, cut)

    def entered(step):
        return rows(step, 0, length)

    def middle(step):
        return rows(step, length, length)

    def logsum(step):
        return rows(step, 2 * length, 8, length)

    def small_entry(step):
        return rows(step, 2 * length + 8, 8)

    def small_middle(step):
        return rows(step, 2 * length + 16, 8)

    results = None
    resid = None
    cot_own = cot_other = None
    for step in range(passes):
        layer = min(step, 1)
        first = [Near(entry_t), Near(entry_other)] if step == 0 else [Near(one) for one in resid]
        weights = [Near(one) for one in (w_query, w_key, w_value, w_out)]
        operands = first + [pass_embed, gain_one, bias_one] + weights
        operands += [heads(past, "k") for past in range(step)]
        operands += [turn(past, "vt") for past in range(step)]
        update = None
        if step > 0:
            operands.append(Scalars(counts))
        if step > 1:
            operands.append(Raw(results))
            update = {0: len(operands) - 1}
        done = order.call(
            functools.partial(attention_forward, step, layer),
            operands,
            ([] if step == 0 else [stacked])
            + [wide_near, entered(step), low(step, "a"), heads(step, "q"), heads(step, "k")]
            + [turn(step, "kt"), heads(step, "v"), turn(step, "vt"), logsum(step)]
            + [heads(step, "o"), part_near],
            [turned, entry_v],
            moves=1,
            update=update,
        )
        if step > 0:
            results = done[0]
            done = done[1:]
        near_u, part = done
        if step == min(2, passes - 1):
            (cot_flat,) = order.call(
                place_pieces,
                [Raw(one) for one in cot_got],
                [((section_count * half_rows, width), BF16, "raw")],
                moves=section_count,
                limit=4,
            )
            cot_own = cot_flat.reshape(section_count, half_rows, width)
            cot_other = swap(cot_own)
        near_r, part_two = order.call(
            functools.partial(feed_forward, layer),
            [Near(part), Near(swap(part)), Near(near_u), gain_two, bias_two]
            + [Near(w_up), Near(w_down)],
            [wide_near, middle(step), low(step, "b"), Held("before", step), hidden(step, "m"), part_near],
        )
        resid = (near_r, part_two, swap(part_two))

    factors = [
        {name: low(step, name) for name in "abef"}
        | {name: hidden(step, name) for name in ("m", "dg")}
        | {name: heads(step, name) for name in ("o", "dq", "dk", "dv")}
        for step in range(passes)
    ]
    state = None

    def feed_step(step):
        nonlocal results
        layer = min(step, 1)
        last = step == passes - 1
        operands = [Scalars(counts), Raw(cot_own), Raw(cot_other)]
        operands += [Near(w_down), Held("before", step), Near(w_up)]
        outs = [wide_near, low(step, "e"), hidden(step, "dg"), part_near]
        update = None
        if last:
            operands += [Near(one) for one in resid]
            outs += [stacked]
            operands.append(Raw(results))
            update = {4: len(operands) - 1}
        else:
            dr, part, other = state
            operands += [Near(part), Near(other), Near(dr), entered(step + 1), gain_one]
            outs += [small_entry(step + 1)]

        def body(ins, outs, mover, *rooms):
            feed_backward(step, layer, last, ins[:9] if last else ins, outs, mover, *rooms)

        done = order.call(
            body,
            operands,
            outs,
            [cot_v] + ([entry_v] if last else []),
            moves=3,
            update=update,
            name=feed_backward.__name__,
        )
        near_dh, part = done[:2]
        if last:
            results = done[2]
        return near_dh, part, swap(part)

    def attention_step(step, fed):
        layer = min(step, 1)
        last = step == passes - 1
        near_dh, part, other = fed
        operands = [Near(part), Near(other), Near(near_dh), middle(step), gain_two]
        operands += [Near(w_out), heads(step, "q"), logsum(step)]
        operands += [heads(past, "k") for past in range(step + 1)]
        operands += [heads(past, "v") for past in range(step + 1)]
        operands += [turn(past, "kt") for past in range(step + 1)]
        cut = (slice(0, step + 1),)
        if not last:
            operands += [Held("order", at, cut) for at in range(2)]
        operands += [Near(one) for one in (w_query, w_key, w_value)]
        outs = [wide_near, low(step, "f"), heads(step, "dq"), heads(step, "dk"), heads(step, "dv")]
        outs += [part_near, small_middle(step)]
        if step > 0:
            outs += [Held("order", at, (slice(0, step),)) for at in range(2)]
        near_dr, part = order.call(
            functools.partial(attention_backward, step, layer, last),
            operands,
            outs,
            [pltpu.VMEM((length, head_width), BF16), turned],
        )
        return near_dr, part, swap(part)

    later, early = list(range(1, passes)), [0]
    def feed_group(steps, start):
        first = [("up", start, [(low(step, "b"), hidden(step, "dg")) for step in steps])]
        second = [("down", start, [(low(step, "e"), hidden(step, "m")) for step in steps])]
        return (first, second)

    def heads_group(steps):
        def product(name, left, right):
            return (name, 0, [(low(step, left), heads(step, right)) for step in steps])

        first = [product("query", "a", "dq"), product("key", "a", "dk")]
        second = [product("out", "f", "o"), product("value", "a", "dv")]
        return (first, second)

    kinds = []
    for layer, steps in ((1, later), (0, early)):
        first = len(kinds)
        columns = hidden_width // SPLITS[layer]
        for start in range(0, hidden_width, columns):
            kinds.append((layer, first, columns, feed_group(steps, start)))
        kinds.append((layer, len(kinds), width, heads_group(steps)))
    made = {}
    shapes_out = {name: (2, width, head_width) for name in ("query", "key", "value", "out")}
    shapes_out |= {name: (2, width, hidden_width) for name in ("up", "down")}
    outputs = {}

    def make_products(group):
        layer, first, columns, products = kinds[group]
        sharing = [at for at, one in enumerate(kinds) if one[1] == first]
        operands, place = [], {}

        def number(held):
            key = (held.name, str(held.index))
            if key not in place:
                place[key] = len(operands)
                operands.append(held)
            return place[key]

        numbered = [
            [[(number(left), number(right)) for left, right in pairs] for _, _, pairs in part]
            for part in products
        ]
        done = order.call(
            functools.partial(weight_first, numbered, (slot_x, slot_y), len(sharing)),
            operands,
            [((width // 2, columns), BF16, "raw")] * (4 * len(sharing)),
            [pltpu.VMEM((width, columns * len(sharing)), BF16)] * 2,
            moves=4 * len(sharing),
            limit=30,
        )
        for at, one in enumerate(sharing):
            made[one] = done[4 * at : 4 * at + 4]

    def stages(group):
        layer, first, columns, products = kinds[group]
        sizes = [columns // len(part) for part in products for _ in part]
        room = lambda rows, cols: pltpu.VMEM((rows, cols), BF16)
        raw = lambda rows, cols: ((rows, cols), BF16, "raw")
        send = lambda value, axis, bits: lax.ppermute(value, axis, xor_pairs(axis, bits))
        if first == group:
            make_products(group)
        kept_a, sent_a, kept_b, sent_b = made[group]
        got_a, got_b = send(sent_a, "section", 1), send(sent_b, "section", 2)
        yield
        kept_a, sent_a, kept_b, sent_b = order.call(
            functools.partial(add_split, (slot_y, slot_x), 0),
            [kept_a, got_a, kept_b, got_b],
            [raw(width // 4, columns)] * 4,
            [room(width // 2, columns)] * 2,
            moves=4,
            limit=30,
        )
        got_a, got_b = send(sent_a, "section", 2), send(sent_b, "section", 1)
        yield
        shape = [width // 4, 2 * columns]
        axes = []
        for level, bits in enumerate(dp_bits):
            axis = 0 if shape[0] % 32 == 0 else 1
            axes.append(axis)
            before = tuple(shape)
            shape[axis] //= 2
            if level == 0:
                own, sent = order.call(
                    functools.partial(add_merge, slots_dp[level], axis),
                    [kept_a, got_a, kept_b, got_b],
                    [raw(*shape)] * 2,
                    [room(*before)],
                    moves=2,
                    limit=24,
                )
            else:
                own, sent = order.call(
                    functools.partial(add_split, (slots_dp[level],), axis),
                    [own, got],
                    [raw(*shape)] * 2,
                    [room(*before)],
                    moves=2,
                    limit=16,
                )
            got = send(sent, "dp", bits)
            yield
        (own,) = order.call(add_last, [own, got], [(tuple(shape), BF16)], limit=16)
        got = send(own, "dp", dp_bits[-1])
        yield
        for level in reversed(range(len(dp_bits))):
            axis = axes[level]
            shape[axis] *= 2
            if level > 0:
                (own,) = order.call(
                    functools.partial(join, (slots_dp[level],), axis),
                    [Raw(own), Raw(got)],
                    [raw(*shape)],
                    moves=2,
                    limit=16,
                )
                got = send(own, "dp", dp_bits[level - 1])
                yield
        own_a, own_b = order.call(
            functools.partial(join_part, slots_dp[0], axes[0]),
            [Raw(own), Raw(got)],
            [raw(width // 4, columns)] * 2,
            [room(*shape)],
            moves=4,
            limit=16,
        )
        got_a, got_b = send(own_a, "section", 2), send(own_b, "section", 1)
        yield
        own_a, own_b = order.call(
            functools.partial(join, (slot_y, slot_x), 0),
            [Raw(own_a), Raw(got_a), Raw(own_b), Raw(got_b)],
            [raw(width // 2, columns)] * 2,
            moves=4,
            limit=16,
        )
        got_a, got_b = send(own_a, "section", 1), send(own_b, "section", 2)
        yield
        names = [(name, start) for part in products for name, start, _ in part]
        before = [outputs.get(name) for name, _ in names]
        given = [one for one in before if one is not None]
        update = {}
        for at, one in enumerate(before):
            if one is not None:
                update[at] = 4 + len(update)
        done = order.call(
            functools.partial(
                finish, layer, len(products[0]), (slot_x, slot_y), [start for _, start in names]
            ),
            [own_a, got_a, own_b, got_b] + [Raw(one) for one in given],
            [(shapes_out[name], F32, "raw") for name, _ in names],
            [pltpu.VMEM((width // 2, size), F32) for size in sizes for _ in range(2)],
            moves=2 * len(names),
            limit=30,
            update=update,
        )
        for (name, _), one in zip(names, done):
            outputs[name] = one

    def small_stages():
        (packed,) = order.call(
            pack_small,
            [small_entry(step) for step in range(passes)] + [small_middle(step) for step in range(passes)],
            [((-(-(8 + passes) // 8) * 8, width), F32)], limit=8
        )
        hops = [("section", 1), ("section", 2)] + [("dp", bits) for bits in dp_bits]
        for axis, bits in hops[:-1]:
            got = lax.ppermute(packed, axis, xor_pairs(axis, bits))
            yield
            (packed,) = order.call(add_small, [packed, got], [(packed.shape, F32)], limit=8)
        axis, bits = hops[-1]
        got = lax.ppermute(packed, axis, xor_pairs(axis, bits))
        yield
        outputs["small"] = order.call(
            part_small,
            [packed, got],
            [((2, width), F32)] * 4 + [((passes, width), F32)],
            limit=8,
        )

    def input_stages(entered_t):
        got = exchange(entered_t)
        yield
        (grad_t,) = order.call(
            place_items,
            [Raw(one) for one in got],
            [((batches, slice_width, half_rows), F32, "raw")],
            [pltpu.VMEM((section_count, slice_width, half_rows), F32)],
            moves=section_count + 1,
            limit=8,
        )
        outputs["inputs"] = jnp.swapaxes(grad_t, 1, 2)

    running = {}

    def advance(name):
        if name not in running:
            running[name] = stages(name)
        next(running[name], None)

    passes_out = None
    for step in reversed(range(2, passes)):
        fed = feed_step(step)
        if step == passes - 1:
            passes_got = exchange(
                order.call(
                    split_items,
                    [Raw(results)],
                    [((half_rows, width), F32, "raw")] * section_count,
                    moves=section_count,
                    limit=4,
                )
            )
        state = attention_step(step, fed)

    def chain():
        nonlocal state, passes_out
        fed = feed_step(1)
        yield
        state = attention_step(1, fed)
        yield
        fed = feed_step(0)
        yield
        state = attention_step(0, fed)
        yield
        near_dr, part, other = state
        entered_t = order.call(
            entry_backward,
            [Near(part), Near(other), Near(near_dr), entered(0), gain_one],
            [small_entry(0)] + [((slice_width, half_rows), F32, "raw")] * section_count,
            [entry_v, pltpu.VMEM((section_count, slice_width, half_rows), F32)],
            moves=section_count,
        )
        (passes_out,) = order.call(
            place_items,
            [Raw(one) for one in passes_got],
            [((batches, half_rows, width), F32, "raw")],
            [pltpu.VMEM((section_count, half_rows, width), F32)],
            moves=section_count + 1,
            limit=8,
        )
        running["inputs"] = input_stages(entered_t)
        next(running["inputs"])
        running["small"] = small_stages()

    running["chain"] = chain()
    for name in schedule(len(dp_bits), len(kinds)):
        advance(name)
    for name in list(running):
        for _ in running[name]:
            pass
    return (
        passes_out[None],
        outputs["inputs"],
        *[outputs[name] for name in ("query", "key", "value", "out", "up", "down")],
        *outputs["small"],
    )


def solution(mesh):
    weight = P(None, None, "tensor")
    return jax.shard_map(
        shards,
        mesh=mesh,
        in_specs=(
            P("dp", "tensor", "section"),
            P("dp"),
            weight,
            weight,
            weight,
            weight,
            weight,
            weight,
            P(),
            P(),
            P(),
            P(),
            P(),
            P("section", "dp", "tensor", None),
        ),
        out_specs=(
            P("section", "dp", "tensor", None),
            P("dp", "tensor", "section"),
            weight,
            weight,
            weight,
            weight,
            weight,
            weight,
            P(),
            P(),
            P(),
            P(),
            P(),
        ),
        check_vma=False,
    )
```

```python
import functools

import jax
import jax.numpy as jnp
from jax import lax
from jax.experimental import pallas as pl
from jax.experimental.pallas import tpu as pltpu
from jax.sharding import PartitionSpec as P

HEADS = 12
EPSILON = 1e-05
MASKED = -1e30
F32 = jnp.float32
BF16 = jnp.bfloat16
ROOT = 0.7978845608028654
CUBIC = 0.044715
NN = (((1,), (0,)), ((), ()))
NT = (((1,), (1,)), ((), ()))
TN = (((0,), (0,)), ((), ()))


def dot(left, right, dims=NN):
    return lax.dot_general(left, right, dims, preferred_element_type=F32)


def norm_parts(rows):
    centred = rows - jnp.mean(rows, axis=-1, keepdims=True)
    spread = jnp.mean(centred * centred, axis=-1, keepdims=True)
    inverse = lax.rsqrt(spread + EPSILON)
    return centred * inverse, inverse


def norm_back(rows, gain, grad):
    normal, inverse = norm_parts(rows)
    scaled = gain * grad
    middle = jnp.mean(scaled, axis=-1, keepdims=True)
    along = jnp.mean(scaled * normal, axis=-1, keepdims=True)
    back = inverse * (scaled - middle - normal * along)
    gain_sum = jnp.sum(grad * normal, axis=0, keepdims=True)
    bias_sum = jnp.sum(grad, axis=0, keepdims=True)
    return back, gain_sum, bias_sum


def both(own, other):
    return own[...].astype(F32) + other[...].astype(F32)


class Incoming:
    def __init__(self, source, place, sem):
        self.copy = pltpu.make_async_copy(source, place, sem)
        self.copy.start()
        self.place = place
        self.waiting = True

    def ref(self):
        if self.waiting:
            self.copy.wait()
            self.waiting = False
        return self.place

    def __getitem__(self, index):
        return self.ref()[index]


class Outgoing:
    def __init__(self, place, target, sem):
        self.place = place
        self.copy = pltpu.make_async_copy(place, target, sem)

    def put(self, value):
        self.place[...] = value
        self.copy.start()

    def __getitem__(self, index):
        return self.place[index]

    def __setitem__(self, index, value):
        self.place[index] = value


class Chosen:
    def __init__(self, array, index):
        self.array, self.index = array, index


class Near:
    def __init__(self, array):
        self.array = array


class Held:
    def __init__(self, name, *index):
        self.name, self.index = name, index


class Raw:
    def __init__(self, array):
        self.array = array


class Far(Raw):
    pass


class Scalars:
    def __init__(self, array):
        self.array = array


class Mover:
    def __init__(self, sems):
        self.sems, self.used = sems, 0

    def start(self, source, target):
        copy = pltpu.make_async_copy(source, target, self.sems.at[self.used])
        self.used += 1
        copy.start()
        return copy


class Order:
    def __init__(self, shapes):
        self.shapes = shapes
        self.stores = {}

    def call(self, body, operands, outs, scratch=(), limit=20, moves=0, update=None, name=None):
        inner = body
        while isinstance(inner, functools.partial):
            inner = inner.func
        name = name or inner.__name__
        kind = lambda one: one[2] if isinstance(one, tuple) and len(one) > 2 else "staged"
        plain = lambda one: not isinstance(one, (Near, Raw, Scalars))
        names = ["order"] + [one.name for one in operands + outs if isinstance(one, Held)]
        names = list(dict.fromkeys(names))
        old = [name for name in names if name in self.stores]
        new = [name for name in names if name not in self.stores]
        given = [one for one in operands if not isinstance(one, Held)]
        made = [one for one in outs if not isinstance(one, Held)]
        arrays = [one.array if isinstance(one, (Chosen, Near, Raw, Scalars)) else one for one in given]

        def shape_of(one):
            if isinstance(one, Held):
                shape, dtype = self.shapes[one.name]
                for index in one.index:
                    if isinstance(index, int):
                        shape = shape[1:]
                    else:
                        sizes = [
                            cut.stop - cut.start if isinstance(cut, slice) else cut for cut in index
                        ]
                        shape = tuple(sizes) + tuple(shape[len(sizes) :])
                return shape, dtype
            if isinstance(one, Chosen):
                return one.array.shape[1:], one.array.dtype
            if isinstance(one, tuple):
                return one[0], one[1]
            return one.shape, one.dtype

        places = [pltpu.VMEM(*shape_of(one)) for one in operands if plain(one)]
        places += [pltpu.VMEM(*shape_of(one)) for one in outs if kind(one) == "staged"]
        first_out = len(old) + len(given)
        total = first_out + len(names) + len(made)
        count = len(places)

        def part(stores, one):
            ref = stores[one.name]
            for index in one.index:
                ref = ref.at[index]
            return ref

        def kernel(*refs):
            in_refs = list(refs[len(old) : first_out])
            stores = dict(zip(old + new, refs[first_out : first_out + len(names)]))
            out_refs = list(refs[first_out + len(names) : total])
            rooms = refs[total : total + count]
            sems, more = refs[total + count], refs[total + count + 1]
            rest = refs[total + count + 2 :]
            ins, results = [], []
            at = 0
            for one in operands:
                ref = part(stores, one) if isinstance(one, Held) else in_refs.pop(0)
                if plain(one):
                    source = ref.at[one.index] if isinstance(one, Chosen) else ref
                    ins.append(Incoming(source, rooms[at], sems.at[at]))
                    at += 1
                else:
                    ins.append(ref)
            for one in outs:
                ref = part(stores, one) if isinstance(one, Held) else out_refs.pop(0)
                if kind(one) == "staged":
                    results.append(Outgoing(rooms[at], ref, sems.at[at]))
                    at += 1
                else:
                    results.append(ref)
            extra = (Mover(more),) if moves else ()
            body(ins, results, *extra, *rest)
            for one in ins:
                if isinstance(one, Incoming):
                    one.ref()
            for one in results:
                if isinstance(one, Outgoing):
                    one.copy.wait()

        anywhere = pl.BlockSpec(memory_space=pl.ANY)
        inside = pl.BlockSpec(memory_space=pltpu.VMEM)
        scalar = pl.BlockSpec(memory_space=pltpu.SMEM)
        spec = lambda one: inside if isinstance(one, Near) else scalar if isinstance(one, Scalars) else anywhere
        aliases = {at: at for at in range(len(old))}
        for out_at, in_at in (update or {}).items():
            shift_in = sum(isinstance(one, Held) for one in operands[:in_at])
            shift_out = sum(isinstance(one, Held) for one in outs[:out_at])
            aliases[len(old) + in_at - shift_in] = len(names) + out_at - shift_out
        shapes = [pltpu.HBM(*self.shapes[name]) for name in old + new]
        for one in made:
            form = pltpu.VMEM if kind(one) == "near" else jax.ShapeDtypeStruct
            shapes.append(form(one[0], one[1]))
        arrays = [
            pltpu.with_memory_space_constraint(array, pltpu.VMEM)
            if isinstance(one, Near)
            else pltpu.with_memory_space_constraint(array, pltpu.HBM)
            if isinstance(one, (Chosen, Far)) or array.size * array.dtype.itemsize < 20000
            and not isinstance(one, (Raw, Scalars))
            else array
            for one, array in zip(given, arrays)
        ]
        done = pl.pallas_call(
            kernel,
            name=name,
            out_shape=tuple(shapes),
            in_specs=[anywhere] * len(old) + [spec(one) for one in given],
            out_specs=(anywhere,) * len(names)
            + tuple(inside if kind(one) == "near" else anywhere for one in made),
            scratch_shapes=places
            + [pltpu.SemaphoreType.DMA((max(count, 1),)), pltpu.SemaphoreType.DMA((max(moves, 1),))]
            + list(scratch),
            input_output_aliases=aliases,
            compiler_params=pltpu.CompilerParams(vmem_limit_bytes=int(limit * 1024 * 1024)),
            cost_estimate=pl.CostEstimate(flops=1000, bytes_accessed=1000, transcendentals=0),
        )(
            *[pltpu.with_memory_space_constraint(self.stores[name], pltpu.HBM) for name in old],
            *arrays,
        )
        self.stores.update(zip(old + new, done[: len(names)]))
        return done[len(names) :]


class Place:
    def __getitem__(self, slot):
        name, bits = slot
        return (lax.axis_index(name) // bits) % 2 if bits else lax.axis_index(name)


HERE = Place()


def causal_mask(length):
    key_place = lax.broadcasted_iota(jnp.int32, (length, length), 0)
    query_place = lax.broadcasted_iota(jnp.int32, (length, length), 1)
    return key_place <= query_place


def lane_half(half, pair):
    lane = lax.broadcasted_iota(jnp.int32, pair.shape, 1)
    keep = (lane < 64) if half == 0 else (lane >= 64)
    return jnp.where(keep, pair, jnp.zeros_like(pair))


def present_in(counts, step):
    item = lax.axis_index("section")
    last = counts.shape[0] - 1
    own_count = jnp.where(item <= last, counts[jnp.minimum(item, last)], 0)
    return jnp.where(own_count > step, 1.0, 0.0).astype(F32)


def attention_forward(step, layer, ins, outs, mover, turned, *rest):
    count = 2 if step == 0 else 3
    first, (embed, gain, bias, wq, wk, wv, wo) = ins[:count], ins[count : count + 7]
    past_k, past_vt = ins[count + 7 : count + 7 + step], ins[count + 7 + step : count + 7 + 2 * step]
    sent = None
    if step == 0:
        own_t, other_t = first
        (entry_v,) = rest
        half = own_t.shape[1]
        place = pl.multiple_of(lax.axis_index("tensor") * half, half)
        entry_v[pl.ds(place, half), :] = own_t[...].T
        entry_v[pl.ds(pl.multiple_of(half - place, half), half), :] = other_t[...].T
        entered = entry_v[...] + embed[0:1, :]
    else:
        near_r, own, other = first
        counts = ins[count + 7 + 2 * step]
        (entry_v,) = rest
        result = near_r[...] + both(own, other)
        entry_v[...] = result * present_in(counts, step - 1)
        half = entry_v.shape[0] // 2
        place = pl.multiple_of(lax.axis_index("tensor") * half, half)
        sent = mover.start(entry_v.at[pl.ds(place, half)], outs[0].at[step - 1])
        outs = outs[1:]
        entered = result + embed[step : step + 1, :]
    near_out = outs[0]
    near_out[...] = entered
    outs = outs[1:]
    u_out, a_out, q_out, k_out, kt_out, v_out, vt_out, lse_out, o_out, part_out = outs
    u_out.put(entered)
    normal, _ = norm_parts(entered)
    a = (normal * gain[layer : layer + 1, :] + bias[layer : layer + 1, :]).astype(BF16)
    a_out.put(a)
    q_out.put((dot(a, wq[layer]).astype(BF16).astype(F32) * 0.125).astype(BF16))
    k_full = dot(a, wk[layer])
    k_out.put(k_full.astype(BF16))
    v_full = dot(a, wv[layer])
    vt_out.put(v_full.T.astype(BF16))
    v_out.put(v_full.astype(BF16))
    kt_out.put(k_full.T.astype(BF16))
    length = entered.shape[0]
    seen = causal_mask(length)
    all_k = past_k + [k_out]
    all_vt = past_vt + [vt_out]
    pairs = wq.shape[2] // 128

    def one_pair(pair, carry):
        lanes = pl.ds(pl.multiple_of(128 * pair, 128), 128)
        for half in range(2):
            query = lane_half(half, q_out[:, lanes])
            scores = [jnp.where(seen, dot(key[:, lanes], query, NT), MASKED) for key in all_k]
            highest = functools.reduce(
                jnp.maximum, [jnp.max(one, axis=0, keepdims=True) for one in scores]
            )
            powers = [jnp.exp(one - highest) for one in scores]
            total = functools.reduce(
                jnp.add, [jnp.sum(one, axis=0, keepdims=True) for one in powers]
            )
            inverse = 1.0 / total
            lse_out[pl.ds(2 * pair + half, 1), :] = highest + jnp.log(total)
            rows = pl.ds(pl.multiple_of(128 * pair + 64 * half, 64), 64)
            mixed = None
            for power, value in zip(powers, all_vt):
                term = dot(value[rows, :], (power * inverse).astype(BF16))
                mixed = term if mixed is None else mixed + term
            turned[rows, :] = mixed
        return carry

    for one in past_k + past_vt:
        one.ref()
    lax.fori_loop(0, pairs, one_pair, 0)
    lse_out.copy.start()
    o = turned[...].T.astype(BF16)
    o_out.put(o)
    part_out[...] = dot(o, wo[layer], NT).astype(BF16)
    if sent is not None:
        sent.wait()


def gelu_parts(hidden):
    square = hidden * hidden
    bent = jnp.tanh(ROOT * hidden * (1.0 + CUBIC * square))
    return square, bent


def feed_forward(layer, ins, outs):
    own, other, u, gain, bias, wu, wd = ins[:7]
    near_out, r_out, b_out, g_out, m_out, part_out = outs[:6]
    middle = u[...] + both(own, other)
    near_out[...] = middle
    r_out.put(middle)
    normal, _ = norm_parts(middle)
    b = (normal * gain[layer : layer + 1, :] + bias[layer : layer + 1, :]).astype(BF16)
    b_out.put(b)
    hidden = dot(b, wu[layer])
    g_out.put(hidden)
    _, bent = gelu_parts(hidden)
    m = (0.5 * hidden * (1.0 + bent)).astype(BF16)
    m_out.put(m)
    part_out[...] = dot(m, wd[layer], NT).astype(BF16)


def small_put(out, rows):
    rows = rows + [jnp.zeros_like(rows[0])] * (8 - len(rows))
    out.put(jnp.concatenate(rows, axis=0))


def feed_backward(step, layer, last, ins, outs, mover, cot_v, *more):
    counts, cot_own, cot_other, wd, g, wu = ins[:6]
    near_out, e_out, dg_out, part_out = outs[:4]
    half = cot_v.shape[0] // 2
    place = pl.multiple_of(lax.axis_index("tensor") * half, half)
    copies = [
        mover.start(cot_own.at[step], cot_v.at[pl.ds(place, half)]),
        mover.start(cot_other.at[step], cot_v.at[pl.ds(pl.multiple_of(half - place, half), half)]),
    ]
    present = present_in(counts, step)
    if last:
        near_r, own, other = ins[6:]
        (end_v,) = more
        end_v[...] = (near_r[...] + both(own, other)) * present
        sent = mover.start(end_v.at[pl.ds(place, half)], outs[4].at[step])
    else:
        own, other, dr, u, gain = ins[6:]
        back, gain_sum, bias_sum = norm_back(u[...], gain[1:2, :], both(own, other))
        entered = dr[...] + back
        small_put(outs[4], [gain_sum, bias_sum, jnp.sum(entered, axis=0, keepdims=True)])
    for copy in copies:
        copy.wait()
    grad = cot_v[...].astype(F32) * present
    if not last:
        grad = grad + entered
    near_out[...] = grad
    e = grad.astype(BF16)
    e_out.put(e)
    raw = dot(e, wd[layer])
    hidden = g[...]
    square, bent = gelu_parts(hidden)
    slope = 0.5 * (1.0 + bent) + 0.5 * hidden * (1.0 - bent * bent) * ROOT * (
        1.0 + 3.0 * CUBIC * square
    )
    dg = (raw * slope).astype(BF16)
    dg_out.put(dg)
    part_out[...] = dot(dg, wu[layer], NT).astype(BF16)
    if last:
        sent.wait()


def attention_backward(step, layer, last, ins, outs, do_v, dqt_v):
    own, other, dh, r, gain, wo, q, lse = ins[:8]
    count = step + 1
    keys, values, keys_t = ins[8 : 8 + count], ins[8 + count : 8 + 2 * count], ins[8 + 2 * count : 8 + 3 * count]
    rest = ins[8 + 3 * count :]
    if not last:
        dk_in, dv_in = rest[:2]
    wq, wk, wv = rest[-3:]
    near_out, f_out, dq_out, dk_out, dv_out, part_out, small_out = outs[:7]
    if step > 0:
        dk_all, dv_all = outs[7:]
    back, gain_sum, bias_sum = norm_back(r[...], gain[layer : layer + 1, :], both(own, other))
    small_put(small_out, [gain_sum, bias_sum])
    grad = dh[...] + back
    near_out[...] = grad
    f = grad.astype(BF16)
    f_out.put(f)
    do_v[...] = dot(f, wo[layer]).astype(BF16)
    length = f.shape[0]
    seen = causal_mask(length)
    pairs = q.place.shape[1] // 128

    def one_pair(pair, carry):
        lanes = pl.ds(pl.multiple_of(128 * pair, 128), 128)
        key_sums = [None] * count
        value_sums = [None] * count
        for half in range(2):
            rows = pl.ds(pl.multiple_of(128 * pair + 64 * half, 64), 64)
            query = lane_half(half, q[:, lanes])
            grad_mix = lane_half(half, do_v[:, lanes])
            total = lse[pl.ds(2 * pair + half, 1), :]
            exact = [
                jnp.exp(jnp.where(seen, dot(key[:, lanes], query, NT), MASKED) - total)
                for key in keys
            ]
            grad_weights = [dot(value[:, lanes], grad_mix, NT) for value in values]
            delta = functools.reduce(
                jnp.add,
                [jnp.sum(p * dp, axis=0, keepdims=True) for p, dp in zip(exact, grad_weights)],
            )
            query_grad = None
            for slot in range(count):
                grad_scores = (exact[slot] * (grad_weights[slot] - delta)).astype(BF16)
                term = dot(keys_t[slot][rows, :], grad_scores)
                query_grad = term if query_grad is None else query_grad + term
                key_term = dot(grad_scores, query)
                value_term = dot(exact[slot].astype(BF16), grad_mix)
                if half == 0:
                    key_sums[slot] = key_term
                    value_sums[slot] = value_term
                else:
                    key_sums[slot] = key_sums[slot] + key_term
                    value_sums[slot] = value_sums[slot] + value_term
            dqt_v[rows, :] = query_grad
        for slot in range(count):
            key_sum, value_sum = key_sums[slot], value_sums[slot]
            if not last:
                key_sum = key_sum + dk_in[slot, :, lanes]
                value_sum = value_sum + dv_in[slot, :, lanes]
            if slot == step:
                dk_out[:, lanes] = key_sum.astype(BF16)
                dv_out[:, lanes] = value_sum.astype(BF16)
            else:
                dk_all[slot, :, lanes] = key_sum
                dv_all[slot, :, lanes] = value_sum
        return carry

    for one in [q, lse] + keys + values + keys_t + ([] if last else [dk_in, dv_in]):
        one.ref()
    lax.fori_loop(0, pairs, one_pair, 0)
    for one in (dk_out, dv_out) + ((dk_all, dv_all) if step > 0 else ()):
        one.copy.start()
    dq = (dqt_v[...].T * 0.125).astype(BF16)
    dq_out.put(dq)
    part = dot(dq, wq[layer], NT) + dot(dk_out[...], wk[layer], NT) + dot(dv_out[...], wv[layer], NT)
    part_out[...] = part.astype(BF16)


def entry_backward(ins, outs, mover, entry_v, pieces_v):
    own, other, dr, u, gain = ins
    back, gain_sum, bias_sum = norm_back(u[...], gain[0:1, :], both(own, other))
    entered = dr[...] + back
    entry_v[...] = entered
    half = entry_v.shape[0] // 2
    place = pl.multiple_of(lax.axis_index("tensor") * half, half)
    turned = entry_v[pl.ds(place, half), :].T
    pieces_v[...] = turned.reshape(pieces_v.shape)
    section = lax.axis_index("section")
    copies = [mover.start(pieces_v.at[section ^ bits], out) for bits, out in enumerate(outs[1:])]
    small_put(outs[0], [gain_sum, bias_sum, jnp.sum(entered, axis=0, keepdims=True)])
    for copy in copies:
        copy.wait()


def place_items(ins, outs, mover, room):
    section = lax.axis_index("section")
    copies = [mover.start(piece, room.at[section ^ bits]) for bits, piece in enumerate(ins)]
    for copy in copies:
        copy.wait()
    mover.start(room.at[pl.ds(0, outs[0].shape[0])], outs[0]).wait()


def place_pieces(ins, outs, mover):
    section = lax.axis_index("section")
    count = len(ins) // len(outs)
    copies = []
    for at, piece in enumerate(ins):
        rows = piece.shape[0]
        place = pl.multiple_of((section ^ (at % count)) * rows, rows)
        copies.append(mover.start(piece, outs[at // count].at[pl.ds(place, rows)]))
    for copy in copies:
        copy.wait()


def split_items(ins, outs, mover):
    last = ins[0].shape[0] - 1
    section = lax.axis_index("section")
    copies = [
        mover.start(ins[0].at[jnp.minimum(section ^ bits, last)], out)
        for bits, out in enumerate(outs)
    ]
    for copy in copies:
        copy.wait()


def split_cotangent(ins, outs, mover, rooms, sent):
    last = ins[0].shape[1] - 1
    section = lax.axis_index("section")
    copies = [
        mover.start(ins[0].at[0].at[jnp.minimum(section ^ bits, last)], rooms.at[bits])
        for bits in range(rooms.shape[0])
    ]
    for bits, out in enumerate(outs):
        copies[bits].wait()
        sent[bits] = rooms[bits].astype(BF16)
        copies.append(mover.start(sent.at[bits], out))
    for copy in copies[len(outs) :]:
        copy.wait()


def load(ins, outs, mover):
    copies = [mover.start(source, target) for source, target in zip(ins, outs)]
    for copy in copies:
        copy.wait()


def pack_small(ins, outs):
    passes = (len(ins)) // 2
    entry, middle = ins[:passes], ins[passes:]
    rows = []
    for kind in (entry, middle):
        for row in range(2):
            rows.append(kind[0][row : row + 1, :])
            later = kind[1][row : row + 1, :]
            for step in range(2, passes):
                later = later + kind[step][row : row + 1, :]
            rows.append(later)
    rows += [entry[step][2:3, :] for step in range(passes)]
    rows += [jnp.zeros_like(rows[0])] * (-len(rows) % 8)
    outs[0].put(jnp.concatenate(rows, axis=0))


def add_small(ins, outs):
    outs[0].put(ins[0][...] + ins[1][...])


def part_small(ins, outs):
    total = ins[0][...] + ins[1][...]
    at = 0
    for out in outs:
        count = out.place.shape[0]
        out.put(total[at : at + count])
        at += count


def halves(slot, room, axis):
    size = room.shape[axis] // 2
    kept = pl.multiple_of(HERE[slot] * size, size)
    sent = pl.multiple_of(size - kept, size)
    if axis == 0:
        return room.at[pl.ds(kept, size)], room.at[pl.ds(sent, size)]
    return room.at[:, pl.ds(kept, size)], room.at[:, pl.ds(sent, size)]


def weight_first(products, splits, sharing, ins, outs, mover, *rooms):
    factors = ins
    copies = []
    for at, (room, slot) in enumerate(zip(rooms, splits)):
        column = 0
        for pairs in products[at]:
            total = None
            for left, right in pairs:
                term = dot(factors[left][...], factors[right][...], TN)
                total = term if total is None else total + term
            room[:, column : column + total.shape[1]] = total.astype(BF16)
            column += total.shape[1]
        kept, sent = halves(slot, room, 0)
        columns = room.shape[1] // sharing
        for one in range(sharing):
            across = (slice(None), pl.ds(one * columns, columns))
            copies.append(mover.start(sent.at[across], outs[4 * one + 2 * at + 1]))
            copies.append(mover.start(kept.at[across], outs[4 * one + 2 * at]))
    for copy in copies:
        copy.wait()


def add_split(slots, axis, ins, outs, mover, *rooms):
    copies = []
    for at, (room, slot) in enumerate(zip(rooms, slots)):
        room[...] = (ins[2 * at][...].astype(F32) + ins[2 * at + 1][...].astype(F32)).astype(BF16)
        kept, sent = halves(slot, room, axis)
        copies.append(mover.start(sent, outs[2 * at + 1]))
        copies.append(mover.start(kept, outs[2 * at]))
    for copy in copies:
        copy.wait()


def add_merge(slot, axis, ins, outs, mover, room):
    columns = room.shape[1] // 2
    for at in range(2):
        total = ins[2 * at][...].astype(F32) + ins[2 * at + 1][...].astype(F32)
        room[:, at * columns : (at + 1) * columns] = total.astype(BF16)
    kept, sent = halves(slot, room, axis)
    copies = [mover.start(sent, outs[1]), mover.start(kept, outs[0])]
    for copy in copies:
        copy.wait()


def add_last(ins, outs):
    outs[0].put((ins[0][...].astype(F32) + ins[1][...].astype(F32)).astype(BF16))


def join(slots, axis, ins, outs, mover):
    copies = []
    for at, slot in enumerate(slots):
        own, other = halves(slot, outs[at], axis)
        copies.append(mover.start(ins[2 * at], own))
        copies.append(mover.start(ins[2 * at + 1], other))
    for copy in copies:
        copy.wait()


def join_part(slot, axis, ins, outs, mover, room):
    own, other = halves(slot, room, axis)
    copies = [mover.start(ins[0], own), mover.start(ins[1], other)]
    for copy in copies:
        copy.wait()
    columns = room.shape[1] // 2
    copies = [mover.start(room.at[:, pl.ds(at * columns, columns)], outs[at]) for at in range(2)]
    for copy in copies:
        copy.wait()


def finish(layer, parts, slots, starts, ins, outs, mover, *rooms):
    halves_in = ins[:4]
    copies = []
    out_at = 0
    for at, slot in enumerate(slots):
        rows = halves_in[2 * at].place.shape[0]
        for which in range(2):
            place = HERE[slot] * rows
            place = pl.multiple_of(place if which == 0 else rows - place, rows)
            column = 0
            for part in range(parts):
                room = rooms[2 * (out_at + part) + which]
                columns = room.shape[1]
                room[...] = halves_in[2 * at + which][:, column : column + columns].astype(F32)
                target = outs[out_at + part].at[layer]
                across = pl.ds(starts[out_at + part], columns)
                copies.append(mover.start(room, target.at[pl.ds(place, rows), across]))
                column += columns
        out_at += parts
    for copy in copies:
        copy.wait()


def swap(value):
    return lax.ppermute(value, "tensor", [(0, 1), (1, 0)])


def xor_pairs(axis, bits):
    return [(place, place ^ bits) for place in range(lax.axis_size(axis))]


def pick(stacked, index):
    return lax.dynamic_index_in_dim(stacked, index, 0, keepdims=False)


SPLITS = (2, 2)
CHAIN, SMALL, INPUTS = 6, 7, 8
STEPS = (
    6, 0, 6, 1, 2, 6, 0, 6, 1, 3, 2, 0, 1, 6, 0, 2, 4, 1, 0, 3,
    2, 7, 1, 0, 4, 8, 1, 3, 1, 2, 4, 7, 5, 7, 0, 7, 1, 4, 2, 3,
    5, 7, 4, 3, 4, 2, 5, 3, 0, 4, 1, 2, 5, 0, 3, 5, 2, 4, 3, 5,
    5, 4, 5, 3, 5,
)


def schedule(levels, groups):
    names = {CHAIN: "chain", SMALL: "small", INPUTS: "inputs"}
    if levels == 2 and groups == sum(SPLITS) + 2:
        return [names.get(step, step) for step in STEPS]
    order = ["chain"]
    order += list(range(SPLITS[1])) + ["chain", SPLITS[1]]
    order += ["chain"] * 3
    for step in range(2 * levels + 5):
        order += list(range(groups))
    return order


def shards(
    inputs,
    counts,
    w_query,
    w_key,
    w_value,
    w_out,
    w_up,
    w_down,
    gain_one,
    bias_one,
    gain_two,
    bias_two,
    pass_embed,
    cotangent,
):
    section_count = lax.axis_size("section")
    section = lax.axis_index("section")
    tensor = lax.axis_index("tensor")
    batches, half_rows, slice_width = inputs.shape
    length = 2 * half_rows
    width = cotangent.shape[3]
    head_width = w_query.shape[2]
    hidden_width = w_up.shape[2]
    passes = pass_embed.shape[0]
    dp_count = lax.axis_size("dp")
    dp_place = lax.axis_index("dp")
    dp_bits = [1 << level for level in range(dp_count.bit_length() - 1)]
    order = Order(
        {
            "order": ((2, passes, length, head_width), F32),
            "low": ((passes, 4, length, width), BF16),
            "hidden": ((passes, 2, length, hidden_width), BF16),
            "heads": ((passes, 7, length, head_width), BF16),
            "turned": ((passes, 4, head_width, length), BF16),
            "wide": ((passes, 2 * length + 24, width), F32),
            "before": ((passes, length, hidden_width), F32),
        }
    )

    def exchange(pieces):
        return [pieces[0]] + [
            lax.ppermute(pieces[bits], "section", xor_pairs("section", bits))
            for bits in range(1, section_count)
        ]

    slot_x, slot_y = ("section", 1), ("section", 2)
    slots_dp = [("dp", bits) for bits in dp_bits]

    inputs_t = jnp.swapaxes(inputs, 1, 2)
    got = exchange(
        order.call(
            split_items,
            [Far(inputs_t)],
            [((slice_width, half_rows), F32, "raw")] * section_count,
            moves=section_count,
            limit=4,
        )
    )
    cot_sent = order.call(
        split_cotangent,
        [Far(cotangent)],
        [((half_rows, width), BF16, "raw")] * section_count,
        [pltpu.VMEM((section_count, half_rows, width), kind) for kind in (F32, BF16)],
        moves=2 * section_count,
        limit=8,
    )
    weights = (w_query, w_key, w_value, w_out, w_up, w_down)
    w_query, w_key, w_value, w_out, w_up, w_down = order.call(
        load,
        [Far(one) for one in weights],
        [(one.shape, one.dtype, "near") for one in weights],
        moves=len(weights),
        limit=8,
    )
    cot_got = exchange(cot_sent)
    entry_t, cot_flat = order.call(
        place_pieces,
        [Raw(one) for one in got + cot_got],
        [
            ((width, half_rows), F32, "near"),
            ((section_count * half_rows, width), BF16, "raw"),
        ],
        moves=2 * section_count,
        limit=8,
    )
    entry_other = swap(entry_t)

    wide_near = ((length, width), F32, "near")
    part_near = ((length, width), BF16, "near")
    stacked = ((passes, half_rows, width), F32, "raw")
    turned = pltpu.VMEM((head_width, length), F32)
    entry_v = pltpu.VMEM((length, width), F32)
    cot_v = pltpu.VMEM((length, width), BF16)
    whole = slice(None)

    def low(step, name):
        return Held("low", step, "abef".index(name))

    def hidden(step, name):
        return Held("hidden", step, ("m", "dg").index(name))

    def heads(step, name):
        return Held("heads", step, ("q", "k", "v", "o", "dq", "dk", "dv").index(name))

    def turn(step, name):
        return Held("turned", step, ("kt", "vt").index(name))

    def rows(step, start, count, columns=None):
        cut = (slice(start, start + count), slice(0, columns or width))
        return Held("wide", step, cut)

    def entered(step):
        return rows(step, 0, length)

    def middle(step):
        return rows(step, length, length)

    def logsum(step):
        return rows(step, 2 * length, 8, length)

    def small_entry(step):
        return rows(step, 2 * length + 8, 8)

    def small_middle(step):
        return rows(step, 2 * length + 16, 8)

    results = None
    resid = None
    cot_own = cot_other = None
    cot_own = cot_flat.reshape(section_count, half_rows, width)
    cot_other = swap(cot_own)
    for step in range(passes):
        layer = min(step, 1)
        first = [Near(entry_t), Near(entry_other)] if step == 0 else [Near(one) for one in resid]
        weights = [Near(one) for one in (w_query, w_key, w_value, w_out)]
        operands = first + [pass_embed, gain_one, bias_one] + weights
        operands += [heads(past, "k") for past in range(step)]
        operands += [turn(past, "vt") for past in range(step)]
        update = None
        if step > 0:
            operands.append(Scalars(counts))
        if step > 1:
            operands.append(Raw(results))
            update = {0: len(operands) - 1}
        done = order.call(
            functools.partial(attention_forward, step, layer),
            operands,
            ([] if step == 0 else [stacked])
            + [wide_near, entered(step), low(step, "a"), heads(step, "q"), heads(step, "k")]
            + [turn(step, "kt"), heads(step, "v"), turn(step, "vt"), logsum(step)]
            + [heads(step, "o"), part_near],
            [turned, entry_v],
            moves=1,
            update=update,
        )
        if step > 0:
            results = done[0]
            done = done[1:]
        near_u, part = done
        near_r, part_two = order.call(
            functools.partial(feed_forward, layer),
            [Near(part), Near(swap(part)), Near(near_u), gain_two, bias_two]
            + [Near(w_up), Near(w_down)],
            [wide_near, middle(step), low(step, "b"), Held("before", step), hidden(step, "m"), part_near],
        )
        resid = (near_r, part_two, swap(part_two))

    factors = [
        {name: low(step, name) for name in "abef"}
        | {name: hidden(step, name) for name in ("m", "dg")}
        | {name: heads(step, name) for name in ("o", "dq", "dk", "dv")}
        for step in range(passes)
    ]
    state = None

    def feed_step(step):
        nonlocal results
        layer = min(step, 1)
        last = step == passes - 1
        operands = [Scalars(counts), Raw(cot_own), Raw(cot_other)]
        operands += [Near(w_down), Held("before", step), Near(w_up)]
        outs = [wide_near, low(step, "e"), hidden(step, "dg"), part_near]
        update = None
        if last:
            operands += [Near(one) for one in resid]
            outs += [stacked]
            operands.append(Raw(results))
            update = {4: len(operands) - 1}
        else:
            dr, part, other = state
            operands += [Near(part), Near(other), Near(dr), entered(step + 1), gain_one]
            outs += [small_entry(step + 1)]

        def body(ins, outs, mover, *rooms):
            feed_backward(step, layer, last, ins[:9] if last else ins, outs, mover, *rooms)

        done = order.call(
            body,
            operands,
            outs,
            [cot_v] + ([entry_v] if last else []),
            moves=3,
            update=update,
            name=feed_backward.__name__,
        )
        near_dh, part = done[:2]
        if last:
            results = done[2]
        return near_dh, part, swap(part)

    def attention_step(step, fed):
        layer = min(step, 1)
        last = step == passes - 1
        near_dh, part, other = fed
        operands = [Near(part), Near(other), Near(near_dh), middle(step), gain_two]
        operands += [Near(w_out), heads(step, "q"), logsum(step)]
        operands += [heads(past, "k") for past in range(step + 1)]
        operands += [heads(past, "v") for past in range(step + 1)]
        operands += [turn(past, "kt") for past in range(step + 1)]
        cut = (slice(0, step + 1),)
        if not last:
            operands += [Held("order", at, cut) for at in range(2)]
        operands += [Near(one) for one in (w_query, w_key, w_value)]
        outs = [wide_near, low(step, "f"), heads(step, "dq"), heads(step, "dk"), heads(step, "dv")]
        outs += [part_near, small_middle(step)]
        if step > 0:
            outs += [Held("order", at, (slice(0, step),)) for at in range(2)]
        near_dr, part = order.call(
            functools.partial(attention_backward, step, layer, last),
            operands,
            outs,
            [pltpu.VMEM((length, head_width), BF16), turned],
        )
        return near_dr, part, swap(part)

    later, early = list(range(1, passes)), [0]
    def feed_group(steps, start):
        first = [("up", start, [(low(step, "b"), hidden(step, "dg")) for step in steps])]
        second = [("down", start, [(low(step, "e"), hidden(step, "m")) for step in steps])]
        return (first, second)

    def heads_group(steps):
        def product(name, left, right):
            return (name, 0, [(low(step, left), heads(step, right)) for step in steps])

        first = [product("query", "a", "dq"), product("key", "a", "dk")]
        second = [product("out", "f", "o"), product("value", "a", "dv")]
        return (first, second)

    kinds = []
    for layer, steps in ((1, later), (0, early)):
        first = len(kinds)
        columns = hidden_width // SPLITS[layer]
        for start in range(0, hidden_width, columns):
            kinds.append((layer, first, columns, feed_group(steps, start)))
        kinds.append((layer, len(kinds), width, heads_group(steps)))
    made = {}
    shapes_out = {name: (2, width, head_width) for name in ("query", "key", "value", "out")}
    shapes_out |= {name: (2, width, hidden_width) for name in ("up", "down")}
    outputs = {}

    def make_products(group):
        layer, first, columns, products = kinds[group]
        sharing = [at for at, one in enumerate(kinds) if one[1] == first]
        operands, place = [], {}

        def number(held):
            key = (held.name, str(held.index))
            if key not in place:
                place[key] = len(operands)
                operands.append(held)
            return place[key]

        numbered = [
            [[(number(left), number(right)) for left, right in pairs] for _, _, pairs in part]
            for part in products
        ]
        done = order.call(
            functools.partial(weight_first, numbered, (slot_x, slot_y), len(sharing)),
            operands,
            [((width // 2, columns), BF16, "raw")] * (4 * len(sharing)),
            [pltpu.VMEM((width, columns * len(sharing)), BF16)] * 2,
            moves=4 * len(sharing),
            limit=30,
        )
        for at, one in enumerate(sharing):
            made[one] = done[4 * at : 4 * at + 4]

    def stages(group):
        layer, first, columns, products = kinds[group]
        sizes = [columns // len(part) for part in products for _ in part]
        room = lambda rows, cols: pltpu.VMEM((rows, cols), BF16)
        raw = lambda rows, cols: ((rows, cols), BF16, "raw")
        send = lambda value, axis, bits: lax.ppermute(value, axis, xor_pairs(axis, bits))
        if first == group:
            make_products(group)
        kept_a, sent_a, kept_b, sent_b = made[group]
        got_a, got_b = send(sent_a, "section", 1), send(sent_b, "section", 2)
        yield
        kept_a, sent_a, kept_b, sent_b = order.call(
            functools.partial(add_split, (slot_y, slot_x), 0),
            [kept_a, got_a, kept_b, got_b],
            [raw(width // 4, columns)] * 4,
            [room(width // 2, columns)] * 2,
            moves=4,
            limit=30,
        )
        got_a, got_b = send(sent_a, "section", 2), send(sent_b, "section", 1)
        yield
        shape = [width // 4, 2 * columns]
        axes = []
        for level, bits in enumerate(dp_bits):
            axis = 0 if shape[0] % 32 == 0 else 1
            axes.append(axis)
            before = tuple(shape)
            shape[axis] //= 2
            if level == 0:
                own, sent = order.call(
                    functools.partial(add_merge, slots_dp[level], axis),
                    [kept_a, got_a, kept_b, got_b],
                    [raw(*shape)] * 2,
                    [room(*before)],
                    moves=2,
                    limit=24,
                )
            else:
                own, sent = order.call(
                    functools.partial(add_split, (slots_dp[level],), axis),
                    [own, got],
                    [raw(*shape)] * 2,
                    [room(*before)],
                    moves=2,
                    limit=16,
                )
            got = send(sent, "dp", bits)
            yield
        (own,) = order.call(add_last, [own, got], [(tuple(shape), BF16)], limit=16)
        got = send(own, "dp", dp_bits[-1])
        yield
        for level in reversed(range(len(dp_bits))):
            axis = axes[level]
            shape[axis] *= 2
            if level > 0:
                (own,) = order.call(
                    functools.partial(join, (slots_dp[level],), axis),
                    [Raw(own), Raw(got)],
                    [raw(*shape)],
                    moves=2,
                    limit=16,
                )
                got = send(own, "dp", dp_bits[level - 1])
                yield
        own_a, own_b = order.call(
            functools.partial(join_part, slots_dp[0], axes[0]),
            [Raw(own), Raw(got)],
            [raw(width // 4, columns)] * 2,
            [room(*shape)],
            moves=4,
            limit=16,
        )
        got_a, got_b = send(own_a, "section", 2), send(own_b, "section", 1)
        yield
        own_a, own_b = order.call(
            functools.partial(join, (slot_y, slot_x), 0),
            [Raw(own_a), Raw(got_a), Raw(own_b), Raw(got_b)],
            [raw(width // 2, columns)] * 2,
            moves=4,
            limit=16,
        )
        got_a, got_b = send(own_a, "section", 1), send(own_b, "section", 2)
        yield
        names = [(name, start) for part in products for name, start, _ in part]
        before = [outputs.get(name) for name, _ in names]
        given = [one for one in before if one is not None]
        update = {}
        for at, one in enumerate(before):
            if one is not None:
                update[at] = 4 + len(update)
        done = order.call(
            functools.partial(
                finish, layer, len(products[0]), (slot_x, slot_y), [start for _, start in names]
            ),
            [own_a, got_a, own_b, got_b] + [Raw(one) for one in given],
            [(shapes_out[name], F32, "raw") for name, _ in names],
            [pltpu.VMEM((width // 2, size), F32) for size in sizes for _ in range(2)],
            moves=2 * len(names),
            limit=30,
            update=update,
        )
        for (name, _), one in zip(names, done):
            outputs[name] = one

    def small_stages():
        (packed,) = order.call(
            pack_small,
            [small_entry(step) for step in range(passes)] + [small_middle(step) for step in range(passes)],
            [((-(-(8 + passes) // 8) * 8, width), F32)], limit=8
        )
        hops = [("section", 1), ("section", 2)] + [("dp", bits) for bits in dp_bits]
        for axis, bits in hops[:-1]:
            got = lax.ppermute(packed, axis, xor_pairs(axis, bits))
            yield
            (packed,) = order.call(add_small, [packed, got], [(packed.shape, F32)], limit=8)
        axis, bits = hops[-1]
        got = lax.ppermute(packed, axis, xor_pairs(axis, bits))
        yield
        outputs["small"] = order.call(
            part_small,
            [packed, got],
            [((2, width), F32)] * 4 + [((passes, width), F32)],
            limit=8,
        )

    def input_stages(entered_t):
        got = exchange(entered_t)
        yield
        (grad_t,) = order.call(
            place_items,
            [Raw(one) for one in got],
            [((batches, slice_width, half_rows), F32, "raw")],
            [pltpu.VMEM((section_count, slice_width, half_rows), F32)],
            moves=section_count + 1,
            limit=8,
        )
        outputs["inputs"] = jnp.swapaxes(grad_t, 1, 2)

    running = {}

    def advance(name):
        if name not in running:
            running[name] = stages(name)
        next(running[name], None)

    passes_out = None
    for step in reversed(range(2, passes)):
        fed = feed_step(step)
        if step == passes - 1:
            passes_got = exchange(
                order.call(
                    split_items,
                    [Raw(results)],
                    [((half_rows, width), F32, "raw")] * section_count,
                    moves=section_count,
                    limit=4,
                )
            )
        state = attention_step(step, fed)

    def chain():
        nonlocal state, passes_out
        fed = feed_step(1)
        yield
        state = attention_step(1, fed)
        yield
        fed = feed_step(0)
        yield
        state = attention_step(0, fed)
        yield
        near_dr, part, other = state
        entered_t = order.call(
            entry_backward,
            [Near(part), Near(other), Near(near_dr), entered(0), gain_one],
            [small_entry(0)] + [((slice_width, half_rows), F32, "raw")] * section_count,
            [entry_v, pltpu.VMEM((section_count, slice_width, half_rows), F32)],
            moves=section_count,
        )
        (passes_out,) = order.call(
            place_items,
            [Raw(one) for one in passes_got],
            [((batches, half_rows, width), F32, "raw")],
            [pltpu.VMEM((section_count, half_rows, width), F32)],
            moves=section_count + 1,
            limit=8,
        )
        running["inputs"] = input_stages(entered_t)
        next(running["inputs"])
        running["small"] = small_stages()

    running["chain"] = chain()
    for name in schedule(len(dp_bits), len(kinds)):
        advance(name)
    for name in list(running):
        for _ in running[name]:
            pass
    return (
        passes_out[None],
        outputs["inputs"],
        *[outputs[name] for name in ("query", "key", "value", "out", "up", "down")],
        *outputs["small"],
    )


def solution(mesh):
    weight = P(None, None, "tensor")
    return jax.shard_map(
        shards,
        mesh=mesh,
        in_specs=(
            P("dp", "tensor", "section"),
            P("dp"),
            weight,
            weight,
            weight,
            weight,
            weight,
            weight,
            P(),
            P(),
            P(),
            P(),
            P(),
            P("section", "dp", "tensor", None),
        ),
        out_specs=(
            P("section", "dp", "tensor", None),
            P("dp", "tensor", "section"),
            weight,
            weight,
            weight,
            weight,
            weight,
            weight,
            P(),
            P(),
            P(),
            P(),
            P(),
        ),
        check_vma=False,
    )
```

```python
import functools

import jax
import jax.numpy as jnp
from jax import lax
from jax.experimental import pallas as pl
from jax.experimental.pallas import tpu as pltpu
from jax.sharding import PartitionSpec as P

HEADS = 12
EPSILON = 1e-05
MASKED = -1e30
F32 = jnp.float32
BF16 = jnp.bfloat16
ROOT = 0.7978845608028654
CUBIC = 0.044715
BLOCKS = 2
NN = (((1,), (0,)), ((), ()))
NT = (((1,), (1,)), ((), ()))
TN = (((0,), (0,)), ((), ()))


def dot(left, right, dims=NN):
    return lax.dot_general(left, right, dims, preferred_element_type=F32)


def norm_parts(rows):
    centred = rows - jnp.mean(rows, axis=-1, keepdims=True)
    spread = jnp.mean(centred * centred, axis=-1, keepdims=True)
    inverse = lax.rsqrt(spread + EPSILON)
    return centred * inverse, inverse


def norm_back(rows, gain, grad):
    normal, inverse = norm_parts(rows)
    scaled = gain * grad
    middle = jnp.mean(scaled, axis=-1, keepdims=True)
    along = jnp.mean(scaled * normal, axis=-1, keepdims=True)
    back = inverse * (scaled - middle - normal * along)
    gain_sum = jnp.sum(grad * normal, axis=0, keepdims=True)
    bias_sum = jnp.sum(grad, axis=0, keepdims=True)
    return back, gain_sum, bias_sum


def both(own, other):
    return own[...].astype(F32) + other[...].astype(F32)


class Incoming:
    def __init__(self, source, place, sem):
        self.copy = pltpu.make_async_copy(source, place, sem)
        self.copy.start()
        self.place = place
        self.waiting = True

    def ref(self):
        if self.waiting:
            self.copy.wait()
            self.waiting = False
        return self.place

    def __getitem__(self, index):
        return self.ref()[index]


class Outgoing:
    def __init__(self, place, target, sem):
        self.place = place
        self.copy = pltpu.make_async_copy(place, target, sem)

    def put(self, value):
        self.place[...] = value
        self.copy.start()

    def __getitem__(self, index):
        return self.place[index]

    def __setitem__(self, index, value):
        self.place[index] = value


class Chosen:
    def __init__(self, array, index):
        self.array, self.index = array, index


class Near:
    def __init__(self, array):
        self.array = array


class Held:
    def __init__(self, name, *index):
        self.name, self.index = name, index


class Raw:
    def __init__(self, array):
        self.array = array


class Far(Raw):
    pass


class Scalars:
    def __init__(self, array):
        self.array = array


class Mover:
    def __init__(self, sems):
        self.sems, self.used = sems, 0

    def start(self, source, target):
        copy = pltpu.make_async_copy(source, target, self.sems.at[self.used])
        self.used += 1
        copy.start()
        return copy


class Order:
    def __init__(self, shapes):
        self.shapes = shapes
        self.stores = {}

    def call(self, body, operands, outs, scratch=(), limit=20, moves=0, update=None, name=None):
        inner = body
        while isinstance(inner, functools.partial):
            inner = inner.func
        name = name or inner.__name__
        kind = lambda one: one[2] if isinstance(one, tuple) and len(one) > 2 else "staged"
        plain = lambda one: not isinstance(one, (Near, Raw, Scalars))
        names = ["order"] + [one.name for one in operands + outs if isinstance(one, Held)]
        names = list(dict.fromkeys(names))
        old = [name for name in names if name in self.stores]
        new = [name for name in names if name not in self.stores]
        given = [one for one in operands if not isinstance(one, Held)]
        made = [one for one in outs if not isinstance(one, Held)]
        arrays = [one.array if isinstance(one, (Chosen, Near, Raw, Scalars)) else one for one in given]

        def shape_of(one):
            if isinstance(one, Held):
                shape, dtype = self.shapes[one.name]
                for index in one.index:
                    if isinstance(index, int):
                        shape = shape[1:]
                    else:
                        sizes = [
                            cut.stop - cut.start if isinstance(cut, slice) else cut for cut in index
                        ]
                        shape = tuple(sizes) + tuple(shape[len(sizes) :])
                return shape, dtype
            if isinstance(one, Chosen):
                return one.array.shape[1:], one.array.dtype
            if isinstance(one, tuple):
                return one[0], one[1]
            return one.shape, one.dtype

        places = [pltpu.VMEM(*shape_of(one)) for one in operands if plain(one)]
        places += [pltpu.VMEM(*shape_of(one)) for one in outs if kind(one) == "staged"]
        first_out = len(old) + len(given)
        total = first_out + len(names) + len(made)
        count = len(places)

        def part(stores, one):
            ref = stores[one.name]
            for index in one.index:
                ref = ref.at[index]
            return ref

        def kernel(*refs):
            in_refs = list(refs[len(old) : first_out])
            stores = dict(zip(old + new, refs[first_out : first_out + len(names)]))
            out_refs = list(refs[first_out + len(names) : total])
            rooms = refs[total : total + count]
            sems, more = refs[total + count], refs[total + count + 1]
            rest = refs[total + count + 2 :]
            ins, results = [], []
            at = 0
            for one in operands:
                ref = part(stores, one) if isinstance(one, Held) else in_refs.pop(0)
                if plain(one):
                    source = ref.at[one.index] if isinstance(one, Chosen) else ref
                    ins.append(Incoming(source, rooms[at], sems.at[at]))
                    at += 1
                else:
                    ins.append(ref)
            for one in outs:
                ref = part(stores, one) if isinstance(one, Held) else out_refs.pop(0)
                if kind(one) == "staged":
                    results.append(Outgoing(rooms[at], ref, sems.at[at]))
                    at += 1
                else:
                    results.append(ref)
            extra = (Mover(more),) if moves else ()
            body(ins, results, *extra, *rest)
            for one in ins:
                if isinstance(one, Incoming):
                    one.ref()
            for one in results:
                if isinstance(one, Outgoing):
                    one.copy.wait()

        anywhere = pl.BlockSpec(memory_space=pl.ANY)
        inside = pl.BlockSpec(memory_space=pltpu.VMEM)
        scalar = pl.BlockSpec(memory_space=pltpu.SMEM)
        spec = lambda one: inside if isinstance(one, Near) else scalar if isinstance(one, Scalars) else anywhere
        aliases = {at: at for at in range(len(old))}
        for out_at, in_at in (update or {}).items():
            shift_in = sum(isinstance(one, Held) for one in operands[:in_at])
            shift_out = sum(isinstance(one, Held) for one in outs[:out_at])
            aliases[len(old) + in_at - shift_in] = len(names) + out_at - shift_out
        shapes = [pltpu.HBM(*self.shapes[name]) for name in old + new]
        for one in made:
            form = pltpu.VMEM if kind(one) == "near" else jax.ShapeDtypeStruct
            shapes.append(form(one[0], one[1]))
        arrays = [
            pltpu.with_memory_space_constraint(array, pltpu.VMEM)
            if isinstance(one, Near)
            else pltpu.with_memory_space_constraint(array, pltpu.HBM)
            if isinstance(one, (Chosen, Far)) or array.size * array.dtype.itemsize < 20000
            and not isinstance(one, (Raw, Scalars))
            else array
            for one, array in zip(given, arrays)
        ]
        done = pl.pallas_call(
            kernel,
            name=name,
            out_shape=tuple(shapes),
            in_specs=[anywhere] * len(old) + [spec(one) for one in given],
            out_specs=(anywhere,) * len(names)
            + tuple(inside if kind(one) == "near" else anywhere for one in made),
            scratch_shapes=places
            + [pltpu.SemaphoreType.DMA((max(count, 1),)), pltpu.SemaphoreType.DMA((max(moves, 1),))]
            + list(scratch),
            input_output_aliases=aliases,
            compiler_params=pltpu.CompilerParams(vmem_limit_bytes=int(limit * 1024 * 1024)),
            cost_estimate=pl.CostEstimate(flops=1000, bytes_accessed=1000, transcendentals=0),
        )(
            *[pltpu.with_memory_space_constraint(self.stores[name], pltpu.HBM) for name in old],
            *arrays,
        )
        self.stores.update(zip(old + new, done[: len(names)]))
        return done[len(names) :]


class Place:
    def __getitem__(self, slot):
        name, bits = slot
        return (lax.axis_index(name) // bits) % 2 if bits else lax.axis_index(name)


HERE = Place()


def causal_mask(length):
    key_place = lax.broadcasted_iota(jnp.int32, (length, length), 0)
    query_place = lax.broadcasted_iota(jnp.int32, (length, length), 1)
    return key_place <= query_place


def lane_half(half, pair):
    lane = lax.broadcasted_iota(jnp.int32, pair.shape, 1)
    keep = (lane < 64) if half == 0 else (lane >= 64)
    return jnp.where(keep, pair, jnp.zeros_like(pair))


def present_in(counts, step):
    item = lax.axis_index("section")
    last = counts.shape[0] - 1
    own_count = jnp.where(item <= last, counts[jnp.minimum(item, last)], 0)
    return jnp.where(own_count > step, 1.0, 0.0).astype(F32)


def attention_forward(step, layer, ins, outs, mover, turned, *rest):
    count = 2 if step == 0 else 3
    first, (embed, gain, bias, wq, wk, wv, wo) = ins[:count], ins[count : count + 7]
    past_k, past_vt = ins[count + 7 : count + 7 + step], ins[count + 7 + step : count + 7 + 2 * step]
    sent = None
    if step == 0:
        own_t, other_t = first
        (entry_v,) = rest
        half = own_t.shape[1]
        place = pl.multiple_of(lax.axis_index("tensor") * half, half)
        entry_v[pl.ds(place, half), :] = own_t[...].T
        entry_v[pl.ds(pl.multiple_of(half - place, half), half), :] = other_t[...].T
        entered = entry_v[...] + embed[0:1, :]
    else:
        near_r, own, other = first
        counts = ins[count + 7 + 2 * step]
        (entry_v,) = rest
        result = near_r[...] + both(own, other)
        entry_v[...] = result * present_in(counts, step - 1)
        half = entry_v.shape[0] // 2
        place = pl.multiple_of(lax.axis_index("tensor") * half, half)
        sent = mover.start(entry_v.at[pl.ds(place, half)], outs[0].at[step - 1])
        outs = outs[1:]
        entered = result + embed[step : step + 1, :]
    near_out = outs[0]
    near_out[...] = entered
    outs = outs[1:]
    u_out, a_out, q_out, k_out, kt_out, v_out, vt_out, lse_out, o_out, part_out = outs
    u_out.put(entered)
    normal, _ = norm_parts(entered)
    a = (normal * gain[layer : layer + 1, :] + bias[layer : layer + 1, :]).astype(BF16)
    a_out.put(a)
    q_out.put((dot(a, wq[layer]).astype(BF16).astype(F32) * 0.125).astype(BF16))
    k_full = dot(a, wk[layer])
    k_out.put(k_full.astype(BF16))
    v_full = dot(a, wv[layer])
    vt_out.put(v_full.T.astype(BF16))
    v_out.put(v_full.astype(BF16))
    kt_out.put(k_full.T.astype(BF16))
    length = entered.shape[0]
    seen = causal_mask(length)
    all_k = past_k + [k_out]
    all_vt = past_vt + [vt_out]
    pairs = wq.shape[2] // 128

    def one_pair(pair, carry):
        lanes = pl.ds(pl.multiple_of(128 * pair, 128), 128)
        for half in range(2):
            query = lane_half(half, q_out[:, lanes])
            scores = [jnp.where(seen, dot(key[:, lanes], query, NT), MASKED) for key in all_k]
            highest = functools.reduce(
                jnp.maximum, [jnp.max(one, axis=0, keepdims=True) for one in scores]
            )
            powers = [jnp.exp(one - highest) for one in scores]
            total = functools.reduce(
                jnp.add, [jnp.sum(one, axis=0, keepdims=True) for one in powers]
            )
            inverse = 1.0 / total
            lse_out[pl.ds(2 * pair + half, 1), :] = highest + jnp.log(total)
            rows = pl.ds(pl.multiple_of(128 * pair + 64 * half, 64), 64)
            mixed = None
            for power, value in zip(powers, all_vt):
                term = dot(value[rows, :], (power * inverse).astype(BF16))
                mixed = term if mixed is None else mixed + term
            turned[rows, :] = mixed
        return carry

    for one in past_k + past_vt:
        one.ref()
    lax.fori_loop(0, pairs, one_pair, 0)
    lse_out.copy.start()
    o = turned[...].T.astype(BF16)
    o_out.put(o)
    part_out[...] = dot(o, wo[layer], NT).astype(BF16)
    if sent is not None:
        sent.wait()


def gelu_parts(hidden):
    square = hidden * hidden
    bent = jnp.tanh(ROOT * hidden * (1.0 + CUBIC * square))
    return square, bent


def feed_forward(layer, ins, outs):
    own, other, u, gain, bias, wu, wd = ins[:7]
    near_out, r_out, b_out, g_out, m_out, part_out = outs[:6]
    middle = u[...] + both(own, other)
    near_out[...] = middle
    r_out.put(middle)
    normal, _ = norm_parts(middle)
    b = (normal * gain[layer : layer + 1, :] + bias[layer : layer + 1, :]).astype(BF16)
    b_out.put(b)
    total = None
    width = wu.shape[2] // BLOCKS
    for block in range(BLOCKS):
        across = slice(block * width, (block + 1) * width)
        hidden = dot(b, wu[layer, :, across])
        g_out[:, across] = hidden
        _, bent = gelu_parts(hidden)
        m = (0.5 * hidden * (1.0 + bent)).astype(BF16)
        m_out[:, across] = m
        term = dot(m, wd[layer, :, across], NT)
        total = term if total is None else total + term
    g_out.copy.start()
    m_out.copy.start()
    part_out[...] = total.astype(BF16)


def small_put(out, rows):
    rows = rows + [jnp.zeros_like(rows[0])] * (8 - len(rows))
    out.put(jnp.concatenate(rows, axis=0))


def feed_backward(step, layer, last, ins, outs, mover, cot_v, *more):
    counts, cot_own, cot_other, wd, wu = ins[:5]
    near_out, e_out, dg_out, part_out = outs[:4]
    half = cot_v.shape[0] // 2
    place = pl.multiple_of(lax.axis_index("tensor") * half, half)
    copies = [
        mover.start(cot_own.at[step], cot_v.at[pl.ds(place, half)]),
        mover.start(cot_other.at[step], cot_v.at[pl.ds(pl.multiple_of(half - place, half), half)]),
    ]
    present = present_in(counts, step)
    if last:
        near_r, own, other, g = ins[5:]
        (end_v,) = more
        end_v[...] = (near_r[...] + both(own, other)) * present
        sent = mover.start(end_v.at[pl.ds(place, half)], outs[4].at[step])
    else:
        own, other, dr, u, gain, g = ins[5:]
        back, gain_sum, bias_sum = norm_back(u[...], gain[1:2, :], both(own, other))
        entered = dr[...] + back
        small_put(outs[4], [gain_sum, bias_sum, jnp.sum(entered, axis=0, keepdims=True)])
    for copy in copies:
        copy.wait()
    grad = cot_v[...].astype(F32) * present
    if not last:
        grad = grad + entered
    near_out[...] = grad
    e = grad.astype(BF16)
    e_out.put(e)
    total = None
    width = wu.shape[2] // BLOCKS
    for block in range(BLOCKS):
        across = slice(block * width, (block + 1) * width)
        raw = dot(e, wd[layer, :, across])
        hidden = g[:, across]
        square, bent = gelu_parts(hidden)
        slope = 0.5 * (1.0 + bent) + 0.5 * hidden * (1.0 - bent * bent) * ROOT * (
            1.0 + 3.0 * CUBIC * square
        )
        dg = (raw * slope).astype(BF16)
        dg_out[:, across] = dg
        term = dot(dg, wu[layer, :, across], NT)
        total = term if total is None else total + term
    dg_out.copy.start()
    part_out[...] = total.astype(BF16)
    if last:
        sent.wait()


def attention_backward(step, layer, last, ins, outs, do_v, dqt_v):
    own, other, dh, r, gain, wo, q, lse = ins[:8]
    count = step + 1
    keys, values, keys_t = ins[8 : 8 + count], ins[8 + count : 8 + 2 * count], ins[8 + 2 * count : 8 + 3 * count]
    rest = ins[8 + 3 * count :]
    if not last:
        dk_in, dv_in = rest[:2]
    wq, wk, wv = rest[-3:]
    near_out, f_out, dq_out, dk_out, dv_out, part_out, small_out = outs[:7]
    if step > 0:
        dk_all, dv_all = outs[7:]
    back, gain_sum, bias_sum = norm_back(r[...], gain[layer : layer + 1, :], both(own, other))
    small_put(small_out, [gain_sum, bias_sum])
    grad = dh[...] + back
    near_out[...] = grad
    f = grad.astype(BF16)
    f_out.put(f)
    do_v[...] = dot(f, wo[layer]).astype(BF16)
    length = f.shape[0]
    seen = causal_mask(length)
    pairs = q.place.shape[1] // 128

    def one_pair(pair, carry):
        lanes = pl.ds(pl.multiple_of(128 * pair, 128), 128)
        key_sums = [None] * count
        value_sums = [None] * count
        for half in range(2):
            rows = pl.ds(pl.multiple_of(128 * pair + 64 * half, 64), 64)
            query = lane_half(half, q[:, lanes])
            grad_mix = lane_half(half, do_v[:, lanes])
            total = lse[pl.ds(2 * pair + half, 1), :]
            exact = [
                jnp.exp(jnp.where(seen, dot(key[:, lanes], query, NT), MASKED) - total)
                for key in keys
            ]
            grad_weights = [dot(value[:, lanes], grad_mix, NT) for value in values]
            delta = functools.reduce(
                jnp.add,
                [jnp.sum(p * dp, axis=0, keepdims=True) for p, dp in zip(exact, grad_weights)],
            )
            query_grad = None
            for slot in range(count):
                grad_scores = (exact[slot] * (grad_weights[slot] - delta)).astype(BF16)
                term = dot(keys_t[slot][rows, :], grad_scores)
                query_grad = term if query_grad is None else query_grad + term
                key_term = dot(grad_scores, query)
                value_term = dot(exact[slot].astype(BF16), grad_mix)
                if half == 0:
                    key_sums[slot] = key_term
                    value_sums[slot] = value_term
                else:
                    key_sums[slot] = key_sums[slot] + key_term
                    value_sums[slot] = value_sums[slot] + value_term
            dqt_v[rows, :] = query_grad
        for slot in range(count):
            key_sum, value_sum = key_sums[slot], value_sums[slot]
            if not last:
                key_sum = key_sum + dk_in[slot, :, lanes]
                value_sum = value_sum + dv_in[slot, :, lanes]
            if slot == step:
                dk_out[:, lanes] = key_sum.astype(BF16)
                dv_out[:, lanes] = value_sum.astype(BF16)
            else:
                dk_all[slot, :, lanes] = key_sum
                dv_all[slot, :, lanes] = value_sum
        return carry

    for one in [q, lse] + keys + values + keys_t + ([] if last else [dk_in, dv_in]):
        one.ref()
    lax.fori_loop(0, pairs, one_pair, 0)
    for one in (dk_out, dv_out) + ((dk_all, dv_all) if step > 0 else ()):
        one.copy.start()
    dq = (dqt_v[...].T * 0.125).astype(BF16)
    dq_out.put(dq)
    part = dot(dq, wq[layer], NT) + dot(dk_out[...], wk[layer], NT) + dot(dv_out[...], wv[layer], NT)
    part_out[...] = part.astype(BF16)


def entry_backward(ins, outs, mover, entry_v, pieces_v):
    own, other, dr, u, gain = ins
    back, gain_sum, bias_sum = norm_back(u[...], gain[0:1, :], both(own, other))
    entered = dr[...] + back
    entry_v[...] = entered
    half = entry_v.shape[0] // 2
    place = pl.multiple_of(lax.axis_index("tensor") * half, half)
    turned = entry_v[pl.ds(place, half), :].T
    pieces_v[...] = turned.reshape(pieces_v.shape)
    section = lax.axis_index("section")
    copies = [mover.start(pieces_v.at[section ^ bits], out) for bits, out in enumerate(outs[1:])]
    small_put(outs[0], [gain_sum, bias_sum, jnp.sum(entered, axis=0, keepdims=True)])
    for copy in copies:
        copy.wait()


def place_items(ins, outs, mover, room):
    section = lax.axis_index("section")
    copies = [mover.start(piece, room.at[section ^ bits]) for bits, piece in enumerate(ins)]
    for copy in copies:
        copy.wait()
    mover.start(room.at[pl.ds(0, outs[0].shape[0])], outs[0]).wait()


def place_pieces(ins, outs, mover):
    section = lax.axis_index("section")
    count = len(ins) // len(outs)
    copies = []
    for at, piece in enumerate(ins):
        rows = piece.shape[0]
        place = pl.multiple_of((section ^ (at % count)) * rows, rows)
        copies.append(mover.start(piece, outs[at // count].at[pl.ds(place, rows)]))
    for copy in copies:
        copy.wait()


def place_beside(ins, outs, mover):
    place_pieces(ins[:-1], outs[:1], mover)


def split_items(ins, outs, mover):
    last = ins[0].shape[0] - 1
    section = lax.axis_index("section")
    copies = [
        mover.start(ins[0].at[jnp.minimum(section ^ bits, last)], out)
        for bits, out in enumerate(outs)
    ]
    for copy in copies:
        copy.wait()


def split_cotangent(ins, outs, mover, rooms, sent):
    last = ins[0].shape[1] - 1
    section = lax.axis_index("section")
    copies = [
        mover.start(ins[0].at[0].at[jnp.minimum(section ^ bits, last)], rooms.at[bits])
        for bits in range(rooms.shape[0])
    ]
    for bits, out in enumerate(outs):
        copies[bits].wait()
        sent[bits] = rooms[bits].astype(BF16)
        copies.append(mover.start(sent.at[bits], out))
    for copy in copies[len(outs) :]:
        copy.wait()


def load(ins, outs, mover):
    copies = [mover.start(source, target) for source, target in zip(ins, outs)]
    for copy in copies:
        copy.wait()


def pack_small(ins, outs):
    passes = (len(ins)) // 2
    entry, middle = ins[:passes], ins[passes:]
    rows = []
    for kind in (entry, middle):
        for row in range(2):
            rows.append(kind[0][row : row + 1, :])
            later = kind[1][row : row + 1, :]
            for step in range(2, passes):
                later = later + kind[step][row : row + 1, :]
            rows.append(later)
    rows += [entry[step][2:3, :] for step in range(passes)]
    rows += [jnp.zeros_like(rows[0])] * (-len(rows) % 8)
    outs[0].put(jnp.concatenate(rows, axis=0))


def add_small(ins, outs):
    outs[0].put(ins[0][...] + ins[1][...])


def part_small(ins, outs):
    total = ins[0][...] + ins[1][...]
    at = 0
    for out in outs:
        count = out.place.shape[0]
        out.put(total[at : at + count])
        at += count


def halves(slot, room, axis):
    size = room.shape[axis] // 2
    kept = pl.multiple_of(HERE[slot] * size, size)
    sent = pl.multiple_of(size - kept, size)
    if axis == 0:
        return room.at[pl.ds(kept, size)], room.at[pl.ds(sent, size)]
    return room.at[:, pl.ds(kept, size)], room.at[:, pl.ds(sent, size)]


def weight_first(products, splits, sharing, ins, outs, mover, *rooms):
    factors = ins
    copies = []
    for at, (room, slot) in enumerate(zip(rooms, splits)):
        column = 0
        for pairs in products[at]:
            total = None
            for left, right in pairs:
                term = dot(factors[left][...], factors[right][...], TN)
                total = term if total is None else total + term
            room[:, column : column + total.shape[1]] = total.astype(BF16)
            column += total.shape[1]
        kept, sent = halves(slot, room, 0)
        columns = room.shape[1] // sharing
        for one in range(sharing):
            across = (slice(None), pl.ds(one * columns, columns))
            copies.append(mover.start(sent.at[across], outs[4 * one + 2 * at + 1]))
            copies.append(mover.start(kept.at[across], outs[4 * one + 2 * at]))
    for copy in copies:
        copy.wait()


def add_split(slots, axis, ins, outs, mover, *rooms):
    copies = []
    for at, (room, slot) in enumerate(zip(rooms, slots)):
        room[...] = (ins[2 * at][...].astype(F32) + ins[2 * at + 1][...].astype(F32)).astype(BF16)
        kept, sent = halves(slot, room, axis)
        copies.append(mover.start(sent, outs[2 * at + 1]))
        copies.append(mover.start(kept, outs[2 * at]))
    for copy in copies:
        copy.wait()


def add_merge(slot, axis, ins, outs, mover, room):
    columns = room.shape[1] // 2
    for at in range(2):
        total = ins[2 * at][...].astype(F32) + ins[2 * at + 1][...].astype(F32)
        room[:, at * columns : (at + 1) * columns] = total.astype(BF16)
    kept, sent = halves(slot, room, axis)
    copies = [mover.start(sent, outs[1]), mover.start(kept, outs[0])]
    for copy in copies:
        copy.wait()


def add_last(ins, outs):
    outs[0].put((ins[0][...].astype(F32) + ins[1][...].astype(F32)).astype(BF16))


def join(slots, axis, ins, outs, mover):
    copies = []
    for at, slot in enumerate(slots):
        own, other = halves(slot, outs[at], axis)
        copies.append(mover.start(ins[2 * at], own))
        copies.append(mover.start(ins[2 * at + 1], other))
    for copy in copies:
        copy.wait()


def join_part(slot, axis, ins, outs, mover, room):
    own, other = halves(slot, room, axis)
    copies = [mover.start(ins[0], own), mover.start(ins[1], other)]
    for copy in copies:
        copy.wait()
    columns = room.shape[1] // 2
    copies = [mover.start(room.at[:, pl.ds(at * columns, columns)], outs[at]) for at in range(2)]
    for copy in copies:
        copy.wait()


def finish(layer, parts, slots, starts, ins, outs, mover, *rooms):
    halves_in = ins[:4]
    copies = []
    out_at = 0
    for at, slot in enumerate(slots):
        rows = halves_in[2 * at].place.shape[0]
        for which in range(2):
            place = HERE[slot] * rows
            place = pl.multiple_of(place if which == 0 else rows - place, rows)
            column = 0
            for part in range(parts):
                room = rooms[2 * (out_at + part) + which]
                columns = room.shape[1]
                room[...] = halves_in[2 * at + which][:, column : column + columns].astype(F32)
                target = outs[out_at + part].at[layer]
                across = pl.ds(starts[out_at + part], columns)
                copies.append(mover.start(room, target.at[pl.ds(place, rows), across]))
                column += columns
        out_at += parts
    for copy in copies:
        copy.wait()


def swap(value):
    return lax.ppermute(value, "tensor", [(0, 1), (1, 0)])


def xor_pairs(axis, bits):
    return [(place, place ^ bits) for place in range(lax.axis_size(axis))]


def pick(stacked, index):
    return lax.dynamic_index_in_dim(stacked, index, 0, keepdims=False)


SPLITS = (2, 2)
CHAIN, SMALL, INPUTS = 6, 7, 8
STEPS = (
    6, 0, 6, 2, 6, 0, 6, 1, 1, 3, 2, 0, 1, 6, 0, 2, 4, 1, 0, 3,
    2, 1, 0, 4, 8, 1, 3, 1, 7, 2, 7, 4, 7, 5, 2, 0, 7, 1, 4, 3,
    5, 4, 7, 3, 4, 2, 5, 0, 3, 4, 1, 2, 5, 0, 3, 5, 2, 4, 3, 5,
    5, 4, 5, 3, 5,
)


def schedule(levels, groups):
    names = {CHAIN: "chain", SMALL: "small", INPUTS: "inputs"}
    if levels == 2 and groups == sum(SPLITS) + 2:
        return [names.get(step, step) for step in STEPS]
    order = ["chain"]
    order += list(range(SPLITS[1])) + ["chain", SPLITS[1]]
    order += ["chain"] * 3
    for step in range(2 * levels + 5):
        order += list(range(groups))
    return order


def shards(
    inputs,
    counts,
    w_query,
    w_key,
    w_value,
    w_out,
    w_up,
    w_down,
    gain_one,
    bias_one,
    gain_two,
    bias_two,
    pass_embed,
    cotangent,
):
    section_count = lax.axis_size("section")
    section = lax.axis_index("section")
    tensor = lax.axis_index("tensor")
    batches, half_rows, slice_width = inputs.shape
    length = 2 * half_rows
    width = cotangent.shape[3]
    head_width = w_query.shape[2]
    hidden_width = w_up.shape[2]
    passes = pass_embed.shape[0]
    dp_count = lax.axis_size("dp")
    dp_place = lax.axis_index("dp")
    dp_bits = [1 << level for level in range(dp_count.bit_length() - 1)]
    order = Order(
        {
            "order": ((2, passes, length, head_width), F32),
            "low": ((passes, 4, length, width), BF16),
            "hidden": ((passes, 2, length, hidden_width), BF16),
            "heads": ((passes, 7, length, head_width), BF16),
            "turned": ((passes, 4, head_width, length), BF16),
            "wide": ((passes, 2 * length + 24, width), F32),
            "before": ((passes, length, hidden_width), F32),
        }
    )

    def exchange(pieces):
        return [pieces[0]] + [
            lax.ppermute(pieces[bits], "section", xor_pairs("section", bits))
            for bits in range(1, section_count)
        ]

    slot_x, slot_y = ("section", 1), ("section", 2)
    slots_dp = [("dp", bits) for bits in dp_bits]

    inputs_t = jnp.swapaxes(inputs, 1, 2)
    got = exchange(
        order.call(
            split_items,
            [Far(inputs_t)],
            [((slice_width, half_rows), F32, "raw")] * section_count,
            moves=section_count,
            limit=4,
        )
    )
    cot_sent = order.call(
        split_cotangent,
        [Far(cotangent)],
        [((half_rows, width), BF16, "raw")] * section_count,
        [pltpu.VMEM((section_count, half_rows, width), kind) for kind in (F32, BF16)],
        moves=2 * section_count,
        limit=8,
    )

    def bring(weights):
        return order.call(
            load,
            [Far(one) for one in weights],
            [(one.shape, one.dtype, "near") for one in weights],
            moves=len(weights),
            limit=8,
        )

    w_query, w_key, w_value, w_out = bring((w_query, w_key, w_value, w_out))
    cot_got = exchange(cot_sent)
    (entry_t,) = order.call(
        place_pieces,
        [Raw(one) for one in got],
        [((width, half_rows), F32, "near")],
        moves=section_count,
        limit=8,
    )
    entry_other = swap(entry_t)

    wide_near = ((length, width), F32, "near")
    part_near = ((length, width), BF16, "near")
    stacked = ((passes, half_rows, width), F32, "raw")
    turned = pltpu.VMEM((head_width, length), F32)
    entry_v = pltpu.VMEM((length, width), F32)
    cot_v = pltpu.VMEM((length, width), BF16)
    whole = slice(None)

    def low(step, name):
        return Held("low", step, "abef".index(name))

    def hidden(step, name):
        return Held("hidden", step, ("m", "dg").index(name))

    def heads(step, name):
        return Held("heads", step, ("q", "k", "v", "o", "dq", "dk", "dv").index(name))

    def turn(step, name):
        return Held("turned", step, ("kt", "vt").index(name))

    def rows(step, start, count, columns=None):
        cut = (slice(start, start + count), slice(0, columns or width))
        return Held("wide", step, cut)

    def entered(step):
        return rows(step, 0, length)

    def middle(step):
        return rows(step, length, length)

    def logsum(step):
        return rows(step, 2 * length, 8, length)

    def small_entry(step):
        return rows(step, 2 * length + 8, 8)

    def small_middle(step):
        return rows(step, 2 * length + 16, 8)

    results = None
    resid = None
    cot_own = cot_other = None
    for step in range(passes):
        layer = min(step, 1)
        first = [Near(entry_t), Near(entry_other)] if step == 0 else [Near(one) for one in resid]
        weights = [Near(one) for one in (w_query, w_key, w_value, w_out)]
        operands = first + [pass_embed, gain_one, bias_one] + weights
        operands += [heads(past, "k") for past in range(step)]
        operands += [turn(past, "vt") for past in range(step)]
        update = None
        if step > 0:
            operands.append(Scalars(counts))
        if step > 1:
            operands.append(Raw(results))
            update = {0: len(operands) - 1}
        done = order.call(
            functools.partial(attention_forward, step, layer),
            operands,
            ([] if step == 0 else [stacked])
            + [wide_near, entered(step), low(step, "a"), heads(step, "q"), heads(step, "k")]
            + [turn(step, "kt"), heads(step, "v"), turn(step, "vt"), logsum(step)]
            + [heads(step, "o"), part_near],
            [turned, entry_v],
            moves=1,
            update=update,
        )
        if step > 0:
            results = done[0]
            done = done[1:]
        near_u, part = done
        if step == 0:
            w_up, w_down = bring((w_up, w_down))
            cot_flat, part = order.call(
                place_beside,
                [Raw(one) for one in cot_got] + [Near(part)],
                [((section_count * half_rows, width), BF16, "raw"), part_near],
                moves=section_count,
                limit=8,
                update={1: section_count},
            )
            cot_own = cot_flat.reshape(section_count, half_rows, width)
            cot_other = swap(cot_own)
        near_r, part_two = order.call(
            functools.partial(feed_forward, layer),
            [Near(part), Near(swap(part)), Near(near_u), gain_two, bias_two]
            + [Near(w_up), Near(w_down)],
            [wide_near, middle(step), low(step, "b"), Held("before", step), hidden(step, "m"), part_near],
        )
        resid = (near_r, part_two, swap(part_two))

    factors = [
        {name: low(step, name) for name in "abef"}
        | {name: hidden(step, name) for name in ("m", "dg")}
        | {name: heads(step, name) for name in ("o", "dq", "dk", "dv")}
        for step in range(passes)
    ]
    state = None

    def feed_step(step):
        nonlocal results
        layer = min(step, 1)
        last = step == passes - 1
        operands = [Scalars(counts), Raw(cot_own), Raw(cot_other)]
        operands += [Near(w_down), Near(w_up)]
        outs = [wide_near, low(step, "e"), hidden(step, "dg"), part_near]
        update = None
        if last:
            operands += [Near(one) for one in resid] + [Held("before", step)]
            outs += [stacked]
            operands.append(Raw(results))
            update = {4: len(operands) - 1}
        else:
            dr, part, other = state
            operands += [Near(part), Near(other), Near(dr), entered(step + 1), gain_one]
            operands += [Held("before", step)]
            outs += [small_entry(step + 1)]

        def body(ins, outs, mover, *rooms):
            feed_backward(step, layer, last, ins[:9] if last else ins, outs, mover, *rooms)

        done = order.call(
            body,
            operands,
            outs,
            [cot_v] + ([entry_v] if last else []),
            moves=3,
            update=update,
            name=feed_backward.__name__,
        )
        near_dh, part = done[:2]
        if last:
            results = done[2]
        return near_dh, part, swap(part)

    def attention_step(step, fed):
        layer = min(step, 1)
        last = step == passes - 1
        near_dh, part, other = fed
        operands = [Near(part), Near(other), Near(near_dh), middle(step), gain_two]
        operands += [Near(w_out), heads(step, "q"), logsum(step)]
        operands += [heads(past, "k") for past in range(step + 1)]
        operands += [heads(past, "v") for past in range(step + 1)]
        operands += [turn(past, "kt") for past in range(step + 1)]
        cut = (slice(0, step + 1),)
        if not last:
            operands += [Held("order", at, cut) for at in range(2)]
        operands += [Near(one) for one in (w_query, w_key, w_value)]
        outs = [wide_near, low(step, "f"), heads(step, "dq"), heads(step, "dk"), heads(step, "dv")]
        outs += [part_near, small_middle(step)]
        if step > 0:
            outs += [Held("order", at, (slice(0, step),)) for at in range(2)]
        near_dr, part = order.call(
            functools.partial(attention_backward, step, layer, last),
            operands,
            outs,
            [pltpu.VMEM((length, head_width), BF16), turned],
        )
        return near_dr, part, swap(part)

    later, early = list(range(1, passes)), [0]
    def feed_group(steps, start):
        first = [("up", start, [(low(step, "b"), hidden(step, "dg")) for step in steps])]
        second = [("down", start, [(low(step, "e"), hidden(step, "m")) for step in steps])]
        return (first, second)

    def heads_group(steps):
        def product(name, left, right):
            return (name, 0, [(low(step, left), heads(step, right)) for step in steps])

        first = [product("query", "a", "dq"), product("key", "a", "dk")]
        second = [product("out", "f", "o"), product("value", "a", "dv")]
        return (first, second)

    kinds = []
    for layer, steps in ((1, later), (0, early)):
        first = len(kinds)
        columns = hidden_width // SPLITS[layer]
        for start in range(0, hidden_width, columns):
            kinds.append((layer, first, columns, feed_group(steps, start)))
        kinds.append((layer, len(kinds), width, heads_group(steps)))
    made = {}
    shapes_out = {name: (2, width, head_width) for name in ("query", "key", "value", "out")}
    shapes_out |= {name: (2, width, hidden_width) for name in ("up", "down")}
    outputs = {}

    def make_products(group):
        layer, first, columns, products = kinds[group]
        sharing = [at for at, one in enumerate(kinds) if one[1] == first]
        operands, place = [], {}

        def number(held):
            key = (held.name, str(held.index))
            if key not in place:
                place[key] = len(operands)
                operands.append(held)
            return place[key]

        numbered = [
            [[(number(left), number(right)) for left, right in pairs] for _, _, pairs in part]
            for part in products
        ]
        done = order.call(
            functools.partial(weight_first, numbered, (slot_x, slot_y), len(sharing)),
            operands,
            [((width // 2, columns), BF16, "raw")] * (4 * len(sharing)),
            [pltpu.VMEM((width, columns * len(sharing)), BF16)] * 2,
            moves=4 * len(sharing),
            limit=30,
        )
        for at, one in enumerate(sharing):
            made[one] = done[4 * at : 4 * at + 4]

    def stages(group):
        layer, first, columns, products = kinds[group]
        sizes = [columns // len(part) for part in products for _ in part]
        room = lambda rows, cols: pltpu.VMEM((rows, cols), BF16)
        raw = lambda rows, cols: ((rows, cols), BF16, "raw")
        send = lambda value, axis, bits: lax.ppermute(value, axis, xor_pairs(axis, bits))
        if first == group:
            make_products(group)
        kept_a, sent_a, kept_b, sent_b = made[group]
        got_a, got_b = send(sent_a, "section", 1), send(sent_b, "section", 2)
        yield
        kept_a, sent_a, kept_b, sent_b = order.call(
            functools.partial(add_split, (slot_y, slot_x), 0),
            [kept_a, got_a, kept_b, got_b],
            [raw(width // 4, columns)] * 4,
            [room(width // 2, columns)] * 2,
            moves=4,
            limit=30,
        )
        got_a, got_b = send(sent_a, "section", 2), send(sent_b, "section", 1)
        yield
        shape = [width // 4, 2 * columns]
        axes = []
        for level, bits in enumerate(dp_bits):
            axis = 0 if shape[0] % 32 == 0 else 1
            axes.append(axis)
            before = tuple(shape)
            shape[axis] //= 2
            if level == 0:
                own, sent = order.call(
                    functools.partial(add_merge, slots_dp[level], axis),
                    [kept_a, got_a, kept_b, got_b],
                    [raw(*shape)] * 2,
                    [room(*before)],
                    moves=2,
                    limit=24,
                )
            else:
                own, sent = order.call(
                    functools.partial(add_split, (slots_dp[level],), axis),
                    [own, got],
                    [raw(*shape)] * 2,
                    [room(*before)],
                    moves=2,
                    limit=16,
                )
            got = send(sent, "dp", bits)
            yield
        (own,) = order.call(add_last, [own, got], [(tuple(shape), BF16)], limit=16)
        got = send(own, "dp", dp_bits[-1])
        yield
        for level in reversed(range(len(dp_bits))):
            axis = axes[level]
            shape[axis] *= 2
            if level > 0:
                (own,) = order.call(
                    functools.partial(join, (slots_dp[level],), axis),
                    [Raw(own), Raw(got)],
                    [raw(*shape)],
                    moves=2,
                    limit=16,
                )
                got = send(own, "dp", dp_bits[level - 1])
                yield
        own_a, own_b = order.call(
            functools.partial(join_part, slots_dp[0], axes[0]),
            [Raw(own), Raw(got)],
            [raw(width // 4, columns)] * 2,
            [room(*shape)],
            moves=4,
            limit=16,
        )
        got_a, got_b = send(own_a, "section", 2), send(own_b, "section", 1)
        yield
        own_a, own_b = order.call(
            functools.partial(join, (slot_y, slot_x), 0),
            [Raw(own_a), Raw(got_a), Raw(own_b), Raw(got_b)],
            [raw(width // 2, columns)] * 2,
            moves=4,
            limit=16,
        )
        got_a, got_b = send(own_a, "section", 1), send(own_b, "section", 2)
        yield
        names = [(name, start) for part in products for name, start, _ in part]
        before = [outputs.get(name) for name, _ in names]
        given = [one for one in before if one is not None]
        update = {}
        for at, one in enumerate(before):
            if one is not None:
                update[at] = 4 + len(update)
        done = order.call(
            functools.partial(
                finish, layer, len(products[0]), (slot_x, slot_y), [start for _, start in names]
            ),
            [own_a, got_a, own_b, got_b] + [Raw(one) for one in given],
            [(shapes_out[name], F32, "raw") for name, _ in names],
            [pltpu.VMEM((width // 2, size), F32) for size in sizes for _ in range(2)],
            moves=2 * len(names),
            limit=30,
            update=update,
        )
        for (name, _), one in zip(names, done):
            outputs[name] = one

    def small_stages():
        (packed,) = order.call(
            pack_small,
            [small_entry(step) for step in range(passes)] + [small_middle(step) for step in range(passes)],
            [((-(-(8 + passes) // 8) * 8, width), F32)], limit=8
        )
        hops = [("section", 1), ("section", 2)] + [("dp", bits) for bits in dp_bits]
        for axis, bits in hops[:-1]:
            got = lax.ppermute(packed, axis, xor_pairs(axis, bits))
            yield
            (packed,) = order.call(add_small, [packed, got], [(packed.shape, F32)], limit=8)
        axis, bits = hops[-1]
        got = lax.ppermute(packed, axis, xor_pairs(axis, bits))
        yield
        outputs["small"] = order.call(
            part_small,
            [packed, got],
            [((2, width), F32)] * 4 + [((passes, width), F32)],
            limit=8,
        )

    def input_stages(entered_t):
        got = exchange(entered_t)
        yield
        (grad_t,) = order.call(
            place_items,
            [Raw(one) for one in got],
            [((batches, slice_width, half_rows), F32, "raw")],
            [pltpu.VMEM((section_count, slice_width, half_rows), F32)],
            moves=section_count + 1,
            limit=8,
        )
        outputs["inputs"] = jnp.swapaxes(grad_t, 1, 2)

    running = {}

    def advance(name):
        if name not in running:
            running[name] = stages(name)
        next(running[name], None)

    passes_out = None
    for step in reversed(range(2, passes)):
        fed = feed_step(step)
        if step == passes - 1:
            passes_got = exchange(
                order.call(
                    split_items,
                    [Raw(results)],
                    [((half_rows, width), F32, "raw")] * section_count,
                    moves=section_count,
                    limit=4,
                )
            )
        state = attention_step(step, fed)

    def chain():
        nonlocal state, passes_out
        fed = feed_step(1)
        yield
        state = attention_step(1, fed)
        yield
        fed = feed_step(0)
        yield
        state = attention_step(0, fed)
        yield
        near_dr, part, other = state
        entered_t = order.call(
            entry_backward,
            [Near(part), Near(other), Near(near_dr), entered(0), gain_one],
            [small_entry(0)] + [((slice_width, half_rows), F32, "raw")] * section_count,
            [entry_v, pltpu.VMEM((section_count, slice_width, half_rows), F32)],
            moves=section_count,
        )
        (passes_out,) = order.call(
            place_items,
            [Raw(one) for one in passes_got],
            [((batches, half_rows, width), F32, "raw")],
            [pltpu.VMEM((section_count, half_rows, width), F32)],
            moves=section_count + 1,
            limit=8,
        )
        running["inputs"] = input_stages(entered_t)
        next(running["inputs"])
        running["small"] = small_stages()

    running["chain"] = chain()
    for name in schedule(len(dp_bits), len(kinds)):
        advance(name)
    for name in list(running):
        for _ in running[name]:
            pass
    return (
        passes_out[None],
        outputs["inputs"],
        *[outputs[name] for name in ("query", "key", "value", "out", "up", "down")],
        *outputs["small"],
    )


def solution(mesh):
    weight = P(None, None, "tensor")
    return jax.shard_map(
        shards,
        mesh=mesh,
        in_specs=(
            P("dp", "tensor", "section"),
            P("dp"),
            weight,
            weight,
            weight,
            weight,
            weight,
            weight,
            P(),
            P(),
            P(),
            P(),
            P(),
            P("section", "dp", "tensor", None),
        ),
        out_specs=(
            P("section", "dp", "tensor", None),
            P("dp", "tensor", "section"),
            weight,
            weight,
            weight,
            weight,
            weight,
            weight,
            P(),
            P(),
            P(),
            P(),
            P(),
        ),
        check_vma=False,
    )
```

```python
import functools

import jax
import jax.numpy as jnp
from jax import lax
from jax.experimental import pallas as pl
from jax.experimental.pallas import tpu as pltpu
from jax.sharding import PartitionSpec as P

HEADS = 12
EPSILON = 1e-05
MASKED = -1e30
F32 = jnp.float32
BF16 = jnp.bfloat16
ROOT = 0.7978845608028654
CUBIC = 0.044715
BLOCKS = 2
NN = (((1,), (0,)), ((), ()))
NT = (((1,), (1,)), ((), ()))
TN = (((0,), (0,)), ((), ()))


def dot(left, right, dims=NN):
    return lax.dot_general(left, right, dims, preferred_element_type=F32)


def norm_parts(rows):
    centred = rows - jnp.mean(rows, axis=-1, keepdims=True)
    spread = jnp.mean(centred * centred, axis=-1, keepdims=True)
    inverse = lax.rsqrt(spread + EPSILON)
    return centred * inverse, inverse


def norm_back(rows, gain, grad):
    normal, inverse = norm_parts(rows)
    scaled = gain * grad
    middle = jnp.mean(scaled, axis=-1, keepdims=True)
    along = jnp.mean(scaled * normal, axis=-1, keepdims=True)
    back = inverse * (scaled - middle - normal * along)
    gain_sum = jnp.sum(grad * normal, axis=0, keepdims=True)
    bias_sum = jnp.sum(grad, axis=0, keepdims=True)
    return back, gain_sum, bias_sum


def both(own, other):
    return own[...].astype(F32) + other[...].astype(F32)


class Incoming:
    def __init__(self, source, place, sem):
        self.copy = pltpu.make_async_copy(source, place, sem)
        self.copy.start()
        self.place = place
        self.waiting = True

    def ref(self):
        if self.waiting:
            self.copy.wait()
            self.waiting = False
        return self.place

    def __getitem__(self, index):
        return self.ref()[index]


class Outgoing:
    def __init__(self, place, target, sem):
        self.place = place
        self.copy = pltpu.make_async_copy(place, target, sem)

    def put(self, value):
        self.place[...] = value
        self.copy.start()

    def __getitem__(self, index):
        return self.place[index]

    def __setitem__(self, index, value):
        self.place[index] = value


class Chosen:
    def __init__(self, array, index):
        self.array, self.index = array, index


class Near:
    def __init__(self, array):
        self.array = array


class Held:
    def __init__(self, name, *index):
        self.name, self.index = name, index


class Raw:
    def __init__(self, array):
        self.array = array


class Far(Raw):
    pass


class Scalars:
    def __init__(self, array):
        self.array = array


class Mover:
    def __init__(self, sems):
        self.sems, self.used = sems, 0

    def start(self, source, target):
        copy = pltpu.make_async_copy(source, target, self.sems.at[self.used])
        self.used += 1
        copy.start()
        return copy


class Order:
    def __init__(self, shapes):
        self.shapes = shapes
        self.stores = {}

    def call(self, body, operands, outs, scratch=(), limit=20, moves=0, update=None, name=None):
        inner = body
        while isinstance(inner, functools.partial):
            inner = inner.func
        name = name or inner.__name__
        kind = lambda one: one[2] if isinstance(one, tuple) and len(one) > 2 else "staged"
        plain = lambda one: not isinstance(one, (Near, Raw, Scalars))
        names = ["order"] + [one.name for one in operands + outs if isinstance(one, Held)]
        names = list(dict.fromkeys(names))
        old = [name for name in names if name in self.stores]
        new = [name for name in names if name not in self.stores]
        given = [one for one in operands if not isinstance(one, Held)]
        made = [one for one in outs if not isinstance(one, Held)]
        arrays = [one.array if isinstance(one, (Chosen, Near, Raw, Scalars)) else one for one in given]

        def shape_of(one):
            if isinstance(one, Held):
                shape, dtype = self.shapes[one.name]
                for index in one.index:
                    if isinstance(index, int):
                        shape = shape[1:]
                    else:
                        sizes = [
                            cut.stop - cut.start if isinstance(cut, slice) else cut for cut in index
                        ]
                        shape = tuple(sizes) + tuple(shape[len(sizes) :])
                return shape, dtype
            if isinstance(one, Chosen):
                return one.array.shape[1:], one.array.dtype
            if isinstance(one, tuple):
                return one[0], one[1]
            return one.shape, one.dtype

        places = [pltpu.VMEM(*shape_of(one)) for one in operands if plain(one)]
        places += [pltpu.VMEM(*shape_of(one)) for one in outs if kind(one) == "staged"]
        first_out = len(old) + len(given)
        total = first_out + len(names) + len(made)
        count = len(places)

        def part(stores, one):
            ref = stores[one.name]
            for index in one.index:
                ref = ref.at[index]
            return ref

        def kernel(*refs):
            in_refs = list(refs[len(old) : first_out])
            stores = dict(zip(old + new, refs[first_out : first_out + len(names)]))
            out_refs = list(refs[first_out + len(names) : total])
            rooms = refs[total : total + count]
            sems, more = refs[total + count], refs[total + count + 1]
            rest = refs[total + count + 2 :]
            ins, results = [], []
            at = 0
            for one in operands:
                ref = part(stores, one) if isinstance(one, Held) else in_refs.pop(0)
                if plain(one):
                    source = ref.at[one.index] if isinstance(one, Chosen) else ref
                    ins.append(Incoming(source, rooms[at], sems.at[at]))
                    at += 1
                else:
                    ins.append(ref)
            for one in outs:
                ref = part(stores, one) if isinstance(one, Held) else out_refs.pop(0)
                if kind(one) == "staged":
                    results.append(Outgoing(rooms[at], ref, sems.at[at]))
                    at += 1
                else:
                    results.append(ref)
            extra = (Mover(more),) if moves else ()
            body(ins, results, *extra, *rest)
            for one in ins:
                if isinstance(one, Incoming):
                    one.ref()
            for one in results:
                if isinstance(one, Outgoing):
                    one.copy.wait()

        anywhere = pl.BlockSpec(memory_space=pl.ANY)
        inside = pl.BlockSpec(memory_space=pltpu.VMEM)
        scalar = pl.BlockSpec(memory_space=pltpu.SMEM)
        spec = lambda one: inside if isinstance(one, Near) else scalar if isinstance(one, Scalars) else anywhere
        aliases = {at: at for at in range(len(old))}
        for out_at, in_at in (update or {}).items():
            shift_in = sum(isinstance(one, Held) for one in operands[:in_at])
            shift_out = sum(isinstance(one, Held) for one in outs[:out_at])
            aliases[len(old) + in_at - shift_in] = len(names) + out_at - shift_out
        shapes = [pltpu.HBM(*self.shapes[name]) for name in old + new]
        for one in made:
            form = pltpu.VMEM if kind(one) == "near" else jax.ShapeDtypeStruct
            shapes.append(form(one[0], one[1]))
        arrays = [
            pltpu.with_memory_space_constraint(array, pltpu.VMEM)
            if isinstance(one, Near)
            else pltpu.with_memory_space_constraint(array, pltpu.HBM)
            if isinstance(one, (Chosen, Far)) or array.size * array.dtype.itemsize < 20000
            and not isinstance(one, (Raw, Scalars))
            else array
            for one, array in zip(given, arrays)
        ]
        done = pl.pallas_call(
            kernel,
            name=name,
            out_shape=tuple(shapes),
            in_specs=[anywhere] * len(old) + [spec(one) for one in given],
            out_specs=(anywhere,) * len(names)
            + tuple(inside if kind(one) == "near" else anywhere for one in made),
            scratch_shapes=places
            + [pltpu.SemaphoreType.DMA((max(count, 1),)), pltpu.SemaphoreType.DMA((max(moves, 1),))]
            + list(scratch),
            input_output_aliases=aliases,
            compiler_params=pltpu.CompilerParams(vmem_limit_bytes=int(limit * 1024 * 1024)),
            cost_estimate=pl.CostEstimate(flops=1000, bytes_accessed=1000, transcendentals=0),
        )(
            *[pltpu.with_memory_space_constraint(self.stores[name], pltpu.HBM) for name in old],
            *arrays,
        )
        self.stores.update(zip(old + new, done[: len(names)]))
        return done[len(names) :]


class Place:
    def __getitem__(self, slot):
        name, bits = slot
        return (lax.axis_index(name) // bits) % 2 if bits else lax.axis_index(name)


HERE = Place()


def causal_mask(length):
    key_place = lax.broadcasted_iota(jnp.int32, (length, length), 0)
    query_place = lax.broadcasted_iota(jnp.int32, (length, length), 1)
    return key_place <= query_place


def lane_half(half, pair):
    lane = lax.broadcasted_iota(jnp.int32, pair.shape, 1)
    keep = (lane < 64) if half == 0 else (lane >= 64)
    return jnp.where(keep, pair, jnp.zeros_like(pair))


def present_in(counts, step):
    item = lax.axis_index("section")
    last = counts.shape[0] - 1
    own_count = jnp.where(item <= last, counts[jnp.minimum(item, last)], 0)
    return jnp.where(own_count > step, 1.0, 0.0).astype(F32)


def attention_forward(step, layer, ins, outs, mover, turned, *rest):
    count = 2 if step == 0 else 3
    first, (embed, gain, bias, wq, wk, wv, wo) = ins[:count], ins[count : count + 7]
    past_k, past_vt = ins[count + 7 : count + 7 + step], ins[count + 7 + step : count + 7 + 2 * step]
    sent = None
    if step == 0:
        own_t, other_t = first
        (entry_v,) = rest
        half = own_t.shape[1]
        place = pl.multiple_of(lax.axis_index("tensor") * half, half)
        entry_v[pl.ds(place, half), :] = own_t[...].T
        entry_v[pl.ds(pl.multiple_of(half - place, half), half), :] = other_t[...].T
        entered = entry_v[...] + embed[0:1, :]
    else:
        near_r, own, other = first
        counts = ins[count + 7 + 2 * step]
        (entry_v,) = rest
        result = near_r[...] + both(own, other)
        entry_v[...] = result * present_in(counts, step - 1)
        half = entry_v.shape[0] // 2
        place = pl.multiple_of(lax.axis_index("tensor") * half, half)
        sent = mover.start(entry_v.at[pl.ds(place, half)], outs[0].at[step - 1])
        outs = outs[1:]
        entered = result + embed[step : step + 1, :]
    near_out = outs[0]
    near_out[...] = entered
    outs = outs[1:]
    u_out, a_out, q_out, k_out, kt_out, v_out, vt_out, lse_out, o_out, part_out = outs
    u_out.put(entered)
    normal, _ = norm_parts(entered)
    a = (normal * gain[layer : layer + 1, :] + bias[layer : layer + 1, :]).astype(BF16)
    a_out.put(a)
    q_out.put((dot(a, wq[layer]).astype(BF16).astype(F32) * 0.125).astype(BF16))
    k_full = dot(a, wk[layer])
    k_out.put(k_full.astype(BF16))
    v_full = dot(a, wv[layer])
    vt_out.put(v_full.T.astype(BF16))
    v_out.put(v_full.astype(BF16))
    kt_out.put(k_full.T.astype(BF16))
    length = entered.shape[0]
    seen = causal_mask(length)
    all_k = past_k + [k_out]
    all_vt = past_vt + [vt_out]
    pairs = wq.shape[2] // 128

    def one_pair(pair, carry):
        lanes = pl.ds(pl.multiple_of(128 * pair, 128), 128)
        for half in range(2):
            query = lane_half(half, q_out[:, lanes])
            scores = [jnp.where(seen, dot(key[:, lanes], query, NT), MASKED) for key in all_k]
            highest = functools.reduce(
                jnp.maximum, [jnp.max(one, axis=0, keepdims=True) for one in scores]
            )
            powers = [jnp.exp(one - highest) for one in scores]
            total = functools.reduce(
                jnp.add, [jnp.sum(one, axis=0, keepdims=True) for one in powers]
            )
            inverse = 1.0 / total
            lse_out[pl.ds(2 * pair + half, 1), :] = highest + jnp.log(total)
            rows = pl.ds(pl.multiple_of(128 * pair + 64 * half, 64), 64)
            mixed = None
            for power, value in zip(powers, all_vt):
                term = dot(value[rows, :], power.astype(BF16))
                mixed = term if mixed is None else mixed + term
            turned[rows, :] = mixed * inverse
        return carry

    for one in past_k + past_vt:
        one.ref()
    lax.fori_loop(0, pairs, one_pair, 0)
    lse_out.copy.start()
    o = turned[...].T.astype(BF16)
    o_out.put(o)
    part_out[...] = dot(o, wo[layer], NT).astype(BF16)
    if sent is not None:
        sent.wait()


def gelu_parts(hidden):
    square = hidden * hidden
    bent = jnp.tanh(ROOT * hidden * (1.0 + CUBIC * square))
    return square, bent


def feed_forward(layer, ins, outs):
    own, other, u, gain, bias, wu, wd = ins[:7]
    near_out, r_out, b_out, g_out, m_out, part_out = outs[:6]
    middle = u[...] + both(own, other)
    near_out[...] = middle
    r_out.put(middle)
    normal, _ = norm_parts(middle)
    b = (normal * gain[layer : layer + 1, :] + bias[layer : layer + 1, :]).astype(BF16)
    b_out.put(b)
    total = None
    width = wu.shape[2] // BLOCKS
    for block in range(BLOCKS):
        across = slice(block * width, (block + 1) * width)
        hidden = dot(b, wu[layer, :, across])
        g_out[:, across] = hidden
        _, bent = gelu_parts(hidden)
        m = (0.5 * hidden * (1.0 + bent)).astype(BF16)
        m_out[:, across] = m
        term = dot(m, wd[layer, :, across], NT)
        total = term if total is None else total + term
    g_out.copy.start()
    m_out.copy.start()
    part_out[...] = total.astype(BF16)


def small_put(out, rows):
    rows = rows + [jnp.zeros_like(rows[0])] * (8 - len(rows))
    out.put(jnp.concatenate(rows, axis=0))


def feed_backward(step, layer, last, ins, outs, mover, cot_v, *more):
    counts, cot_own, cot_other, wd, wu = ins[:5]
    near_out, e_out, dg_out, part_out = outs[:4]
    half = cot_v.shape[0] // 2
    place = pl.multiple_of(lax.axis_index("tensor") * half, half)
    copies = [
        mover.start(cot_own.at[step], cot_v.at[pl.ds(place, half)]),
        mover.start(cot_other.at[step], cot_v.at[pl.ds(pl.multiple_of(half - place, half), half)]),
    ]
    present = present_in(counts, step)
    if last:
        near_r, own, other, g = ins[5:]
        (end_v,) = more
        end_v[...] = (near_r[...] + both(own, other)) * present
        sent = mover.start(end_v.at[pl.ds(place, half)], outs[4].at[step])
    else:
        own, other, dr, u, gain, g = ins[5:]
        back, gain_sum, bias_sum = norm_back(u[...], gain[1:2, :], both(own, other))
        entered = dr[...] + back
        small_put(outs[4], [gain_sum, bias_sum, jnp.sum(entered, axis=0, keepdims=True)])
    for copy in copies:
        copy.wait()
    grad = cot_v[...].astype(F32) * present
    if not last:
        grad = grad + entered
    near_out[...] = grad
    e = grad.astype(BF16)
    e_out.put(e)
    total = None
    width = wu.shape[2] // BLOCKS
    for block in range(BLOCKS):
        across = slice(block * width, (block + 1) * width)
        raw = dot(e, wd[layer, :, across])
        hidden = g[:, across]
        square, bent = gelu_parts(hidden)
        slope = 0.5 * (1.0 + bent) + 0.5 * hidden * (1.0 - bent * bent) * ROOT * (
            1.0 + 3.0 * CUBIC * square
        )
        dg = (raw * slope).astype(BF16)
        dg_out[:, across] = dg
        term = dot(dg, wu[layer, :, across], NT)
        total = term if total is None else total + term
    dg_out.copy.start()
    part_out[...] = total.astype(BF16)
    if last:
        sent.wait()


def attention_backward(step, layer, last, ins, outs, do_v, dqt_v, delta_v):
    own, other, dh, r, gain, wo, q, lse = ins[:8]
    o, ins = ins[8], ins[:8] + ins[9:]
    count = step + 1
    keys, values, keys_t = ins[8 : 8 + count], ins[8 + count : 8 + 2 * count], ins[8 + 2 * count : 8 + 3 * count]
    rest = ins[8 + 3 * count :]
    if not last:
        dk_in, dv_in = rest[:2]
    wq, wk, wv = rest[-3:]
    near_out, f_out, dq_out, dk_out, dv_out, part_out, small_out = outs[:7]
    if step > 0:
        dk_all, dv_all = outs[7:]
    back, gain_sum, bias_sum = norm_back(r[...], gain[layer : layer + 1, :], both(own, other))
    small_put(small_out, [gain_sum, bias_sum])
    grad = dh[...] + back
    near_out[...] = grad
    f = grad.astype(BF16)
    f_out.put(f)
    do_v[...] = dot(f, wo[layer]).astype(BF16)
    both_mixed = do_v[...].astype(F32) * o[...].astype(F32)
    head_of = lax.broadcasted_iota(jnp.int32, (8, do_v.shape[1]), 1) // 64
    own_head = lax.broadcasted_iota(jnp.int32, (8, do_v.shape[1]), 0) == head_of
    delta_v[...] = lax.dot_general(
        jnp.where(own_head, 1.0, 0.0).astype(F32),
        both_mixed,
        NT,
        precision=lax.Precision.HIGHEST,
        preferred_element_type=F32,
    )
    length = f.shape[0]
    seen = causal_mask(length)
    pairs = q.place.shape[1] // 128

    def one_pair(pair, carry):
        lanes = pl.ds(pl.multiple_of(128 * pair, 128), 128)
        key_sums = [None] * count
        value_sums = [None] * count
        for half in range(2):
            rows = pl.ds(pl.multiple_of(128 * pair + 64 * half, 64), 64)
            query = lane_half(half, q[:, lanes])
            grad_mix = lane_half(half, do_v[:, lanes])
            total = lse[pl.ds(2 * pair + half, 1), :]
            exact = [
                jnp.exp(jnp.where(seen, dot(key[:, lanes], query, NT), MASKED) - total)
                for key in keys
            ]
            grad_weights = [dot(value[:, lanes], grad_mix, NT) for value in values]
            delta = delta_v[pl.ds(2 * pair + half, 1), :]
            query_grad = None
            for slot in range(count):
                grad_scores = (exact[slot] * (grad_weights[slot] - delta)).astype(BF16)
                term = dot(keys_t[slot][rows, :], grad_scores)
                query_grad = term if query_grad is None else query_grad + term
                key_term = dot(grad_scores, query)
                value_term = dot(exact[slot].astype(BF16), grad_mix)
                if half == 0:
                    key_sums[slot] = key_term
                    value_sums[slot] = value_term
                else:
                    key_sums[slot] = key_sums[slot] + key_term
                    value_sums[slot] = value_sums[slot] + value_term
            dqt_v[rows, :] = query_grad
        for slot in range(count):
            key_sum, value_sum = key_sums[slot], value_sums[slot]
            if not last:
                key_sum = key_sum + dk_in[slot, :, lanes]
                value_sum = value_sum + dv_in[slot, :, lanes]
            if slot == step:
                dk_out[:, lanes] = key_sum.astype(BF16)
                dv_out[:, lanes] = value_sum.astype(BF16)
            else:
                dk_all[slot, :, lanes] = key_sum
                dv_all[slot, :, lanes] = value_sum
        return carry

    for one in [q, lse] + keys + values + keys_t + ([] if last else [dk_in, dv_in]):
        one.ref()
    lax.fori_loop(0, pairs, one_pair, 0)
    for one in (dk_out, dv_out) + ((dk_all, dv_all) if step > 0 else ()):
        one.copy.start()
    dq = (dqt_v[...].T * 0.125).astype(BF16)
    dq_out.put(dq)
    part = dot(dq, wq[layer], NT) + dot(dk_out[...], wk[layer], NT) + dot(dv_out[...], wv[layer], NT)
    part_out[...] = part.astype(BF16)


def entry_backward(ins, outs, mover, entry_v, pieces_v):
    own, other, dr, u, gain = ins
    back, gain_sum, bias_sum = norm_back(u[...], gain[0:1, :], both(own, other))
    entered = dr[...] + back
    entry_v[...] = entered
    half = entry_v.shape[0] // 2
    place = pl.multiple_of(lax.axis_index("tensor") * half, half)
    turned = entry_v[pl.ds(place, half), :].T
    pieces_v[...] = turned.reshape(pieces_v.shape)
    section = lax.axis_index("section")
    copies = [mover.start(pieces_v.at[section ^ bits], out) for bits, out in enumerate(outs[1:])]
    small_put(outs[0], [gain_sum, bias_sum, jnp.sum(entered, axis=0, keepdims=True)])
    for copy in copies:
        copy.wait()


def place_items(ins, outs, mover, room):
    section = lax.axis_index("section")
    copies = [mover.start(piece, room.at[section ^ bits]) for bits, piece in enumerate(ins)]
    for copy in copies:
        copy.wait()
    mover.start(room.at[pl.ds(0, outs[0].shape[0])], outs[0]).wait()


def place_pieces(ins, outs, mover):
    section = lax.axis_index("section")
    count = len(ins) // len(outs)
    copies = []
    for at, piece in enumerate(ins):
        rows = piece.shape[0]
        place = pl.multiple_of((section ^ (at % count)) * rows, rows)
        copies.append(mover.start(piece, outs[at // count].at[pl.ds(place, rows)]))
    for copy in copies:
        copy.wait()


def place_beside(ins, outs, mover):
    place_pieces(ins[:-1], outs[:1], mover)


def split_items(ins, outs, mover):
    last = ins[0].shape[0] - 1
    section = lax.axis_index("section")
    copies = [
        mover.start(ins[0].at[jnp.minimum(section ^ bits, last)], out)
        for bits, out in enumerate(outs)
    ]
    for copy in copies:
        copy.wait()


def split_cotangent(ins, outs, mover, rooms, sent):
    last = ins[0].shape[1] - 1
    section = lax.axis_index("section")
    copies = [
        mover.start(ins[0].at[0].at[jnp.minimum(section ^ bits, last)], rooms.at[bits])
        for bits in range(rooms.shape[0])
    ]
    for bits, out in enumerate(outs):
        copies[bits].wait()
        sent[bits] = rooms[bits].astype(BF16)
        copies.append(mover.start(sent.at[bits], out))
    for copy in copies[len(outs) :]:
        copy.wait()


def load(ins, outs, mover):
    copies = [mover.start(source, target) for source, target in zip(ins, outs)]
    for copy in copies:
        copy.wait()


def pack_small(ins, outs):
    passes = (len(ins)) // 2
    entry, middle = ins[:passes], ins[passes:]
    rows = []
    for kind in (entry, middle):
        for row in range(2):
            rows.append(kind[0][row : row + 1, :])
            later = kind[1][row : row + 1, :]
            for step in range(2, passes):
                later = later + kind[step][row : row + 1, :]
            rows.append(later)
    rows += [entry[step][2:3, :] for step in range(passes)]
    rows += [jnp.zeros_like(rows[0])] * (-len(rows) % 8)
    outs[0].put(jnp.concatenate(rows, axis=0))


def add_small(ins, outs):
    outs[0].put(ins[0][...] + ins[1][...])


def part_small(ins, outs):
    total = ins[0][...] + ins[1][...]
    at = 0
    for out in outs:
        count = out.place.shape[0]
        out.put(total[at : at + count])
        at += count


def halves(slot, room, axis):
    size = room.shape[axis] // 2
    kept = pl.multiple_of(HERE[slot] * size, size)
    sent = pl.multiple_of(size - kept, size)
    if axis == 0:
        return room.at[pl.ds(kept, size)], room.at[pl.ds(sent, size)]
    return room.at[:, pl.ds(kept, size)], room.at[:, pl.ds(sent, size)]


def weight_first(products, splits, sharing, ins, outs, mover, *rooms):
    factors = ins
    copies = []
    for at, (room, slot) in enumerate(zip(rooms, splits)):
        column = 0
        for pairs in products[at]:
            total = None
            for left, right in pairs:
                term = dot(factors[left][...], factors[right][...], TN)
                total = term if total is None else total + term
            room[:, column : column + total.shape[1]] = total.astype(BF16)
            column += total.shape[1]
        kept, sent = halves(slot, room, 0)
        columns = room.shape[1] // sharing
        for one in range(sharing):
            across = (slice(None), pl.ds(one * columns, columns))
            copies.append(mover.start(sent.at[across], outs[4 * one + 2 * at + 1]))
            copies.append(mover.start(kept.at[across], outs[4 * one + 2 * at]))
    for copy in copies:
        copy.wait()


def add_split(slots, axis, ins, outs, mover, *rooms):
    copies = []
    for at, (room, slot) in enumerate(zip(rooms, slots)):
        room[...] = (ins[2 * at][...].astype(F32) + ins[2 * at + 1][...].astype(F32)).astype(BF16)
        kept, sent = halves(slot, room, axis)
        copies.append(mover.start(sent, outs[2 * at + 1]))
        copies.append(mover.start(kept, outs[2 * at]))
    for copy in copies:
        copy.wait()


def add_merge(slot, axis, ins, outs, mover, room):
    columns = room.shape[1] // 2
    for at in range(2):
        total = ins[2 * at][...].astype(F32) + ins[2 * at + 1][...].astype(F32)
        room[:, at * columns : (at + 1) * columns] = total.astype(BF16)
    kept, sent = halves(slot, room, axis)
    copies = [mover.start(sent, outs[1]), mover.start(kept, outs[0])]
    for copy in copies:
        copy.wait()


def add_last(ins, outs):
    outs[0].put((ins[0][...].astype(F32) + ins[1][...].astype(F32)).astype(BF16))


def join(slots, axis, ins, outs, mover):
    copies = []
    for at, slot in enumerate(slots):
        own, other = halves(slot, outs[at], axis)
        copies.append(mover.start(ins[2 * at], own))
        copies.append(mover.start(ins[2 * at + 1], other))
    for copy in copies:
        copy.wait()


def join_part(slot, axis, ins, outs, mover, room):
    own, other = halves(slot, room, axis)
    copies = [mover.start(ins[0], own), mover.start(ins[1], other)]
    for copy in copies:
        copy.wait()
    columns = room.shape[1] // 2
    copies = [mover.start(room.at[:, pl.ds(at * columns, columns)], outs[at]) for at in range(2)]
    for copy in copies:
        copy.wait()


def finish(layer, parts, slots, starts, ins, outs, mover, *rooms):
    halves_in = ins[:4]
    copies = []
    out_at = 0
    for at, slot in enumerate(slots):
        rows = halves_in[2 * at].place.shape[0]
        for which in range(2):
            place = HERE[slot] * rows
            place = pl.multiple_of(place if which == 0 else rows - place, rows)
            column = 0
            for part in range(parts):
                room = rooms[2 * (out_at + part) + which]
                columns = room.shape[1]
                room[...] = halves_in[2 * at + which][:, column : column + columns].astype(F32)
                target = outs[out_at + part].at[layer]
                across = pl.ds(starts[out_at + part], columns)
                copies.append(mover.start(room, target.at[pl.ds(place, rows), across]))
                column += columns
        out_at += parts
    for copy in copies:
        copy.wait()


def swap(value):
    return lax.ppermute(value, "tensor", [(0, 1), (1, 0)])


def xor_pairs(axis, bits):
    return [(place, place ^ bits) for place in range(lax.axis_size(axis))]


def pick(stacked, index):
    return lax.dynamic_index_in_dim(stacked, index, 0, keepdims=False)


SPLITS = (2, 2)
CHAIN, SMALL, INPUTS = 6, 7, 8
STEPS = (
    6, 0, 6, 2, 6, 0, 6, 1, 1, 3, 2, 0, 1, 6, 0, 2, 4, 1, 0, 3,
    2, 1, 0, 4, 8, 1, 3, 1, 7, 2, 7, 4, 7, 5, 2, 0, 7, 1, 4, 3,
    5, 4, 7, 3, 4, 2, 5, 0, 3, 4, 1, 2, 5, 0, 3, 5, 2, 4, 3, 5,
    5, 4, 5, 3, 5,
)


def schedule(levels, groups):
    names = {CHAIN: "chain", SMALL: "small", INPUTS: "inputs"}
    if levels == 2 and groups == sum(SPLITS) + 2:
        return [names.get(step, step) for step in STEPS]
    order = ["chain"]
    order += list(range(SPLITS[1])) + ["chain", SPLITS[1]]
    order += ["chain"] * 3
    for step in range(2 * levels + 5):
        order += list(range(groups))
    return order


def shards(
    inputs,
    counts,
    w_query,
    w_key,
    w_value,
    w_out,
    w_up,
    w_down,
    gain_one,
    bias_one,
    gain_two,
    bias_two,
    pass_embed,
    cotangent,
):
    section_count = lax.axis_size("section")
    section = lax.axis_index("section")
    tensor = lax.axis_index("tensor")
    batches, half_rows, slice_width = inputs.shape
    length = 2 * half_rows
    width = cotangent.shape[3]
    head_width = w_query.shape[2]
    hidden_width = w_up.shape[2]
    passes = pass_embed.shape[0]
    dp_count = lax.axis_size("dp")
    dp_place = lax.axis_index("dp")
    dp_bits = [1 << level for level in range(dp_count.bit_length() - 1)]
    order = Order(
        {
            "order": ((2, passes, length, head_width), F32),
            "low": ((passes, 4, length, width), BF16),
            "hidden": ((passes, 2, length, hidden_width), BF16),
            "heads": ((passes, 7, length, head_width), BF16),
            "turned": ((passes, 4, head_width, length), BF16),
            "wide": ((passes, 2 * length + 24, width), F32),
            "before": ((passes, length, hidden_width), F32),
        }
    )

    def exchange(pieces):
        return [pieces[0]] + [
            lax.ppermute(pieces[bits], "section", xor_pairs("section", bits))
            for bits in range(1, section_count)
        ]

    slot_x, slot_y = ("section", 1), ("section", 2)
    slots_dp = [("dp", bits) for bits in dp_bits]

    inputs_t = jnp.swapaxes(inputs, 1, 2)
    got = exchange(
        order.call(
            split_items,
            [Far(inputs_t)],
            [((slice_width, half_rows), F32, "raw")] * section_count,
            moves=section_count,
            limit=4,
        )
    )
    cot_sent = order.call(
        split_cotangent,
        [Far(cotangent)],
        [((half_rows, width), BF16, "raw")] * section_count,
        [pltpu.VMEM((section_count, half_rows, width), kind) for kind in (F32, BF16)],
        moves=2 * section_count,
        limit=8,
    )

    def bring(weights):
        return order.call(
            load,
            [Far(one) for one in weights],
            [(one.shape, one.dtype, "near") for one in weights],
            moves=len(weights),
            limit=8,
        )

    w_query, w_key, w_value, w_out = bring((w_query, w_key, w_value, w_out))
    cot_got = exchange(cot_sent)
    (entry_t,) = order.call(
        place_pieces,
        [Raw(one) for one in got],
        [((width, half_rows), F32, "near")],
        moves=section_count,
        limit=8,
    )
    entry_other = swap(entry_t)

    wide_near = ((length, width), F32, "near")
    part_near = ((length, width), BF16, "near")
    stacked = ((passes, half_rows, width), F32, "raw")
    turned = pltpu.VMEM((head_width, length), F32)
    entry_v = pltpu.VMEM((length, width), F32)
    cot_v = pltpu.VMEM((length, width), BF16)
    whole = slice(None)

    def low(step, name):
        return Held("low", step, "abef".index(name))

    def hidden(step, name):
        return Held("hidden", step, ("m", "dg").index(name))

    def heads(step, name):
        return Held("heads", step, ("q", "k", "v", "o", "dq", "dk", "dv").index(name))

    def turn(step, name):
        return Held("turned", step, ("kt", "vt").index(name))

    def rows(step, start, count, columns=None):
        cut = (slice(start, start + count), slice(0, columns or width))
        return Held("wide", step, cut)

    def entered(step):
        return rows(step, 0, length)

    def middle(step):
        return rows(step, length, length)

    def logsum(step):
        return rows(step, 2 * length, 8, length)

    def small_entry(step):
        return rows(step, 2 * length + 8, 8)

    def small_middle(step):
        return rows(step, 2 * length + 16, 8)

    results = None
    resid = None
    cot_own = cot_other = None
    for step in range(passes):
        layer = min(step, 1)
        first = [Near(entry_t), Near(entry_other)] if step == 0 else [Near(one) for one in resid]
        weights = [Near(one) for one in (w_query, w_key, w_value, w_out)]
        operands = first + [pass_embed, gain_one, bias_one] + weights
        operands += [heads(past, "k") for past in range(step)]
        operands += [turn(past, "vt") for past in range(step)]
        update = None
        if step > 0:
            operands.append(Scalars(counts))
        if step > 1:
            operands.append(Raw(results))
            update = {0: len(operands) - 1}
        done = order.call(
            functools.partial(attention_forward, step, layer),
            operands,
            ([] if step == 0 else [stacked])
            + [wide_near, entered(step), low(step, "a"), heads(step, "q"), heads(step, "k")]
            + [turn(step, "kt"), heads(step, "v"), turn(step, "vt"), logsum(step)]
            + [heads(step, "o"), part_near],
            [turned, entry_v],
            moves=1,
            update=update,
        )
        if step > 0:
            results = done[0]
            done = done[1:]
        near_u, part = done
        if step == 0:
            w_up, w_down = bring((w_up, w_down))
            cot_flat, part = order.call(
                place_beside,
                [Raw(one) for one in cot_got] + [Near(part)],
                [((section_count * half_rows, width), BF16, "raw"), part_near],
                moves=section_count,
                limit=8,
                update={1: section_count},
            )
            cot_own = cot_flat.reshape(section_count, half_rows, width)
            cot_other = swap(cot_own)
        near_r, part_two = order.call(
            functools.partial(feed_forward, layer),
            [Near(part), Near(swap(part)), Near(near_u), gain_two, bias_two]
            + [Near(w_up), Near(w_down)],
            [wide_near, middle(step), low(step, "b"), Held("before", step), hidden(step, "m"), part_near],
        )
        resid = (near_r, part_two, swap(part_two))

    factors = [
        {name: low(step, name) for name in "abef"}
        | {name: hidden(step, name) for name in ("m", "dg")}
        | {name: heads(step, name) for name in ("o", "dq", "dk", "dv")}
        for step in range(passes)
    ]
    state = None

    def feed_step(step):
        nonlocal results
        layer = min(step, 1)
        last = step == passes - 1
        operands = [Scalars(counts), Raw(cot_own), Raw(cot_other)]
        operands += [Near(w_down), Near(w_up)]
        outs = [wide_near, low(step, "e"), hidden(step, "dg"), part_near]
        update = None
        if last:
            operands += [Near(one) for one in resid] + [Held("before", step)]
            outs += [stacked]
            operands.append(Raw(results))
            update = {4: len(operands) - 1}
        else:
            dr, part, other = state
            operands += [Near(part), Near(other), Near(dr), entered(step + 1), gain_one]
            operands += [Held("before", step)]
            outs += [small_entry(step + 1)]

        def body(ins, outs, mover, *rooms):
            feed_backward(step, layer, last, ins[:9] if last else ins, outs, mover, *rooms)

        done = order.call(
            body,
            operands,
            outs,
            [cot_v] + ([entry_v] if last else []),
            moves=3,
            update=update,
            name=feed_backward.__name__,
        )
        near_dh, part = done[:2]
        if last:
            results = done[2]
        return near_dh, part, swap(part)

    def attention_step(step, fed):
        layer = min(step, 1)
        last = step == passes - 1
        near_dh, part, other = fed
        operands = [Near(part), Near(other), Near(near_dh), middle(step), gain_two]
        operands += [Near(w_out), heads(step, "q"), logsum(step), heads(step, "o")]
        operands += [heads(past, "k") for past in range(step + 1)]
        operands += [heads(past, "v") for past in range(step + 1)]
        operands += [turn(past, "kt") for past in range(step + 1)]
        cut = (slice(0, step + 1),)
        if not last:
            operands += [Held("order", at, cut) for at in range(2)]
        operands += [Near(one) for one in (w_query, w_key, w_value)]
        outs = [wide_near, low(step, "f"), heads(step, "dq"), heads(step, "dk"), heads(step, "dv")]
        outs += [part_near, small_middle(step)]
        if step > 0:
            outs += [Held("order", at, (slice(0, step),)) for at in range(2)]
        near_dr, part = order.call(
            functools.partial(attention_backward, step, layer, last),
            operands,
            outs,
            [pltpu.VMEM((length, head_width), BF16), turned, pltpu.VMEM((8, length), F32)],
        )
        return near_dr, part, swap(part)

    later, early = list(range(1, passes)), [0]
    def feed_group(steps, start):
        first = [("up", start, [(low(step, "b"), hidden(step, "dg")) for step in steps])]
        second = [("down", start, [(low(step, "e"), hidden(step, "m")) for step in steps])]
        return (first, second)

    def heads_group(steps):
        def product(name, left, right):
            return (name, 0, [(low(step, left), heads(step, right)) for step in steps])

        first = [product("query", "a", "dq"), product("key", "a", "dk")]
        second = [product("out", "f", "o"), product("value", "a", "dv")]
        return (first, second)

    kinds = []
    for layer, steps in ((1, later), (0, early)):
        first = len(kinds)
        columns = hidden_width // SPLITS[layer]
        for start in range(0, hidden_width, columns):
            kinds.append((layer, first, columns, feed_group(steps, start)))
        kinds.append((layer, len(kinds), width, heads_group(steps)))
    made = {}
    shapes_out = {name: (2, width, head_width) for name in ("query", "key", "value", "out")}
    shapes_out |= {name: (2, width, hidden_width) for name in ("up", "down")}
    outputs = {}

    def make_products(group):
        layer, first, columns, products = kinds[group]
        sharing = [at for at, one in enumerate(kinds) if one[1] == first]
        operands, place = [], {}

        def number(held):
            key = (held.name, str(held.index))
            if key not in place:
                place[key] = len(operands)
                operands.append(held)
            return place[key]

        numbered = [
            [[(number(left), number(right)) for left, right in pairs] for _, _, pairs in part]
            for part in products
        ]
        done = order.call(
            functools.partial(weight_first, numbered, (slot_x, slot_y), len(sharing)),
            operands,
            [((width // 2, columns), BF16, "raw")] * (4 * len(sharing)),
            [pltpu.VMEM((width, columns * len(sharing)), BF16)] * 2,
            moves=4 * len(sharing),
            limit=30,
        )
        for at, one in enumerate(sharing):
            made[one] = done[4 * at : 4 * at + 4]

    def stages(group):
        layer, first, columns, products = kinds[group]
        sizes = [columns // len(part) for part in products for _ in part]
        room = lambda rows, cols: pltpu.VMEM((rows, cols), BF16)
        raw = lambda rows, cols: ((rows, cols), BF16, "raw")
        send = lambda value, axis, bits: lax.ppermute(value, axis, xor_pairs(axis, bits))
        if first == group:
            make_products(group)
        kept_a, sent_a, kept_b, sent_b = made[group]
        got_a, got_b = send(sent_a, "section", 1), send(sent_b, "section", 2)
        yield
        kept_a, sent_a, kept_b, sent_b = order.call(
            functools.partial(add_split, (slot_y, slot_x), 0),
            [kept_a, got_a, kept_b, got_b],
            [raw(width // 4, columns)] * 4,
            [room(width // 2, columns)] * 2,
            moves=4,
            limit=30,
        )
        got_a, got_b = send(sent_a, "section", 2), send(sent_b, "section", 1)
        yield
        shape = [width // 4, 2 * columns]
        axes = []
        for level, bits in enumerate(dp_bits):
            axis = 0 if shape[0] % 32 == 0 else 1
            axes.append(axis)
            before = tuple(shape)
            shape[axis] //= 2
            if level == 0:
                own, sent = order.call(
                    functools.partial(add_merge, slots_dp[level], axis),
                    [kept_a, got_a, kept_b, got_b],
                    [raw(*shape)] * 2,
                    [room(*before)],
                    moves=2,
                    limit=24,
                )
            else:
                own, sent = order.call(
                    functools.partial(add_split, (slots_dp[level],), axis),
                    [own, got],
                    [raw(*shape)] * 2,
                    [room(*before)],
                    moves=2,
                    limit=16,
                )
            got = send(sent, "dp", bits)
            yield
        (own,) = order.call(add_last, [own, got], [(tuple(shape), BF16)], limit=16)
        got = send(own, "dp", dp_bits[-1])
        yield
        for level in reversed(range(len(dp_bits))):
            axis = axes[level]
            shape[axis] *= 2
            if level > 0:
                (own,) = order.call(
                    functools.partial(join, (slots_dp[level],), axis),
                    [Raw(own), Raw(got)],
                    [raw(*shape)],
                    moves=2,
                    limit=16,
                )
                got = send(own, "dp", dp_bits[level - 1])
                yield
        own_a, own_b = order.call(
            functools.partial(join_part, slots_dp[0], axes[0]),
            [Raw(own), Raw(got)],
            [raw(width // 4, columns)] * 2,
            [room(*shape)],
            moves=4,
            limit=16,
        )
        got_a, got_b = send(own_a, "section", 2), send(own_b, "section", 1)
        yield
        own_a, own_b = order.call(
            functools.partial(join, (slot_y, slot_x), 0),
            [Raw(own_a), Raw(got_a), Raw(own_b), Raw(got_b)],
            [raw(width // 2, columns)] * 2,
            moves=4,
            limit=16,
        )
        got_a, got_b = send(own_a, "section", 1), send(own_b, "section", 2)
        yield
        names = [(name, start) for part in products for name, start, _ in part]
        before = [outputs.get(name) for name, _ in names]
        given = [one for one in before if one is not None]
        update = {}
        for at, one in enumerate(before):
            if one is not None:
                update[at] = 4 + len(update)
        done = order.call(
            functools.partial(
                finish, layer, len(products[0]), (slot_x, slot_y), [start for _, start in names]
            ),
            [own_a, got_a, own_b, got_b] + [Raw(one) for one in given],
            [(shapes_out[name], F32, "raw") for name, _ in names],
            [pltpu.VMEM((width // 2, size), F32) for size in sizes for _ in range(2)],
            moves=2 * len(names),
            limit=30,
            update=update,
        )
        for (name, _), one in zip(names, done):
            outputs[name] = one

    def small_stages():
        (packed,) = order.call(
            pack_small,
            [small_entry(step) for step in range(passes)] + [small_middle(step) for step in range(passes)],
            [((-(-(8 + passes) // 8) * 8, width), F32)], limit=8
        )
        hops = [("section", 1), ("section", 2)] + [("dp", bits) for bits in dp_bits]
        for axis, bits in hops[:-1]:
            got = lax.ppermute(packed, axis, xor_pairs(axis, bits))
            yield
            (packed,) = order.call(add_small, [packed, got], [(packed.shape, F32)], limit=8)
        axis, bits = hops[-1]
        got = lax.ppermute(packed, axis, xor_pairs(axis, bits))
        yield
        outputs["small"] = order.call(
            part_small,
            [packed, got],
            [((2, width), F32)] * 4 + [((passes, width), F32)],
            limit=8,
        )

    def input_stages(entered_t):
        got = exchange(entered_t)
        yield
        (grad_t,) = order.call(
            place_items,
            [Raw(one) for one in got],
            [((batches, slice_width, half_rows), F32, "raw")],
            [pltpu.VMEM((section_count, slice_width, half_rows), F32)],
            moves=section_count + 1,
            limit=8,
        )
        outputs["inputs"] = jnp.swapaxes(grad_t, 1, 2)

    running = {}

    def advance(name):
        if name not in running:
            running[name] = stages(name)
        next(running[name], None)

    passes_out = None
    for step in reversed(range(2, passes)):
        fed = feed_step(step)
        if step == passes - 1:
            passes_got = exchange(
                order.call(
                    split_items,
                    [Raw(results)],
                    [((half_rows, width), F32, "raw")] * section_count,
                    moves=section_count,
                    limit=4,
                )
            )
        state = attention_step(step, fed)

    def chain():
        nonlocal state, passes_out
        fed = feed_step(1)
        yield
        state = attention_step(1, fed)
        yield
        fed = feed_step(0)
        yield
        state = attention_step(0, fed)
        yield
        near_dr, part, other = state
        entered_t = order.call(
            entry_backward,
            [Near(part), Near(other), Near(near_dr), entered(0), gain_one],
            [small_entry(0)] + [((slice_width, half_rows), F32, "raw")] * section_count,
            [entry_v, pltpu.VMEM((section_count, slice_width, half_rows), F32)],
            moves=section_count,
        )
        (passes_out,) = order.call(
            place_items,
            [Raw(one) for one in passes_got],
            [((batches, half_rows, width), F32, "raw")],
            [pltpu.VMEM((section_count, half_rows, width), F32)],
            moves=section_count + 1,
            limit=8,
        )
        running["inputs"] = input_stages(entered_t)
        next(running["inputs"])
        running["small"] = small_stages()

    running["chain"] = chain()
    for name in schedule(len(dp_bits), len(kinds)):
        advance(name)
    for name in list(running):
        for _ in running[name]:
            pass
    return (
        passes_out[None],
        outputs["inputs"],
        *[outputs[name] for name in ("query", "key", "value", "out", "up", "down")],
        *outputs["small"],
    )


def solution(mesh):
    weight = P(None, None, "tensor")
    return jax.shard_map(
        shards,
        mesh=mesh,
        in_specs=(
            P("dp", "tensor", "section"),
            P("dp"),
            weight,
            weight,
            weight,
            weight,
            weight,
            weight,
            P(),
            P(),
            P(),
            P(),
            P(),
            P("section", "dp", "tensor", None),
        ),
        out_specs=(
            P("section", "dp", "tensor", None),
            P("dp", "tensor", "section"),
            weight,
            weight,
            weight,
            weight,
            weight,
            weight,
            P(),
            P(),
            P(),
            P(),
            P(),
        ),
        check_vma=False,
    )
```
